128 devices in a mesh: grp: 2 (over core), dp: 16 (over z, x), mp: 4 (over y).
Axes of the slice: x: 4, y: 4, z: 4, core: 2. Of those that a mesh axis runs over, the one named last changes fastest.
Arguments:
- hidden: bfloat16 [4096, 5120], P(('dp', 'mp')), may hold values from -6 to 6
- enc_weight: bfloat16 [5120, 8192], P(None, 'mp'), may hold values from -0.078125 to 0.078125
- enc_bias: bfloat16 [8192], P('mp'), may hold values from -5 to 5
- enc_frozen: bfloat16 [5120, 64], replicated, may hold values from -0.078125 to 0.078125
- enc_adapter: bfloat16 [64, 8192], P(None, 'mp'), may hold values from -0.75 to 0.75
- text_rows: bfloat16 [10240, 8192], P(('dp', 'mp')), may hold values from -6 to 6
- norm_gain: bfloat16 [8192], replicated, may hold values from 0.5 to 1.5
- value_weight: bfloat16 [8192, 1024], P(('dp', 'mp')), may hold values from -0.0625 to 0.0625
- value_bias: bfloat16 [1024], replicated, may hold values from -5 to 5
- llm_frozen: bfloat16 [8192, 64], P(('dp', 'mp')), may hold values from -0.0625 to 0.0625
- llm_adapter: bfloat16 [64, 1024], replicated, may hold values from -0.75 to 0.75
- targets: bfloat16 [10240, 1024], P(('dp', 'mp')), may hold values from -6 to 6
- dest_owner: int32 [4096, 1], replicated, may hold values from 0 to 63; in each aligned block of 256 rows (0 to 255, 256 to 511, ...) at most 8 rows name the same one
- seq_length: int32 [64], P(('dp', 'mp')), may hold values from 128 to 160
Outputs:
- grad_enc: float32 [64, 8192], P('grp', 'mp')
- grad_llm: float32 [64, 1024], P('grp')
The draws below stay inside these ranges and needn't reach their ends.
Inputs may be any that keep to these rules, and one draw needn't show every extreme that they name: `dest_owner`: within the tokens of one encoder block (aligned blocks of 256 rows) no LLM device is named more than 8 times, and some device is named exactly 8 times in some blocks.
All inputs are finite; a program needn't handle non-finite values.
Results may differ from the reference program's by a relative error of at most 0.003.
Values may be sent and summed in bfloat16 or wider, within the bound.
No kernel may reach another device: no remote copies, remote signals or barrier semaphores. Data moves between devices by JAX's collectives and lax.ppermute only.
A program may use at most 128 MiB of HBM per device.

```python
import math
import jax
import jax.numpy as jnp
import numpy as np
from jax import lax

D = 8192
MH = 5120
KV = 1024
RANK = 64
ENC_DEV = 256
LLM_DEV = 160
OWNERS = 64
CAP = 8
IMG = 4096
N_DP = 16
N_MP = 4


def touch_ends(values, rng, low, top_value):
    shape = values.shape
    place = [jax.random.randint(jax.random.fold_in(rng, axis), (), 0, shape[axis]) for axis in range(len(shape))]
    values = values.at[tuple(place)].set(low)
    longest = shape.index(max(shape))
    place[longest] = (place[longest] + 1) % shape[longest]
    return values.at[tuple(place)].set(top_value)


def level_of(stream_key, dims, shards, low, top_value):
    def one(dim, parts):
        heights = jax.random.uniform(jax.random.fold_in(jax.random.fold_in(stream_key, 6), dim), (parts,), jnp.float32, low / len(shards), top_value / len(shards))
        return jnp.repeat(jnp.exp(heights), dims[dim] // parts).reshape((-1,) + (1,) * (len(dims) - dim - 1))

    factor_of = one(*shards[0])
    for cut in shards[1:]:
        factor_of = factor_of * one(*cut)
    return factor_of


def deal_out(key, own, number, rows, count, top, reach, slope):
    sequence = jax.random.permutation(key, count)
    heavy_load, common = shares(count, rows * top, reach, slope, True), shares(count, rows * top, reach, slope, False)
    places = jnp.arange(count)

    def named(sizes, offset_by):
        used = int((sizes > 0).sum())
        fixed = max(1, used // 4)
        moved = fixed + (places - fixed + offset_by * (used - fixed)) % max(1, count - fixed)
        return jnp.zeros((count,), jnp.int32).at[sequence[jnp.where(places < fixed, places, moved)]].set(jnp.asarray(sizes, jnp.int32))

    sizes = jnp.where(number % 4 == 0, named(heavy_load, number // 4), named(common, number - number // 4 - 1))
    mixed = jax.random.permutation(jax.random.fold_in(own, 3), count)
    donor, sink = mixed[0:count // 2 * 2:2], mixed[1:count // 2 * 2:2]
    room = jnp.minimum(sizes[donor] - 1, reach - sizes[sink]) // 2
    room = jnp.where((donor == sequence[0]) | (sink == sequence[0]) | (sizes[sink] == 0), 0, jnp.maximum(room, 0))
    moved = jax.random.randint(jax.random.fold_in(own, 4), (count // 2,), 0, 1 << 20) % (room + 1)
    sizes = sizes.at[donor].add(-moved).at[sink].add(moved)
    items = jnp.searchsorted(jnp.cumsum(sizes), jnp.arange(rows * top), side="right").astype(jnp.int32)
    listing = items.reshape(top, rows).T
    listing = listing[jax.random.permutation(jax.random.fold_in(own, 1), rows)]
    offset_by = jax.random.randint(jax.random.fold_in(own, 2), (rows, 1), 0, top)
    return jnp.take_along_axis(listing, (jnp.arange(top)[None, :] + offset_by) % top, axis=1)


def shares(number_of, total, most, slope, full):
    portions = [(1 << 20) // math.isqrt(grade ** slope) + 1 for grade in range(1, number_of + 1)]
    largest = most if full else min(most, max(-(-total // number_of), total * portions[0] // sum(portions)))
    least = 1 if total - largest >= number_of - 1 else 0
    given, surplus = [largest] + [least] * (number_of - 1), total - largest - least * (number_of - 1)
    while surplus > 0:
        candidates = [i for i in range(1, number_of) if given[i] < largest] or [i for i in range(1, number_of) if given[i] < most]
        pool, left = sum([portions[i] for i in candidates]), surplus
        for i in candidates:
            extra = min(most - given[i], max(1, left * portions[i] // pool), surplus)
            given[i] = given[i] + extra
            surplus = surplus - extra
    return np.array(given)


def noise(own_key, dims, scale, most, shards=(), kind=jnp.bfloat16):
    values = scale * jax.random.normal(own_key, dims, jnp.float32)
    if shards:
        values = values * level_of(own_key, dims, shards, -0.22, 0.18)
    return jnp.clip(values, -most, most).astype(kind)


def setup_inputs(seed: int = 0) -> dict:
    streams_of = jax.random.split(jax.random.key(seed), 15)
    hidden = noise(streams_of[0], (IMG, MH), 1.0, 6.0, ((0, 64),))
    enc_weight = noise(streams_of[1], (MH, D), MH ** -0.5, 0.078125, ((1, 4),))
    enc_bias = noise(streams_of[2], (D,), 1.0, 5.0, ((0, 4),))
    enc_frozen = noise(streams_of[3], (MH, RANK), MH ** -0.5, 0.078125)
    enc_adapter = noise(streams_of[4], (RANK, D), RANK ** -0.5, 0.75, ((1, 4),))
    text_rows = noise(streams_of[5], (OWNERS * LLM_DEV, D), 1.0, 6.0, ((0, 64),))
    norm_gain = jnp.clip(1.0 + 0.1 * jax.random.normal(streams_of[6], (D,), jnp.float32), 0.5, 1.5).astype(jnp.bfloat16)
    value_weight = noise(streams_of[7], (D, KV), D ** -0.5, 0.0625, ((0, 64),))
    value_bias = noise(streams_of[8], (KV,), 1.0, 5.0)
    llm_frozen = noise(streams_of[9], (D, RANK), D ** -0.5, 0.0625, ((0, 64),))
    llm_adapter = noise(streams_of[10], (RANK, KV), RANK ** -0.5, 0.75)
    targets = noise(streams_of[11], (OWNERS * LLM_DEV, KV), 1.0, 6.0, ((0, 64),))
    dest_owner_keys = jax.random.split(jax.random.fold_in(streams_of[12], 1), IMG // ENC_DEV)
    dest_owner_turns = jax.random.permutation(jax.random.fold_in(streams_of[12], 3), IMG // ENC_DEV)
    dest_owner = jax.vmap(lambda own, number: deal_out(jax.random.fold_in(streams_of[12], 2), own, number, ENC_DEV, OWNERS, 1, CAP, 2))(dest_owner_keys, dest_owner_turns).reshape((IMG, 1))
    seq_length = touch_ends(jax.random.randint(streams_of[13], (OWNERS,), N_DP * CAP, LLM_DEV + 1), jax.random.fold_in(streams_of[13], 1), N_DP * CAP, LLM_DEV).astype(jnp.int32)
    return dict(hidden=hidden, enc_weight=enc_weight, enc_bias=enc_bias, enc_frozen=enc_frozen, enc_adapter=enc_adapter, text_rows=text_rows, norm_gain=norm_gain, value_weight=value_weight, value_bias=value_bias, llm_frozen=llm_frozen, llm_adapter=llm_adapter, targets=targets, dest_owner=dest_owner, seq_length=seq_length)


epsilon = 1e-06

def reference(hidden, enc_weight, enc_bias, enc_frozen, enc_adapter, text_rows, norm_gain, value_weight, value_bias, llm_frozen, llm_adapter, targets, dest_owner, seq_length):
    owners = N_DP * N_MP
    enc_low = jnp.dot(hidden, enc_frozen, preferred_element_type=jnp.float32).astype(jnp.bfloat16)
    merged_rows = jnp.dot(hidden, enc_weight, preferred_element_type=jnp.float32) + enc_bias.astype(jnp.float32)
    merged_rows = (merged_rows + jnp.dot(enc_low, enc_adapter, preferred_element_type=jnp.float32)).astype(jnp.bfloat16)
    destiny = dest_owner[:, 0].reshape(N_DP, ENC_DEV)
    markers = (destiny[:, :, None] == jnp.arange(owners, dtype=jnp.int32)[None, None, :]).astype(jnp.int32)
    slot_rank = lax.optimization_barrier(jnp.sum((jnp.cumsum(markers, axis=1) - markers) * markers, axis=2))
    placing = destiny * LLM_DEV + slot_rank * N_DP + jnp.arange(N_DP, dtype=jnp.int32)[:, None]
    placing = placing.reshape(-1).astype(jnp.int32)
    all_rows = text_rows.at[placing].set(merged_rows)
    wide_rows = all_rows.astype(jnp.float32)
    inverse = lax.rsqrt(lax.optimization_barrier(jnp.mean(wide_rows * wide_rows, axis=1, keepdims=True)) + epsilon)
    gain_wide = norm_gain.astype(jnp.float32)
    normed = (wide_rows * inverse * gain_wide).astype(jnp.bfloat16)
    low_rank = jnp.dot(normed, llm_frozen, preferred_element_type=jnp.float32).astype(jnp.bfloat16)
    values_out = jnp.dot(normed, value_weight, preferred_element_type=jnp.float32) + value_bias.astype(jnp.float32)
    values_out = values_out + jnp.dot(low_rank, llm_adapter, preferred_element_type=jnp.float32)
    position = jnp.arange(owners * LLM_DEV, dtype=jnp.int32) % LLM_DEV
    length = jnp.repeat(seq_length, LLM_DEV)
    row_weight = jnp.where(position < length, 1.0 / length.astype(jnp.float32), 0.0).astype(jnp.float32)
    dvalues = ((values_out - targets.astype(jnp.float32)) * row_weight[:, None]).astype(jnp.bfloat16)
    grad_llm = jnp.dot(low_rank.T, dvalues, preferred_element_type=jnp.float32)
    low_grad = jnp.dot(dvalues, llm_adapter.T, preferred_element_type=jnp.float32).astype(jnp.bfloat16)
    picked_dv = dvalues[placing]
    picked_low = low_grad[placing]
    picked_rows = wide_rows[placing]
    picked_inverse = inverse[placing]
    dnormed = jnp.dot(picked_dv, value_weight.T, preferred_element_type=jnp.float32)
    dnormed = dnormed + jnp.dot(picked_low, llm_frozen.T, preferred_element_type=jnp.float32)
    scaled = gain_wide * dnormed
    cubed = picked_inverse * picked_inverse * picked_inverse
    image_grad = picked_inverse * scaled - picked_rows * cubed * lax.optimization_barrier(jnp.mean(scaled * picked_rows, axis=1, keepdims=True))
    image_grad = image_grad.astype(jnp.bfloat16)
    grad_enc = jnp.dot(enc_low.T, image_grad, preferred_element_type=jnp.float32)
    return (grad_enc, grad_llm)
```

```python
import jax
import jax.numpy as jnp
from jax import lax
from jax.sharding import PartitionSpec as P

ENC_DEV = 256


epsilon = 1e-06


def joined_along(parts, dim):
    parts = jnp.moveaxis(parts, 0, dim)
    lengths = parts.shape
    return parts.reshape(*lengths[:dim], lengths[dim] * lengths[dim + 1], *lengths[dim + 2 :])


def from_everyone(array, axis):
    devices = lax.axis_size(axis)
    return lax.all_to_all(
        jnp.broadcast_to(array[None], (devices, *array.shape)), axis, 0, 0, tiled=True
    )


def gathered_copies(array, axis, dim):
    return joined_along(from_everyone(array, axis), dim)


def passed_along(value, axis, steps):
    count = lax.axis_size(axis)
    first, last = (max(0, -steps), min(count, count - steps))
    return lax.ppermute(value, axis, [(source, source + steps) for source in range(first, last)])


def sent_together(arrays, axis, dim, along):
    ends, at = ([], 0)
    for a in arrays[:-1]:
        at += a.shape[along]
        ends.append(at)
    both = jnp.concatenate(arrays, axis=along)
    return tuple(jnp.split(lax.all_gather(both, axis, axis=dim, tiled=True), ends, axis=along))


def rows_for(lines, devices):
    spare = -lines.shape[0] % devices
    if not spare:
        return lines
    return jnp.concatenate([lines, jnp.zeros((spare, *lines.shape[1:]), lines.dtype)])


def split_up(array, dim, devices):
    lengths = array.shape
    parts = array.reshape(*lengths[:dim], devices, lengths[dim] // devices, *lengths[dim + 1 :])
    return jnp.moveaxis(parts, dim, 0)


def summed_on_arrival(array, axis, dim):
    devices = lax.axis_size(axis)
    parts = lax.all_to_all(split_up(array, dim, devices), axis, 0, 0, tiled=True)
    return jnp.sum(parts, axis=0)


def nested_sum(array, axes):
    lines = array.reshape(-1, array.shape[-1])
    padded = rows_for(lines, lax.axis_size(axes))
    whole = gathered_copies(summed_on_arrival(padded, axes, 0), axes, 0)
    return lax.slice_in_dim(whole, 0, len(lines)).reshape(array.shape)


def swapped(array, axis, bit):
    return lax.ppermute(array, axis, [(i, i ^ 1 << bit) for i in range(lax.axis_size(axis))])


def slot_ranks(destiny, owners):
    count = destiny.shape[0]
    place = jnp.arange(count, dtype=jnp.int32)
    earlier = (destiny[:, None] == destiny[None, :]) & (place[None, :] < place[:, None])
    return jnp.sum(earlier.astype(jnp.int32), axis=1)


def body(
    hidden,
    enc_weight,
    enc_bias,
    enc_frozen,
    enc_adapter,
    text_rows,
    norm_gain,
    value_weight,
    value_bias,
    llm_frozen,
    llm_adapter,
    targets,
    dest_owner,
    seq_length,
):
    data_ways = lax.axis_size("dp")
    model_ways = lax.axis_size("mp")
    owners = data_ways * model_ways
    capacity = 2 * ENC_DEV // owners
    area = capacity * data_ways
    encoder = lax.axis_index("grp") == 0
    data_index = lax.axis_index("dp")
    owner_index = data_index * model_ways + lax.axis_index("mp")
    part_width = enc_weight.shape[1]
    rank_width = enc_frozen.shape[1]
    kv_width = llm_adapter.shape[1]
    group_rows = gathered_copies(hidden, "mp", 0)

    def encode(source):
        low_rank = jnp.dot(source, enc_frozen, preferred_element_type=jnp.float32).astype(
            jnp.bfloat16
        )
        merged = jnp.dot(source, enc_weight, preferred_element_type=jnp.float32) + enc_bias.astype(
            jnp.float32
        )
        merged = merged + jnp.dot(low_rank, enc_adapter, preferred_element_type=jnp.float32)
        return (merged.astype(jnp.bfloat16), low_rank)

    def rest_encode(source):
        return (
            jnp.zeros((source.shape[0], part_width), jnp.bfloat16),
            jnp.zeros((source.shape[0], rank_width), jnp.bfloat16),
        )

    merged_rows, enc_low = lax.cond(encoder, encode, rest_encode, group_rows)
    destiny = dest_owner[:, 0]
    own_dest = lax.dynamic_slice_in_dim(destiny, data_index * ENC_DEV, ENC_DEV)
    bucket_index = slot_ranks(own_dest, owners) * owners + own_dest
    outgoing = (
        jnp.zeros((capacity * owners, part_width), jnp.bfloat16).at[bucket_index].set(merged_rows)
    )
    outgoing = outgoing.reshape(capacity, owners, part_width)
    grouped = lax.all_to_all(outgoing, ("dp", "mp"), split_axis=1, concat_axis=1, tiled=True)
    arrived = passed_along(grouped, "grp", 1)
    counts = jnp.sum((destiny.reshape(data_ways, ENC_DEV) == owner_index).astype(jnp.int32), axis=1)
    usable = (jnp.arange(capacity, dtype=jnp.int32)[:, None] < counts[None, :]).reshape(area, 1)
    gathered = sent_together((value_weight, llm_frozen), ("dp", "mp"), 0, 1)

    def learn_layer(operands):
        incoming, whole_value, whole_frozen = operands
        image_rows = incoming.reshape(area, -1)
        head_rows = jnp.where(usable, image_rows, text_rows[:area])
        all_rows = jnp.concatenate([head_rows, text_rows[area:]], axis=0)
        wide_rows = all_rows.astype(jnp.float32)
        inverse = lax.rsqrt(jnp.mean(wide_rows * wide_rows, axis=1, keepdims=True) + epsilon)
        gain_wide = norm_gain.astype(jnp.float32)
        normed = (wide_rows * inverse * gain_wide).astype(jnp.bfloat16)
        low_rank = jnp.dot(normed, whole_frozen, preferred_element_type=jnp.float32).astype(
            jnp.bfloat16
        )
        values_out = jnp.dot(
            normed, whole_value, preferred_element_type=jnp.float32
        ) + value_bias.astype(jnp.float32)
        values_out = values_out + jnp.dot(low_rank, llm_adapter, preferred_element_type=jnp.float32)
        length = seq_length[0]
        position = jnp.arange(all_rows.shape[0], dtype=jnp.int32)
        row_weight = jnp.where(position < length, 1.0 / length.astype(jnp.float32), 0.0)
        dvalues = ((values_out - targets.astype(jnp.float32)) * row_weight[:, None]).astype(
            jnp.bfloat16
        )
        grad_part = jnp.dot(low_rank.T, dvalues, preferred_element_type=jnp.float32)
        head_dv = dvalues[:area]
        low_grad = jnp.dot(head_dv, llm_adapter.T, preferred_element_type=jnp.float32).astype(
            jnp.bfloat16
        )
        dnormed = jnp.dot(head_dv, whole_value.T, preferred_element_type=jnp.float32)
        dnormed = dnormed + jnp.dot(low_grad, whole_frozen.T, preferred_element_type=jnp.float32)
        scaled = gain_wide * dnormed
        head_wide = wide_rows[:area]
        head_inverse = inverse[:area]
        cubed = head_inverse * head_inverse * head_inverse
        image_grad = head_inverse * scaled - head_wide * cubed * jnp.mean(
            scaled * head_wide, axis=1, keepdims=True
        )
        image_grad = image_grad.astype(jnp.bfloat16)
        reply_rows = jnp.where(usable, image_grad, jnp.zeros_like(image_grad))
        return (grad_part, reply_rows.reshape(capacity, owners, part_width))

    def rest_learn(operands):
        return (
            jnp.zeros((rank_width, kv_width), jnp.float32),
            jnp.zeros((capacity, owners, part_width), jnp.bfloat16),
        )

    llm_part, reply_rows = lax.cond(
        encoder, rest_learn, learn_layer, (arrived, gathered[0], gathered[1])
    )
    llm_total = nested_sum(llm_part, ("dp", "mp"))
    grouped_back = lax.all_to_all(reply_rows, ("dp", "mp"), split_axis=1, concat_axis=1, tiled=True)
    returned = passed_along(grouped_back, "grp", -1)

    def adapt_grad(operands):
        back_rows, low_rank = operands
        image_grad = back_rows.reshape(capacity * owners, part_width)[bucket_index]
        return jnp.dot(low_rank.T, image_grad, preferred_element_type=jnp.float32)

    def rest_adapt(operands):
        return jnp.zeros((rank_width, part_width), jnp.float32)

    enc_part = lax.cond(encoder, adapt_grad, rest_adapt, (returned, enc_low))
    enc_total = nested_sum(enc_part, "dp")
    half_rank = rank_width // 2
    enc_count = half_rank * part_width
    llm_count = half_rank * kv_width
    span = max(enc_count, llm_count)
    enc_upper = enc_total[half_rank:].reshape(-1)
    llm_lower = jnp.pad(llm_total[:half_rank].reshape(-1), (0, span - llm_count))
    sending = jnp.where(encoder, enc_upper, llm_lower)
    received = swapped(sending, "grp", 0)
    grad_enc = jnp.where(encoder, enc_total[:half_rank], received.reshape(half_rank, part_width))
    grad_llm = jnp.where(
        encoder, received[:llm_count].reshape(half_rank, kv_width), llm_total[half_rank:]
    )
    return (grad_enc, grad_llm)


def solution(mesh):
    return jax.shard_map(
        body,
        mesh=mesh,
        in_specs=(
            P(("dp", "mp"), None),
            P(None, "mp"),
            P("mp"),
            P(),
            P(None, "mp"),
            P(("dp", "mp"), None),
            P(),
            P(("dp", "mp"), None),
            P(),
            P(("dp", "mp"), None),
            P(),
            P(("dp", "mp"), None),
            P(),
            P(("dp", "mp")),
        ),
        out_specs=(P("grp", "mp"), P("grp", None)),
        check_vma=False,
    )
```

```python
import jax
import jax.numpy as jnp
from jax import lax
from jax.sharding import PartitionSpec as P

ENC_DEV = 256
epsilon = 1e-06
f32 = jnp.float32
bf16 = jnp.bfloat16


def dot(a, b):
    return jnp.dot(a, b, preferred_element_type=f32)


def dot_tn(a, b):
    return lax.dot_general(a, b, (((0,), (0,)), ((), ())), preferred_element_type=f32)


def dot_nt(a, b):
    return lax.dot_general(a, b, (((1,), (1,)), ((), ())), preferred_element_type=f32)


def split_two(a):
    high = a.astype(bf16)
    return high, (a - high.astype(f32)).astype(bf16)


def split_three(a):
    high, rest = a.astype(bf16), a - a.astype(bf16).astype(f32)
    middle, last = split_two(rest)
    return high, middle, last


def turned(array, axis, step):
    count = lax.axis_size(axis)
    return lax.ppermute(array, axis, [(i, (i + step) % count) for i in range(count)])


def crossed(array):
    return lax.ppermute(array, "grp", [(0, 1), (1, 0)])


def to_everyone(array, axes):
    count = lax.axis_size(axes)
    return lax.all_to_all(
        jnp.broadcast_to(array[None], (count, *array.shape)), axes, 0, 0, tiled=True
    )


def body(
    hidden,
    enc_weight,
    enc_bias,
    enc_frozen,
    enc_adapter,
    text_rows,
    norm_gain,
    value_weight,
    value_bias,
    llm_frozen,
    llm_adapter,
    targets,
    dest_owner,
    seq_length,
):
    n_dp = lax.axis_size("dp")
    n_mp = lax.axis_size("mp")
    side = n_mp
    owners = n_dp * n_mp
    grp = lax.axis_index("grp")
    dp = lax.axis_index("dp")
    mp = lax.axis_index("mp")
    first = grp == 0
    width = text_rows.shape[1]
    part_width = enc_weight.shape[1]
    rank = enc_frozen.shape[1]
    half_rank = rank // 2
    kv = value_weight.shape[1]
    half_kv = kv // 2
    shard = value_weight.shape[0]
    block_rows = hidden.shape[0]
    mine_rows = block_rows // 2
    capacity = 2 * ENC_DEV // owners

    own_hidden = lax.dynamic_slice_in_dim(hidden, grp * mine_rows, mine_rows)
    hid = jnp.concatenate([own_hidden] + [turned(own_hidden, "mp", k) for k in range(1, n_mp)])

    swap = [
        ((z * side + x) * side + y, (y * side + x) * side + z)
        for z in range(side)
        for x in range(side)
        for y in range(side)
    ]
    w_half = lax.dynamic_slice_in_dim(value_weight, grp * half_kv, half_kv, axis=1)
    w_moved = lax.ppermute(w_half, ("dp", "mp"), swap)
    w_mine = to_everyone(w_moved, "dp")
    w_mine = w_mine.reshape(side, side, shard, half_kv).transpose(1, 0, 2, 3).reshape(-1, half_kv)
    w_other = crossed(w_mine)

    a_half = lax.dynamic_slice_in_dim(llm_frozen.T, grp * half_rank, half_rank)
    a_mine = to_everyone(a_half, ("dp", "mp")).transpose(1, 0, 2).reshape(half_rank, width)
    a_all = jnp.concatenate([a_mine, crossed(a_mine)])
    a_part = lax.dynamic_slice_in_dim(a_all, mp * part_width, part_width, axis=1)
    b_ranked = jnp.where(first, llm_adapter, jnp.roll(llm_adapter, half_rank, axis=0))
    b_local = jnp.where(first, b_ranked, jnp.roll(b_ranked, half_kv, axis=1))
    bias_wide = value_bias.astype(f32)
    bias_local = jnp.where(first, bias_wide, jnp.roll(bias_wide, half_kv))

    own_length = seq_length[0]
    area = capacity * n_dp
    t_half = lax.dynamic_slice(targets, (0, grp * half_kv), (area, half_kv))
    t_half = t_half.reshape(capacity, n_dp, half_kv).transpose(1, 0, 2)
    t_half = jnp.concatenate(
        [t_half, jnp.full((n_dp, capacity, 128), own_length.astype(bf16))], axis=2
    )
    t_here = lax.all_to_all(t_half, "dp", 0, 0, tiled=True).reshape(n_dp * capacity, -1)
    t_mine = jnp.concatenate([t_here] + [turned(t_here, "mp", k) for k in range(1, n_mp)])
    t_other = crossed(t_mine[:, :half_kv])
    t_table = jnp.concatenate([t_mine[:, :half_kv], t_other, t_mine[:, half_kv:]], axis=1)
    destiny = dest_owner[:, 0]
    block_dest = lax.dynamic_slice_in_dim(destiny, dp * ENC_DEV, ENC_DEV)
    start = mp * block_rows + grp * mine_rows
    own_dest = lax.dynamic_slice_in_dim(block_dest, start, mine_rows)
    place = start + jnp.arange(mine_rows, dtype=jnp.int32)
    earlier = (own_dest[:, None] == block_dest[None, :]) & (
        jnp.arange(ENC_DEV, dtype=jnp.int32)[None, :] < place[:, None]
    )
    slot = jnp.sum(earlier.astype(jnp.int32), axis=1)
    source = (mp - own_dest % n_mp) % n_mp
    line = source * (n_dp * capacity) + (own_dest // n_mp) * capacity + slot
    pick = (line[:, None] == jnp.arange(n_mp * n_dp * capacity, dtype=jnp.int32)[None, :]).astype(
        bf16
    )
    picked = dot(pick, t_table)
    own_targets = picked[:, :kv]
    length = picked[:, kv : kv + 1]
    position = (slot * n_dp + dp)[:, None].astype(f32)
    weight = jnp.where(position < length, 1.0 / length, 0.0)

    gain_wide = norm_gain.astype(f32)
    text_count = text_rows.shape[0] // 2
    text_wide = lax.dynamic_slice_in_dim(text_rows, grp * text_count, text_count).astype(f32)
    text_inverse = lax.rsqrt(jnp.mean(text_wide * text_wide, axis=1, keepdims=True) + epsilon)
    text_normed = (text_wide * text_inverse * gain_wide).astype(bf16)
    text_low = dot_nt(text_normed, a_all).astype(bf16)
    owner_index = dp * n_mp + mp
    counts = jnp.sum((destiny.reshape(n_dp, ENC_DEV) == owner_index).astype(jnp.int32), axis=1)
    row = grp * text_count + jnp.arange(text_count, dtype=jnp.int32)
    taken = (row < area) & (
        row // n_dp
        < jnp.sum(
            jnp.where(
                (row % n_dp)[:, None] == jnp.arange(n_dp, dtype=jnp.int32)[None, :], counts, 0
            ),
            axis=1,
        )
    )
    keep = (row < own_length) & ~taken
    text_kept = jnp.where(keep[:, None], text_low, jnp.zeros_like(text_low))
    text_weight = 1.0 / own_length.astype(f32)
    text_sum = dot_tn(text_kept, text_normed) * text_weight
    own_text_targets = lax.dynamic_slice_in_dim(targets, grp * text_count, text_count).astype(f32)
    rest = bias_wide + dot(text_low, b_ranked) - own_text_targets
    rest_high, rest_low = split_two(rest)
    rest_sum = dot_tn(
        jnp.concatenate([text_kept, text_kept]), jnp.concatenate([rest_high, rest_low])
    )
    rest_sum = rest_sum * text_weight
    both_sums = jnp.concatenate([text_sum, rest_sum], axis=1)
    both_sums = both_sums[:half_rank] + crossed(both_sums[half_rank:])
    text_parts = both_sums[:, :width].reshape(half_rank, owners, shard).transpose(1, 0, 2)
    text_parts = lax.all_to_all(text_parts.astype(bf16), ("dp", "mp"), 0, 0, tiled=True)
    text_here = jnp.sum(text_parts.astype(f32), axis=0)
    here_high, here_low = split_two(text_here)
    text_grad = dot(jnp.concatenate([here_high, here_low]), value_weight)
    text_grad = text_grad[:half_rank] + text_grad[half_rank:] + both_sums[:, width:]
    text_grad = text_grad + (
        turned(text_grad, "mp", 1) + turned(text_grad, "mp", 2) + turned(text_grad, "mp", 3)
    )

    enc_low = dot(hid, enc_frozen).astype(bf16)
    merged = dot(hid, enc_weight) + enc_bias.astype(f32) + dot(enc_low, enc_adapter)
    image = merged.astype(bf16)
    image_wide = image.astype(f32)
    gain_part = lax.dynamic_slice_in_dim(gain_wide, mp * part_width, part_width)
    scaled_rows = (image_wide * gain_part).astype(bf16)
    squares = jnp.sum(image_wide * image_wide, axis=1, keepdims=True)
    part = jnp.concatenate(
        [
            dot(scaled_rows, w_mine),
            dot(scaled_rows, w_other),
            dot_nt(scaled_rows, a_part),
            jnp.broadcast_to(squares, (squares.shape[0], 128 - rank)),
        ],
        axis=1,
    )
    total = part[:mine_rows]
    for k in range(1, n_mp):
        total = total + turned(part[k * mine_rows : (k + 1) * mine_rows], "mp", -k)
    raw_values = total[:, :kv]
    raw_low = total[:, kv : kv + rank]
    inverse = lax.rsqrt(total[:, kv + rank : kv + rank + 1] / width + epsilon)
    low = (raw_low * inverse).astype(bf16)
    values_out = raw_values * inverse + bias_local + dot(low, b_local)
    dvalues = ((values_out - own_targets) * weight).astype(bf16)
    dlow = dot_nt(dvalues, b_local).astype(bf16)
    centre = (
        jnp.sum(dvalues.astype(f32) * raw_values, axis=1, keepdims=True)
        + jnp.sum(dlow.astype(f32) * raw_low, axis=1, keepdims=True)
    ) / width
    factor = inverse * inverse * inverse * centre
    packed = jnp.concatenate(
        [dvalues, low, *split_three(inverse), *split_three(factor), jnp.zeros((mine_rows, 58), bf16)],
        axis=1,
    )
    packed = jnp.concatenate([packed] + [turned(packed, "mp", k) for k in range(1, n_mp)])
    dvalues = packed[:, :kv]
    low = packed[:, kv : kv + rank]
    numbers = packed[:, kv + rank :].astype(f32)
    inverse = numbers[:, 0:1] + numbers[:, 1:2] + numbers[:, 2:3]
    factor = numbers[:, 3:4] + numbers[:, 4:5] + numbers[:, 5:6]
    dlow = dot_nt(dvalues, b_local).astype(bf16)
    dnormed = (
        dot_nt(dvalues[:, :half_kv], w_mine)
        + dot_nt(dvalues[:, half_kv:], w_other)
        + dot(dlow, a_part)
    )
    dimage = (inverse * (gain_part * dnormed) - image_wide * factor).astype(bf16)
    enc_grad = dot_tn(enc_low, dimage)
    llm_grad = dot_tn(low, dvalues)
    llm_grad = jnp.where(first, llm_grad, jnp.roll(llm_grad, half_kv, axis=1))

    enc_mine = lax.dynamic_slice_in_dim(enc_grad, grp * half_rank, half_rank)
    enc_give = lax.dynamic_slice_in_dim(enc_grad, (1 - grp) * half_rank, half_rank)
    mine = jnp.concatenate([enc_mine, llm_grad[:half_rank] + text_grad], axis=1)
    give = jnp.concatenate([enc_give, llm_grad[half_rank:]], axis=1)
    mine = mine + crossed(give)
    mine = mine.reshape(n_dp, half_rank // n_dp, -1)
    mine = jnp.sum(lax.all_to_all(mine, "dp", 0, 0, tiled=True), axis=0)
    whole = to_everyone(mine, "dp").reshape(half_rank, -1)
    return whole[:, :part_width], whole[:, part_width:]


def solution(mesh):
    return jax.shard_map(
        body,
        mesh=mesh,
        in_specs=(
            P(("dp", "mp"), None),
            P(None, "mp"),
            P("mp"),
            P(),
            P(None, "mp"),
            P(("dp", "mp"), None),
            P(),
            P(("dp", "mp"), None),
            P(),
            P(("dp", "mp"), None),
            P(),
            P(("dp", "mp"), None),
            P(),
            P(("dp", "mp")),
        ),
        out_specs=(P("grp", "mp"), P("grp", None)),
        check_vma=False,
    )
```

```python
import jax
import jax.numpy as jnp
from jax import lax
from jax.sharding import PartitionSpec as P

ENC_DEV = 256
epsilon = 1e-06
f32 = jnp.float32
bf16 = jnp.bfloat16


def dot(a, b):
    return jnp.dot(a, b, preferred_element_type=f32)


def dot_tn(a, b):
    return lax.dot_general(a, b, (((0,), (0,)), ((), ())), preferred_element_type=f32)


def dot_nt(a, b):
    return lax.dot_general(a, b, (((1,), (1,)), ((), ())), preferred_element_type=f32)


def split_two(a):
    high = lax.reduce_precision(a, 8, 7)
    return high.astype(bf16), (a - high).astype(bf16)


def split_three(a):
    high = lax.reduce_precision(a, 8, 7)
    return (high.astype(bf16), *split_two(a - high))


def turned(array, axis, step):
    count = lax.axis_size(axis)
    return lax.ppermute(array, axis, [(i, (i + step) % count) for i in range(count)])


def crossed(array):
    return lax.ppermute(array, "grp", [(0, 1), (1, 0)])


def along(array, z_step, x_step, side):
    pairs = [
        (z * side + x, (z + z_step) % side * side + (x + x_step) % side)
        for z in range(side)
        for x in range(side)
    ]
    return lax.ppermute(array, "dp", pairs)


def to_everyone(array, axes):
    count = lax.axis_size(axes)
    return lax.all_to_all(
        jnp.broadcast_to(array[None], (count, *array.shape)), axes, 0, 0, tiled=True
    )


def body(
    hidden,
    enc_weight,
    enc_bias,
    enc_frozen,
    enc_adapter,
    text_rows,
    norm_gain,
    value_weight,
    value_bias,
    llm_frozen,
    llm_adapter,
    targets,
    dest_owner,
    seq_length,
):
    n_dp = lax.axis_size("dp")
    n_mp = lax.axis_size("mp")
    side = n_mp
    owners = n_dp * n_mp
    grp = lax.axis_index("grp")
    dp = lax.axis_index("dp")
    mp = lax.axis_index("mp")
    first = grp == 0
    width = text_rows.shape[1]
    part_width = enc_weight.shape[1]
    rank = enc_frozen.shape[1]
    half_rank = rank // 2
    kv = value_weight.shape[1]
    half_kv = kv // 2
    shard = value_weight.shape[0]
    block_rows = hidden.shape[0]
    mine_rows = block_rows // 2
    capacity = 2 * ENC_DEV // owners

    swap = [
        ((z * side + x) * side + y, (y * side + x) * side + z)
        for z in range(side)
        for x in range(side)
        for y in range(side)
    ]
    col = dp % side
    w_half = lax.dynamic_slice_in_dim(value_weight, grp * half_kv, half_kv, axis=1)
    w_moved = lax.ppermute(w_half, ("dp", "mp"), swap)

    own_hidden = lax.dynamic_slice_in_dim(hidden, grp * mine_rows, mine_rows)
    hid = jnp.concatenate([own_hidden] + [turned(own_hidden, "mp", k) for k in range(1, n_mp)])

    w_line = [along(w_moved, k, 0, side) for k in (3, 2, 1)] + [w_moved]
    w_line = lax.dynamic_slice_in_dim(
        jnp.concatenate(w_line + w_line), ((side - 1 - dp // side) % side) * shard, side * shard
    )
    w_mine = jnp.zeros((side * side * shard, half_kv), bf16)
    for k in range(side):
        piece = along(w_line, 0, k, side) if k else w_line
        w_mine = lax.dynamic_update_slice_in_dim(
            w_mine, piece, ((col - k) % side) * (side * shard), axis=0
        )

    a_all = to_everyone(llm_frozen.T, ("dp", "mp")).transpose(1, 0, 2).reshape(rank, width)
    a_part = lax.dynamic_slice_in_dim(a_all, mp * part_width, part_width, axis=1)
    b_half = lax.dynamic_slice_in_dim(llm_adapter, grp * half_kv, half_kv, axis=1)
    bias_wide = value_bias.astype(f32)
    bias_half = lax.dynamic_slice_in_dim(bias_wide, grp * half_kv, half_kv)

    own_length = seq_length[0]
    area = capacity * n_dp
    t_half = lax.dynamic_slice(targets, (0, grp * half_kv), (area, half_kv))
    t_half = t_half.reshape(capacity, n_dp, half_kv).transpose(1, 0, 2)
    t_half = jnp.concatenate(
        [t_half, jnp.full((n_dp, capacity, 128), own_length.astype(bf16))], axis=2
    )
    t_here = lax.all_to_all(t_half, "dp", 0, 0, tiled=True).reshape(n_dp * capacity, -1)
    t_table = jnp.concatenate([t_here] + [turned(t_here, "mp", k) for k in range(1, n_mp)])
    destiny = dest_owner[:, 0]
    block_dest = lax.dynamic_slice_in_dim(destiny, dp * ENC_DEV, ENC_DEV)
    local = jnp.arange(ENC_DEV, dtype=jnp.int32)
    from_mp = (mp - local % (ENC_DEV // 2) // mine_rows) % n_mp
    from_grp = (grp + local // (ENC_DEV // 2)) % 2
    place = from_mp * block_rows + from_grp * mine_rows + local % mine_rows
    own_dest = jnp.sum(jnp.where(place[:, None] == local[None, :], block_dest[None, :], 0), axis=1)
    earlier = (own_dest[:, None] == block_dest[None, :]) & (local[None, :] < place[:, None])
    slot = jnp.sum(earlier.astype(jnp.int32), axis=1)
    source = (mp - own_dest % n_mp) % n_mp
    line = source * (n_dp * capacity) + (own_dest // n_mp) * capacity + slot
    pick = (line[:, None] == jnp.arange(n_mp * n_dp * capacity, dtype=jnp.int32)[None, :]).astype(
        bf16
    )
    picked = dot(pick, t_table)
    own_targets = picked[:, :half_kv]
    length = picked[:, half_kv : half_kv + 1]
    position = (slot * n_dp + dp)[:, None].astype(f32)
    weight = jnp.where(position < length, 1.0 / length, 0.0)

    gain_wide = norm_gain.astype(f32)
    text_count = text_rows.shape[0] // 2
    text_wide = lax.dynamic_slice_in_dim(text_rows, grp * text_count, text_count).astype(f32)
    text_inverse = lax.rsqrt(jnp.mean(text_wide * text_wide, axis=1, keepdims=True) + epsilon)
    text_normed = (text_wide * text_inverse * gain_wide).astype(bf16)
    text_low = dot_nt(text_normed, a_all).astype(bf16)
    owner_index = dp * n_mp + mp
    counts = jnp.sum((destiny.reshape(n_dp, ENC_DEV) == owner_index).astype(jnp.int32), axis=1)
    row = grp * text_count + jnp.arange(text_count, dtype=jnp.int32)
    taken = (row < area) & (
        row // n_dp
        < jnp.sum(
            jnp.where(
                (row % n_dp)[:, None] == jnp.arange(n_dp, dtype=jnp.int32)[None, :], counts, 0
            ),
            axis=1,
        )
    )
    keep = (row < own_length) & ~taken
    text_kept = jnp.where(keep[:, None], text_low, jnp.zeros_like(text_low))
    text_weight = 1.0 / own_length.astype(f32)
    text_sum = dot_tn(text_kept, text_normed) * text_weight
    own_text_targets = lax.dynamic_slice_in_dim(targets, grp * text_count, text_count).astype(f32)
    rest = bias_wide + dot(text_low, llm_adapter) - own_text_targets
    rest_high, rest_low = split_two(rest)
    rest_sum = dot_tn(
        jnp.concatenate([text_kept, text_kept]), jnp.concatenate([rest_high, rest_low])
    )
    rest_sum = rest_sum * text_weight
    text_here = lax.dynamic_slice_in_dim(text_sum, mp * part_width, part_width, axis=1)
    text_sent = text_sum.astype(bf16)
    for k in range(1, n_mp):
        block = lax.dynamic_slice_in_dim(
            text_sent, ((mp - k) % n_mp) * part_width, part_width, axis=1
        )
        text_here = text_here + turned(block, "mp", -k).astype(f32)
    rest_mine = lax.dynamic_slice_in_dim(rest_sum, grp * half_kv, half_kv, axis=1)
    rest_give = lax.dynamic_slice_in_dim(rest_sum, (1 - grp) * half_kv, half_kv, axis=1)
    came = crossed(jnp.concatenate([text_here, rest_give], axis=1))
    here_high, here_low = split_two(text_here + came[:, :part_width])
    text_grad = dot(jnp.concatenate([here_high, here_low]), w_mine)
    text_grad = text_grad[:rank] + text_grad[rank:] + rest_mine + came[:, part_width:]
    text_grad = text_grad + (
        turned(text_grad, "mp", 1) + turned(text_grad, "mp", 2) + turned(text_grad, "mp", 3)
    )

    enc_low = dot(hid, enc_frozen).astype(bf16)
    merged = dot(hid, enc_weight) + enc_bias.astype(f32) + dot(enc_low, enc_adapter)
    image = merged.astype(bf16)
    image = jnp.concatenate([image, crossed(image)])
    enc_low = jnp.concatenate([enc_low, crossed(enc_low)])
    image_wide = image.astype(f32)
    gain_part = lax.dynamic_slice_in_dim(gain_wide, mp * part_width, part_width)
    scaled_rows = (image_wide * gain_part).astype(bf16)
    squares = jnp.sum(image_wide * image_wide, axis=1, keepdims=True)
    part_values = dot(scaled_rows, w_mine)
    part_low = dot_nt(scaled_rows, a_part)
    pad = jnp.zeros((ENC_DEV, 128 - rank - 3), bf16)
    sent = jnp.concatenate(
        [part_values.astype(bf16), part_low.astype(bf16), *split_three(squares), pad], axis=1
    )
    total = jnp.concatenate(
        [part_values, part_low, squares, jnp.zeros((ENC_DEV, 128 - rank - 1), f32)], axis=1
    ).reshape(2, n_mp, mine_rows, -1)
    for k in range(1, n_mp):
        other = turned(sent, "mp", k).astype(f32)
        edge = half_kv + rank
        other_squares = (
            other[:, edge : edge + 1] + other[:, edge + 1 : edge + 2] + other[:, edge + 2 : edge + 3]
        )
        other = jnp.concatenate(
            [other[:, :edge], other_squares, jnp.zeros((ENC_DEV, 128 - rank - 1), f32)], axis=1
        )
        total = total + jnp.roll(other.reshape(2, n_mp, mine_rows, -1), k, axis=1)
    total = total.reshape(ENC_DEV, -1)
    raw_values = total[:, :half_kv]
    raw_low = total[:, half_kv : half_kv + rank]
    inverse = lax.rsqrt(total[:, half_kv + rank : half_kv + rank + 1] / width + epsilon)
    low = (raw_low * inverse).astype(bf16)
    values_out = raw_values * inverse + bias_half + dot(low, b_half)
    dvalues = ((values_out - own_targets) * weight).astype(bf16)
    dlow = dot_nt(dvalues, b_half).astype(bf16)
    centre = (
        jnp.sum(dvalues.astype(f32) * raw_values, axis=1, keepdims=True)
        + jnp.sum(dlow.astype(f32) * raw_low, axis=1, keepdims=True)
    ) / width
    factor = inverse * inverse * inverse * centre
    dnormed = dot_nt(dvalues, w_mine) + dot(dlow, a_part)
    dimage = (inverse * (gain_part * dnormed) - image_wide * factor).astype(bf16)
    enc_grad = dot_tn(enc_low, dimage)
    llm_grad = dot_tn(low, dvalues) + text_grad

    both = jnp.concatenate([enc_grad, llm_grad], axis=1)
    mine = lax.dynamic_slice_in_dim(both, grp * half_rank, half_rank)
    came = crossed(lax.dynamic_slice_in_dim(both, (1 - grp) * half_rank, half_rank))
    llm_mine, llm_came = mine[:, part_width:], came[:, part_width:]
    mine = jnp.concatenate(
        [
            mine[:, :part_width] + came[:, :part_width],
            jnp.where(first, llm_mine, llm_came),
            jnp.where(first, llm_came, llm_mine),
        ],
        axis=1,
    )
    mine = mine.reshape(n_dp, half_rank // n_dp, -1)
    mine = jnp.sum(lax.all_to_all(mine, "dp", 0, 0, tiled=True), axis=0)
    whole = to_everyone(mine, "dp").reshape(half_rank, -1)
    return whole[:, :part_width], whole[:, part_width:]


def solution(mesh):
    return jax.shard_map(
        body,
        mesh=mesh,
        in_specs=(
            P(("dp", "mp"), None),
            P(None, "mp"),
            P("mp"),
            P(),
            P(None, "mp"),
            P(("dp", "mp"), None),
            P(),
            P(("dp", "mp"), None),
            P(),
            P(("dp", "mp"), None),
            P(),
            P(("dp", "mp"), None),
            P(),
            P(("dp", "mp")),
        ),
        out_specs=(P("grp", "mp"), P("grp", None)),
        check_vma=False,
    )
```

```python
import functools

import jax
import jax.numpy as jnp
from jax import lax
from jax.experimental import pallas as pl
from jax.experimental.pallas import tpu as pltpu
from jax.sharding import PartitionSpec as P

ENC_DEV = 256
epsilon = 1e-06
f32 = jnp.float32
bf16 = jnp.bfloat16


def dot(a, b):
    return jnp.dot(a, b, preferred_element_type=f32)


def dot_tn(a, b):
    return lax.dot_general(a, b, (((0,), (0,)), ((), ())), preferred_element_type=f32)


def dot_nt(a, b):
    return lax.dot_general(a, b, (((1,), (1,)), ((), ())), preferred_element_type=f32)


def split_two(a):
    high = lax.reduce_precision(a, 8, 7)
    return high.astype(bf16), (a - high).astype(bf16)


def split_three(a):
    high = lax.reduce_precision(a, 8, 7)
    return (high.astype(bf16), *split_two(a - high))


def turned(array, axis, step):
    count = lax.axis_size(axis)
    return lax.ppermute(array, axis, [(i, (i + step) % count) for i in range(count)])


def crossed(array):
    return lax.ppermute(array, "grp", [(0, 1), (1, 0)])


def along(array, z_step, x_step, side):
    pairs = [
        (z * side + x, (z + z_step) % side * side + (x + x_step) % side)
        for z in range(side)
        for x in range(side)
    ]
    return lax.ppermute(array, "dp", pairs)


def to_everyone(array, axes):
    count = lax.axis_size(axes)
    return lax.all_to_all(
        jnp.broadcast_to(array[None], (count, *array.shape)), axes, 0, 0, tiled=True
    )


def cut(array, start, size, axis=0):
    starts = [jnp.int32(0)] * array.ndim
    starts[axis] = start
    sizes = list(array.shape)
    sizes[axis] = size
    return lax.dynamic_slice(array, starts, sizes, allow_negative_indices=False)


VMEM = pl.BlockSpec(memory_space=pltpu.VMEM)
SMEM = pl.BlockSpec(memory_space=pltpu.SMEM)
PARAMS = pltpu.CompilerParams(vmem_limit_bytes=48 * 1024 * 1024)


def block_start(col, k, side, size):
    return pl.multiple_of(((col + side - k) & (side - 1)) * size, 128)


def partial_kernel(
    place, near, far, gain, a_part, w0, w1, w2, w3, sent, kept, *, block, half_kv, rank, chunk
):
    rows = near.shape[0]
    pieces = (w0, w1, w2, w3)
    side = len(pieces)
    for h, source in enumerate((near, far)):
        values = jnp.zeros((rows, half_kv), f32)
        low = jnp.zeros((rows, rank), f32)
        squares = jnp.zeros((rows, 1), f32)
        for k, piece in enumerate(pieces):
            here = pl.ds(block_start(place[0], k, side, block), block)
            wide = source[:, here].astype(f32)
            scaled = (wide * gain[:, here]).astype(bf16)
            squares = squares + jnp.sum(wide * wide, axis=1, keepdims=True)
            values = values + dot(scaled, piece[:block, :])
            low = low + dot_nt(scaled, a_part[:, here])
        out = slice(h * rows, (h + 1) * rows)
        kept[out, :half_kv] = values
        high = squares.astype(bf16)
        left = squares - high.astype(f32)
        middle = left.astype(bf16)
        last = left - middle.astype(f32)
        lane = lax.broadcasted_iota(jnp.int32, (rows, rank), 1)
        three = jnp.where(
            lane == 0,
            high.astype(f32),
            jnp.where(lane == 1, middle.astype(f32), jnp.where(lane == 2, last, 0.0)),
        )
        extra = jnp.concatenate([low, three], axis=1)
        kept[out, half_kv:] = extra
        sent[out, :half_kv] = values.astype(bf16)
        sent[out, half_kv:] = extra.astype(bf16)
    per = chunk // 2
    for k, piece in enumerate(pieces):
        for pair in range(side // 2):
            wide, lengths = [], []
            for z in (2 * pair, 2 * pair + 1):
                both = piece[block + z * chunk : block + (z + 1) * chunk, :].astype(f32)
                wide.append(both[:per])
                lengths.append(both[per:, :128])
            at = 2 * rows + (k * side + 2 * pair) * per
            sent[at : at + chunk, :half_kv] = jnp.concatenate(wide).astype(bf16)
            sent[at : at + chunk, half_kv:] = jnp.concatenate(lengths).astype(bf16)


def image_kernel(
    place,
    kept,
    sent,
    got1,
    got2,
    got3,
    near,
    far,
    low_near,
    low_far,
    gain,
    a_part,
    w0,
    w1,
    w2,
    w3,
    b_half,
    bias,
    line,
    position,
    out,
    *,
    block,
    half_kv,
    rank,
    width,
    step,
):
    pieces = (w0, w1, w2, w3)
    side = len(pieces)
    got = (got1, got2, got3)
    count = kept.shape[0]
    parts = []
    for h in range(2):
        for p in range(side):
            at = h * side * step + p * step
            total = kept[at : at + step, :]
            for k in range(1, side):
                there = h * side * step + ((p - k) % side) * step
                total = total + got[k - 1][there : there + step, :].astype(f32)
            parts.append(total)
    total = jnp.concatenate(parts)
    raw_values = total[:, :half_kv]
    raw_low = total[:, half_kv : half_kv + rank]
    squares = jnp.sum(total[:, half_kv + rank :], axis=1, keepdims=True)
    lines = side * (sent.shape[0] - count)
    pick = (line[...] == lax.broadcasted_iota(jnp.int32, (count, lines), 1)).astype(bf16)
    table = jnp.concatenate([sent[count:, :]] + [g[count:, :] for g in got])
    picked = dot(pick, table)
    length = picked[:, half_kv : half_kv + 1]
    weight = jnp.where(position[...] < length, 1.0 / length, 0.0)
    inverse = lax.rsqrt(squares / width + epsilon)
    low = (raw_low * inverse).astype(bf16)
    values_out = raw_values * inverse + bias[...] + dot(low, b_half[...])
    dvalues = ((values_out - picked[:, :half_kv]) * weight).astype(bf16)
    dlow = dot_nt(dvalues, b_half[...]).astype(bf16)
    centre = (
        jnp.sum(dvalues.astype(f32) * raw_values, axis=1, keepdims=True)
        + jnp.sum(dlow.astype(f32) * raw_low, axis=1, keepdims=True)
    ) / width
    factor = inverse * inverse * inverse * centre
    out[:, side * block :] = dot_tn(low, dvalues)
    enc_low = jnp.concatenate([low_near[...], low_far[...]])
    for k, piece in enumerate(pieces):
        here = pl.ds(block_start(place[0], k, side, block), block)
        dnormed = dot_nt(dvalues, piece[:block, :]) + dot(dlow, a_part[:, here])
        wide = jnp.concatenate([near[:, here], far[:, here]]).astype(f32)
        dimage = (inverse * (gain[:, here] * dnormed) - wide * factor).astype(bf16)
        out[:, here] = dot_tn(enc_low, dimage)


def body(
    hidden,
    enc_weight,
    enc_bias,
    enc_frozen,
    enc_adapter,
    text_rows,
    norm_gain,
    value_weight,
    value_bias,
    llm_frozen,
    llm_adapter,
    targets,
    dest_owner,
    seq_length,
):
    n_dp = lax.axis_size("dp")
    n_mp = lax.axis_size("mp")
    side = n_mp
    owners = n_dp * n_mp
    grp = lax.axis_index("grp")
    dp = lax.axis_index("dp")
    mp = lax.axis_index("mp")
    first = grp == 0
    width = text_rows.shape[1]
    part_width = enc_weight.shape[1]
    rank = enc_frozen.shape[1]
    half_rank = rank // 2
    kv = value_weight.shape[1]
    half_kv = kv // 2
    shard = value_weight.shape[0]
    block = side * shard
    block_rows = hidden.shape[0]
    mine_rows = block_rows // 2
    capacity = 2 * ENC_DEV // owners
    chunk = 2 * capacity
    area = capacity * n_dp
    slab, col = dp // side, dp & (side - 1)
    wrap = side - 1

    swap = [
        ((z * side + x) * side + y, (y * side + x) * side + z)
        for z in range(side)
        for x in range(side)
        for y in range(side)
    ]
    w_half = cut(value_weight, grp * half_kv, half_kv, 1)
    w_moved = lax.ppermute(w_half, ("dp", "mp"), swap)

    own_hidden = cut(hidden, grp * mine_rows, mine_rows)
    hid = jnp.concatenate([own_hidden] + [turned(own_hidden, "mp", k) for k in range(1, n_mp)])

    own_length = seq_length[0]
    t_half = cut(targets[:area], grp * half_kv, half_kv, 1)
    t_half = t_half.reshape(capacity, n_dp, half_kv).transpose(1, 0, 2)
    t_half = jnp.concatenate([t_half, jnp.full_like(t_half, own_length.astype(bf16))], axis=1)
    t_half = t_half.reshape(side, side * chunk, half_kv)
    w_line, t_line = [w_moved], [cut(t_half, slab, 1)[0]]
    for k in range(1, side):
        t_given = cut(t_half, (slab + k) & wrap, 1)[0]
        came = along(jnp.concatenate([w_moved, t_given]), k, 0, side)
        w_line.append(came[:shard])
        t_line.append(came[shard:])
    w_line = w_line[::-1]
    w_line = cut(jnp.concatenate(w_line + w_line), ((2 * side - 1 - slab) & wrap) * shard, block)
    t_line = jnp.stack(t_line).reshape(side, side, chunk, half_kv)
    pieces = []
    for k in range(side):
        t_given = cut(t_line, (col + k) & wrap, 1, 1).reshape(side * chunk, half_kv)
        piece = jnp.concatenate([w_line, t_given])
        pieces.append(along(piece, 0, k, side) if k else piece)

    a_turned = jnp.where(first, llm_frozen.T, jnp.roll(llm_frozen.T, half_rank, axis=0))
    a_all = to_everyone(a_turned, ("dp", "mp")).transpose(1, 0, 2).reshape(rank, width)
    a_part = cut(a_all, mp * part_width, part_width, 1)
    b_all = jnp.where(first, llm_adapter, jnp.roll(llm_adapter, half_rank, axis=0))
    b_half = cut(b_all, grp * half_kv, half_kv, 1)
    bias_wide = value_bias.astype(f32)[None]
    bias_half = cut(bias_wide, grp * half_kv, half_kv, 1)

    destiny = dest_owner[:, 0]
    block_dest = cut(destiny, dp * ENC_DEV, ENC_DEV)
    local = jnp.arange(ENC_DEV, dtype=jnp.int32)
    from_mp = (mp - (local % (ENC_DEV // 2)) // mine_rows) & wrap
    from_grp = (grp + local // (ENC_DEV // 2)) & 1
    place = from_mp * block_rows + from_grp * mine_rows + (local & (mine_rows - 1))
    own_dest = jnp.sum(jnp.where(place[:, None] == local[None, :], block_dest[None, :], 0), axis=1)
    earlier = (own_dest[:, None] == block_dest[None, :]) & (local[None, :] < place[:, None])
    slot = jnp.sum(earlier.astype(jnp.int32), axis=1)
    own_mp, own_col, own_slab = own_dest & wrap, (own_dest // side) & wrap, own_dest // (side * side)
    line = (((mp - own_mp) & wrap) * side + ((col - own_col) & wrap)) * side
    line = (line + ((slab - own_slab) & wrap)) * capacity + slot
    position = (slot * n_dp + dp).astype(f32)

    gain_wide = norm_gain.astype(f32)[None]
    text_count = text_rows.shape[0] // 2
    text_wide = cut(text_rows, grp * text_count, text_count).astype(f32)
    text_inverse = lax.rsqrt(jnp.mean(text_wide * text_wide, axis=1, keepdims=True) + epsilon)
    text_normed = (text_wide * text_inverse * gain_wide).astype(bf16)
    text_low = dot_nt(text_normed, a_all).astype(bf16)
    owner_index = dp * n_mp + mp
    counts = jnp.sum((destiny.reshape(n_dp, ENC_DEV) == owner_index).astype(jnp.int32), axis=1)
    row = grp * text_count + jnp.arange(text_count, dtype=jnp.int32)
    taken = (row < area) & (
        row // n_dp
        < jnp.sum(
            jnp.where(
                (row & (n_dp - 1))[:, None] == jnp.arange(n_dp, dtype=jnp.int32)[None, :],
                counts,
                0,
            ),
            axis=1,
        )
    )
    keep = (row < own_length) & ~taken
    text_kept = jnp.where(keep[:, None], text_low, jnp.zeros_like(text_low))
    text_weight = 1.0 / own_length.astype(f32)
    text_sum = dot_tn(text_kept, text_normed) * text_weight
    own_text_targets = cut(targets, grp * text_count, text_count).astype(f32)
    rest = bias_wide + dot(text_low, b_all) - own_text_targets
    rest_high, rest_low = split_two(rest)
    rest_sum = dot_tn(
        jnp.concatenate([text_kept, text_kept]), jnp.concatenate([rest_high, rest_low])
    )
    rest_sum = rest_sum * text_weight
    text_here = cut(text_sum, mp * part_width, part_width, 1)
    text_sent = text_sum.astype(bf16)
    for k in range(1, n_mp):
        given = cut(text_sent, ((mp - k) & wrap) * part_width, part_width, 1)
        text_here = text_here + turned(given, "mp", -k).astype(f32)
    rest_mine = cut(rest_sum, grp * half_kv, half_kv, 1)
    rest_give = cut(rest_sum, (1 - grp) * half_kv, half_kv, 1)
    came = jnp.roll(crossed(jnp.concatenate([text_here, rest_give], axis=1)), half_rank, axis=0)
    here_high, here_low = split_two(text_here + came[:, :part_width])
    here_both = jnp.concatenate([here_high, here_low])
    text_grad = jnp.zeros((2 * rank, half_kv), f32)
    for k in range(side):
        given = cut(here_both, ((col - k) & wrap) * block, block, 1)
        text_grad = text_grad + dot(given, pieces[k][:block])
    text_grad = text_grad[:rank] + text_grad[rank:] + rest_mine + came[:, part_width:]
    text_grad = text_grad + (
        turned(text_grad, "mp", 1) + turned(text_grad, "mp", 2) + turned(text_grad, "mp", 3)
    )

    enc_low = dot(hid, enc_frozen).astype(bf16)
    merged = dot(hid, enc_weight) + enc_bias.astype(f32) + dot(enc_low, enc_adapter)
    image = merged.astype(bf16)
    image_far = crossed(image)
    enc_low = jnp.where(first, enc_low, jnp.roll(enc_low, half_rank, axis=1))
    enc_low_far = jnp.roll(crossed(enc_low), half_rank, axis=1)
    gain_part = cut(gain_wide, mp * part_width, part_width, 1)
    where = col[None].astype(jnp.int32)
    sizes = dict(block=block, half_kv=half_kv, rank=rank)
    sent, kept = pl.pallas_call(
        functools.partial(partial_kernel, chunk=chunk, **sizes),
        out_shape=(
            jax.ShapeDtypeStruct((ENC_DEV + area, half_kv + 128), bf16),
            jax.ShapeDtypeStruct((ENC_DEV, half_kv + 128), f32),
        ),
        in_specs=[SMEM] + [VMEM] * 8,
        out_specs=(VMEM, VMEM),
        compiler_params=PARAMS,
        name="partial_products",
    )(where, image, image_far, gain_part, a_part, *pieces)
    got = [turned(sent, "mp", k) for k in range(1, n_mp)]
    both = pl.pallas_call(
        functools.partial(image_kernel, width=float(width), step=mine_rows, **sizes),
        out_shape=jax.ShapeDtypeStruct((rank, part_width + half_kv), f32),
        in_specs=[SMEM] + [VMEM] * 19,
        out_specs=VMEM,
        compiler_params=PARAMS,
        name="image_gradients",
    )(
        where,
        kept,
        sent,
        *got,
        image,
        image_far,
        enc_low,
        enc_low_far,
        gain_part,
        a_part,
        *pieces,
        b_half,
        bias_half,
        line[:, None],
        position[:, None],
    )

    both = jnp.concatenate([both[:, :part_width], both[:, part_width:] + text_grad], axis=1)
    mine = both[:half_rank]
    came = crossed(both[half_rank:])
    llm_mine, llm_came = mine[:, part_width:], came[:, part_width:]
    mine = jnp.concatenate(
        [
            mine[:, :part_width] + came[:, :part_width],
            jnp.where(first, llm_mine, llm_came),
            jnp.where(first, llm_came, llm_mine),
        ],
        axis=1,
    )
    mine = mine.reshape(n_dp, half_rank // n_dp, -1)
    mine = jnp.sum(lax.all_to_all(mine, "dp", 0, 0, tiled=True), axis=0)
    whole = to_everyone(mine, "dp").reshape(half_rank, -1)
    return whole[:, :part_width], whole[:, part_width:]


def solution(mesh):
    return jax.shard_map(
        body,
        mesh=mesh,
        in_specs=(
            P(("dp", "mp"), None),
            P(None, "mp"),
            P("mp"),
            P(),
            P(None, "mp"),
            P(("dp", "mp"), None),
            P(),
            P(("dp", "mp"), None),
            P(),
            P(("dp", "mp"), None),
            P(),
            P(("dp", "mp"), None),
            P(),
            P(("dp", "mp")),
        ),
        out_specs=(P("grp", "mp"), P("grp", None)),
        check_vma=False,
    )
```

```python
import functools

import jax
import jax.numpy as jnp
from jax import lax
from jax.experimental import pallas as pl
from jax.experimental.pallas import tpu as pltpu
from jax.sharding import PartitionSpec as P

ENC_DEV = 256
epsilon = 1e-06
f32 = jnp.float32
bf16 = jnp.bfloat16


def dot(a, b):
    return jnp.dot(a, b, preferred_element_type=f32)


def dot_tn(a, b):
    return lax.dot_general(a, b, (((0,), (0,)), ((), ())), preferred_element_type=f32)


def dot_nt(a, b):
    return lax.dot_general(a, b, (((1,), (1,)), ((), ())), preferred_element_type=f32)


def split_two(a):
    high = lax.reduce_precision(a, 8, 7)
    return high.astype(bf16), (a - high).astype(bf16)


def split_three(a):
    high = lax.reduce_precision(a, 8, 7)
    return (high.astype(bf16), *split_two(a - high))


def turned(array, axis, step):
    count = lax.axis_size(axis)
    return lax.ppermute(array, axis, [(i, (i + step) % count) for i in range(count)])


def crossed(array):
    return lax.ppermute(array, "grp", [(0, 1), (1, 0)])


def along(array, z_step, x_step, side):
    pairs = [
        (z * side + x, (z + z_step) % side * side + (x + x_step) % side)
        for z in range(side)
        for x in range(side)
    ]
    return lax.ppermute(array, "dp", pairs)


def to_everyone(array, axes):
    count = lax.axis_size(axes)
    return lax.all_to_all(
        jnp.broadcast_to(array[None], (count, *array.shape)), axes, 0, 0, tiled=True
    )


def cut(array, start, size, axis=0):
    starts = [jnp.int32(0)] * array.ndim
    starts[axis] = start
    sizes = list(array.shape)
    sizes[axis] = size
    return lax.dynamic_slice(array, starts, sizes, allow_negative_indices=False)


VMEM = pl.BlockSpec(memory_space=pltpu.VMEM)
SMEM = pl.BlockSpec(memory_space=pltpu.SMEM)
PARAMS = pltpu.CompilerParams(vmem_limit_bytes=48 * 1024 * 1024)


def block_start(col, k, side, size):
    return pl.multiple_of(((col + side - k) & (side - 1)) * size, 128)


def partial_kernel(
    place, near, far, gain, a_part, w0, w1, w2, w3, sent, kept, *, block, half_kv, rank, chunk
):
    rows = near.shape[0]
    pieces = (w0, w1, w2, w3)
    side = len(pieces)
    for h, source in enumerate((near, far)):
        values = jnp.zeros((rows, half_kv), f32)
        low = jnp.zeros((rows, rank), f32)
        squares = jnp.zeros((rows, 1), f32)
        for k, piece in enumerate(pieces):
            here = pl.ds(block_start(place[0], k, side, block), block)
            wide = source[:, here].astype(f32)
            scaled = (wide * gain[:, here]).astype(bf16)
            squares = squares + jnp.sum(wide * wide, axis=1, keepdims=True)
            values = values + dot(scaled, piece[:block, :])
            low = low + dot_nt(scaled, a_part[:, here])
        out = slice(h * rows, (h + 1) * rows)
        kept[out, :half_kv] = values
        high = squares.astype(bf16)
        left = squares - high.astype(f32)
        middle = left.astype(bf16)
        last = left - middle.astype(f32)
        lane = lax.broadcasted_iota(jnp.int32, (rows, rank), 1)
        three = jnp.where(
            lane == 0,
            high.astype(f32),
            jnp.where(lane == 1, middle.astype(f32), jnp.where(lane == 2, last, 0.0)),
        )
        extra = jnp.concatenate([low, three], axis=1)
        kept[out, half_kv:] = extra
        sent[out, :half_kv] = values.astype(bf16)
        sent[out, half_kv:] = extra.astype(bf16)
    per = chunk // 2
    for k, piece in enumerate(pieces):
        for pair in range(side // 2):
            wide, lengths = [], []
            for z in (2 * pair, 2 * pair + 1):
                both = piece[block + z * chunk : block + (z + 1) * chunk, :].astype(f32)
                wide.append(both[:per])
                lengths.append(both[per:, :128])
            at = 2 * rows + (k * side + 2 * pair) * per
            sent[at : at + chunk, :half_kv] = jnp.concatenate(wide).astype(bf16)
            sent[at : at + chunk, half_kv:] = jnp.concatenate(lengths).astype(bf16)


def image_kernel(
    place,
    kept,
    sent,
    got1,
    got2,
    got3,
    near,
    far,
    low_near,
    low_far,
    gain,
    a_part,
    w0,
    w1,
    w2,
    w3,
    b_half,
    bias,
    line,
    position,
    mine,
    give,
    *,
    block,
    half_kv,
    rank,
    width,
    step,
):
    pieces = (w0, w1, w2, w3)
    side = len(pieces)
    got = (got1, got2, got3)
    count = kept.shape[0]
    parts = []
    for h in range(2):
        for p in range(side):
            at = h * side * step + p * step
            total = kept[at : at + step, :]
            for k in range(1, side):
                there = h * side * step + ((p - k) % side) * step
                total = total + got[k - 1][there : there + step, :].astype(f32)
            parts.append(total)
    total = jnp.concatenate(parts)
    raw_values = total[:, :half_kv]
    raw_low = total[:, half_kv : half_kv + rank]
    squares = jnp.sum(total[:, half_kv + rank :], axis=1, keepdims=True)
    lines = side * (sent.shape[0] - count)
    pick = (line[...] == lax.broadcasted_iota(jnp.int32, (count, lines), 1)).astype(bf16)
    table = jnp.concatenate([sent[count:, :]] + [g[count:, :] for g in got])
    picked = dot(pick, table)
    length = picked[:, half_kv : half_kv + 1]
    weight = jnp.where(position[...] < length, 1.0 / length, 0.0)
    inverse = lax.rsqrt(squares / width + epsilon)
    low = (raw_low * inverse).astype(bf16)
    values_out = raw_values * inverse + bias[...] + dot(low, b_half[...])
    dvalues = ((values_out - picked[:, :half_kv]) * weight).astype(bf16)
    dlow = dot_nt(dvalues, b_half[...]).astype(bf16)
    centre = (
        jnp.sum(dvalues.astype(f32) * raw_values, axis=1, keepdims=True)
        + jnp.sum(dlow.astype(f32) * raw_low, axis=1, keepdims=True)
    ) / width
    factor = inverse * inverse * inverse * centre
    grad = dot_tn(low, dvalues)
    half = rank // 2
    mine[:, side * block :] = grad[:half]
    give[:, side * block :] = grad[half:]
    enc_low = jnp.concatenate([low_near[...], low_far[...]])
    for k, piece in enumerate(pieces):
        here = pl.ds(block_start(place[0], k, side, block), block)
        dnormed = dot_nt(dvalues, piece[:block, :]) + dot(dlow, a_part[:, here])
        wide = jnp.concatenate([near[:, here], far[:, here]]).astype(f32)
        dimage = (inverse * (gain[:, here] * dnormed) - wide * factor).astype(bf16)
        grad = dot_tn(enc_low, dimage)
        mine[:, here] = grad[:half]
        give[:, here] = grad[half:]


def body(
    hidden,
    enc_weight,
    enc_bias,
    enc_frozen,
    enc_adapter,
    text_rows,
    norm_gain,
    value_weight,
    value_bias,
    llm_frozen,
    llm_adapter,
    targets,
    dest_owner,
    seq_length,
):
    n_dp = lax.axis_size("dp")
    n_mp = lax.axis_size("mp")
    side = n_mp
    owners = n_dp * n_mp
    grp = lax.axis_index("grp")
    dp = lax.axis_index("dp")
    mp = lax.axis_index("mp")
    first = grp == 0
    width = text_rows.shape[1]
    part_width = enc_weight.shape[1]
    rank = enc_frozen.shape[1]
    half_rank = rank // 2
    kv = value_weight.shape[1]
    half_kv = kv // 2
    shard = value_weight.shape[0]
    block = side * shard
    block_rows = hidden.shape[0]
    mine_rows = block_rows // 2
    capacity = 2 * ENC_DEV // owners
    chunk = 2 * capacity
    area = capacity * n_dp
    slab, col = dp // side, dp & (side - 1)
    wrap = side - 1

    swap = [
        ((z * side + x) * side + y, (y * side + x) * side + z)
        for z in range(side)
        for x in range(side)
        for y in range(side)
    ]
    w_half = cut(value_weight, grp * half_kv, half_kv, 1)
    w_moved = lax.ppermute(w_half, ("dp", "mp"), swap)

    own_hidden = cut(hidden, grp * mine_rows, mine_rows)
    hid_next, hid_last = turned(own_hidden, "mp", 1), turned(own_hidden, "mp", -1)
    hid = jnp.concatenate([own_hidden, hid_next, turned(hid_next, "mp", 1), hid_last])

    own_length = seq_length[0]
    t_half = cut(targets[:area], grp * half_kv, half_kv, 1)
    t_half = t_half.reshape(capacity, n_dp, half_kv).transpose(1, 0, 2)
    t_half = jnp.concatenate([t_half, jnp.full_like(t_half, own_length.astype(bf16))], axis=1)
    t_half = t_half.reshape(side, side * chunk, half_kv)
    w_line, t_line = [w_moved], [cut(t_half, slab, 1)[0]]
    for k in range(1, side):
        t_given = cut(t_half, (slab + k) & wrap, 1)[0]
        came = along(jnp.concatenate([w_moved, t_given]), k, 0, side)
        w_line.append(came[:shard])
        t_line.append(came[shard:])
    w_line = w_line[::-1]
    w_line = cut(jnp.concatenate(w_line + w_line), ((2 * side - 1 - slab) & wrap) * shard, block)
    t_line = jnp.stack(t_line).reshape(side, side, chunk, half_kv)
    pieces = []
    for k in range(side):
        t_given = cut(t_line, (col + k) & wrap, 1, 1).reshape(side * chunk, half_kv)
        piece = jnp.concatenate([w_line, t_given])
        pieces.append(along(piece, 0, k, side) if k else piece)

    a_half, _ = lax.optimization_barrier((cut(llm_frozen.T, grp * half_rank, half_rank), w_moved))
    a_mine = to_everyone(a_half, ("dp", "mp")).transpose(1, 0, 2).reshape(half_rank, width)
    a_all = jnp.concatenate([a_mine, crossed(a_mine)])
    a_part = cut(a_all, mp * part_width, part_width, 1)
    b_all = jnp.where(first, llm_adapter, jnp.roll(llm_adapter, half_rank, axis=0))
    b_half = cut(b_all, grp * half_kv, half_kv, 1)
    bias_wide = value_bias.astype(f32)[None]
    bias_half = cut(bias_wide, grp * half_kv, half_kv, 1)

    destiny = dest_owner[:, 0]
    block_dest = cut(destiny, dp * ENC_DEV, ENC_DEV)
    local = jnp.arange(ENC_DEV, dtype=jnp.int32)
    from_mp = (mp - (local % (ENC_DEV // 2)) // mine_rows) & wrap
    from_grp = (grp + local // (ENC_DEV // 2)) & 1
    place = from_mp * block_rows + from_grp * mine_rows + (local & (mine_rows - 1))
    own_dest = jnp.sum(jnp.where(place[:, None] == local[None, :], block_dest[None, :], 0), axis=1)
    earlier = (own_dest[:, None] == block_dest[None, :]) & (local[None, :] < place[:, None])
    slot = jnp.sum(earlier.astype(jnp.int32), axis=1)
    own_mp, own_col, own_slab = own_dest & wrap, (own_dest // side) & wrap, own_dest // (side * side)
    line = (((mp - own_mp) & wrap) * side + ((col - own_col) & wrap)) * side
    line = (line + ((slab - own_slab) & wrap)) * capacity + slot
    position = (slot * n_dp + dp).astype(f32)

    gain_wide = norm_gain.astype(f32)[None]
    text_count = text_rows.shape[0] // 2
    text_wide = cut(text_rows, grp * text_count, text_count).astype(f32)
    text_inverse = lax.rsqrt(jnp.mean(text_wide * text_wide, axis=1, keepdims=True) + epsilon)
    text_normed = (text_wide * text_inverse * gain_wide).astype(bf16)
    text_low = dot_nt(text_normed, a_all).astype(bf16)
    owner_index = dp * n_mp + mp
    counts = jnp.sum((destiny.reshape(n_dp, ENC_DEV) == owner_index).astype(jnp.int32), axis=1)
    row = grp * text_count + jnp.arange(text_count, dtype=jnp.int32)
    taken = (row < area) & (
        row // n_dp
        < jnp.sum(
            jnp.where(
                (row & (n_dp - 1))[:, None] == jnp.arange(n_dp, dtype=jnp.int32)[None, :],
                counts,
                0,
            ),
            axis=1,
        )
    )
    keep = (row < own_length) & ~taken
    text_kept = jnp.where(keep[:, None], text_low, jnp.zeros_like(text_low))
    text_weight = 1.0 / own_length.astype(f32)
    text_sum = dot_tn(text_kept, text_normed) * text_weight
    own_text_targets = cut(targets, grp * text_count, text_count).astype(f32)
    rest = bias_wide + dot(text_low, b_all) - own_text_targets
    rest_high, rest_low = split_two(rest)
    rest_sum = dot_tn(
        jnp.concatenate([text_kept, text_kept]), jnp.concatenate([rest_high, rest_low])
    )
    rest_sum = rest_sum * text_weight
    both_sums = jnp.concatenate([text_sum, rest_sum], axis=1)
    both_sums = both_sums[:half_rank] + crossed(both_sums[half_rank:])
    text_parts = both_sums[:, :width].reshape(half_rank, owners, shard).transpose(1, 0, 2)
    text_parts = lax.all_to_all(text_parts.astype(bf16), ("dp", "mp"), 0, 0, tiled=True)
    text_here = jnp.sum(text_parts.astype(f32), axis=0)
    here_high, here_low = split_two(text_here)
    text_grad = dot(jnp.concatenate([here_high, here_low]), value_weight)
    text_grad = text_grad[:half_rank] + text_grad[half_rank:] + both_sums[:, width:]
    text_grad = text_grad + (
        turned(text_grad, "mp", 1) + turned(text_grad, "mp", 2) + turned(text_grad, "mp", 3)
    )

    enc_low = dot(hid, enc_frozen).astype(bf16)
    merged = dot(hid, enc_weight) + enc_bias.astype(f32) + dot(enc_low, enc_adapter)
    image = merged.astype(bf16)
    image_far = crossed(image)
    enc_low = jnp.where(first, enc_low, jnp.roll(enc_low, half_rank, axis=1))
    enc_low_far = jnp.roll(crossed(enc_low), half_rank, axis=1)
    gain_part = cut(gain_wide, mp * part_width, part_width, 1)
    where = col[None].astype(jnp.int32)
    sizes = dict(block=block, half_kv=half_kv, rank=rank)
    sent, kept = pl.pallas_call(
        functools.partial(partial_kernel, chunk=chunk, **sizes),
        out_shape=(
            jax.ShapeDtypeStruct((ENC_DEV + area, half_kv + 128), bf16),
            jax.ShapeDtypeStruct((ENC_DEV, half_kv + 128), f32),
        ),
        in_specs=[SMEM] + [VMEM] * 8,
        out_specs=(VMEM, VMEM),
        compiler_params=PARAMS,
        name="partial_products",
    )(where, image, image_far, gain_part, a_part, *pieces)
    got = [turned(sent, "mp", k) for k in range(1, n_mp)]
    mine, give = pl.pallas_call(
        functools.partial(image_kernel, width=float(width), step=mine_rows, **sizes),
        out_shape=(jax.ShapeDtypeStruct((half_rank, part_width + half_kv), f32),) * 2,
        in_specs=[SMEM] + [VMEM] * 19,
        out_specs=(VMEM, VMEM),
        compiler_params=PARAMS,
        name="image_gradients",
    )(
        where,
        kept,
        sent,
        *got,
        image,
        image_far,
        enc_low,
        enc_low_far,
        gain_part,
        a_part,
        *pieces,
        b_half,
        bias_half,
        line[:, None],
        position[:, None],
    )

    came = crossed(give)
    llm_mine, llm_came = mine[:, part_width:], came[:, part_width:]
    mine = jnp.concatenate(
        [
            mine[:, :part_width] + came[:, :part_width],
            jnp.where(first, llm_mine, llm_came) + text_grad[:, :half_kv],
            jnp.where(first, llm_came, llm_mine) + text_grad[:, half_kv:],
        ],
        axis=1,
    )
    mine = mine.reshape(n_dp, half_rank // n_dp, -1)
    mine = jnp.sum(lax.all_to_all(mine, "dp", 0, 0, tiled=True), axis=0)
    whole = to_everyone(mine, "dp").reshape(half_rank, -1)
    return whole[:, :part_width], whole[:, part_width:]


def solution(mesh):
    return jax.shard_map(
        body,
        mesh=mesh,
        in_specs=(
            P(("dp", "mp"), None),
            P(None, "mp"),
            P("mp"),
            P(),
            P(None, "mp"),
            P(("dp", "mp"), None),
            P(),
            P(("dp", "mp"), None),
            P(),
            P(("dp", "mp"), None),
            P(),
            P(("dp", "mp"), None),
            P(),
            P(("dp", "mp")),
        ),
        out_specs=(P("grp", "mp"), P("grp", None)),
        check_vma=False,
    )
```

```python
import functools

import jax
import jax.numpy as jnp
from jax import lax
from jax.experimental import pallas as pl
from jax.experimental.pallas import tpu as pltpu
from jax.sharding import PartitionSpec as P

ENC_DEV = 256
epsilon = 1e-06
f32 = jnp.float32
bf16 = jnp.bfloat16


def dot(a, b):
    return jnp.dot(a, b, preferred_element_type=f32)


def dot_tn(a, b):
    return lax.dot_general(a, b, (((0,), (0,)), ((), ())), preferred_element_type=f32)


def dot_nt(a, b):
    return lax.dot_general(a, b, (((1,), (1,)), ((), ())), preferred_element_type=f32)


def split_two(a):
    high = lax.reduce_precision(a, 8, 7)
    return high.astype(bf16), (a - high).astype(bf16)


def split_three(a):
    high = lax.reduce_precision(a, 8, 7)
    return (high.astype(bf16), *split_two(a - high))


def turned(array, axis, step):
    count = lax.axis_size(axis)
    return lax.ppermute(array, axis, [(i, (i + step) % count) for i in range(count)])


def crossed(array):
    return lax.ppermute(array, "grp", [(0, 1), (1, 0)])


def along(array, z_step, x_step, side):
    pairs = [
        (z * side + x, (z + z_step) % side * side + (x + x_step) % side)
        for z in range(side)
        for x in range(side)
    ]
    return lax.ppermute(array, "dp", pairs)


def to_everyone(array, axes):
    count = lax.axis_size(axes)
    return lax.all_to_all(
        jnp.broadcast_to(array[None], (count, *array.shape)), axes, 0, 0, tiled=True
    )


def cut(array, start, size, axis=0):
    starts = [jnp.int32(0)] * array.ndim
    starts[axis] = start
    sizes = list(array.shape)
    sizes[axis] = size
    return lax.dynamic_slice(array, starts, sizes, allow_negative_indices=False)


VMEM = pl.BlockSpec(memory_space=pltpu.VMEM)
SMEM = pl.BlockSpec(memory_space=pltpu.SMEM)
PARAMS = pltpu.CompilerParams(vmem_limit_bytes=48 * 1024 * 1024)


def block_start(col, k, side, size):
    return pl.multiple_of(((col + side - k) & (side - 1)) * size, 128)


def partial_kernel(
    place,
    near,
    far,
    gain,
    a_part,
    w0,
    w1,
    w2,
    w3,
    line,
    position,
    own,
    to1,
    to2,
    to3,
    sums,
    *,
    block,
    half_kv,
    rank,
    chunk,
    step,
):
    rows = near.shape[0]
    pieces = (w0, w1, w2, w3)
    side = len(pieces)
    per = chunk // 2
    wide_rows, lengths = [], []
    for piece in pieces:
        for z in range(side):
            both = piece[block + z * chunk : block + (z + 1) * chunk, :].astype(f32)
            wide_rows.append(both[:per])
            lengths.append(both[per:, :128])
    table = jnp.concatenate(wide_rows).astype(bf16)
    lengths = jnp.concatenate(lengths).astype(bf16)
    lane = lax.broadcasted_iota(jnp.int32, (rows, rank), 1)
    for h, source in enumerate((near, far)):
        out = slice(h * rows, (h + 1) * rows)
        values = jnp.zeros((rows, half_kv), f32)
        low = jnp.zeros((rows, rank), f32)
        squares = jnp.zeros((rows, 1), f32)
        for k, piece in enumerate(pieces):
            here = pl.ds(block_start(place[0], k, side, block), block)
            wide = source[:, here].astype(f32)
            scaled = (wide * gain[:, here]).astype(bf16)
            squares = squares + jnp.sum(wide * wide, axis=1, keepdims=True)
            values = values + dot(scaled, piece[:block, :])
            low = low + dot_nt(scaled, a_part[:, here])
        entries = lax.broadcasted_iota(jnp.int32, (rows, table.shape[0]), 1)
        pick = (line[out, :] == entries).astype(bf16)
        length = dot(pick, lengths)[:, :1]
        high = squares.astype(bf16).astype(f32)
        middle = (squares - high).astype(bf16).astype(f32)
        last = squares - high - middle
        extra = jnp.zeros((rows, rank), f32)
        for i, number in enumerate((high, middle, last, length)):
            extra = jnp.where(lane == i, number, extra)
        sums[out, :half_kv] = values
        sums[out, half_kv : half_kv + 2 * rank] = jnp.concatenate([low, extra], axis=1)
        sums[out, half_kv + 2 * rank :] = dot(pick, table)
    lane = lax.broadcasted_iota(jnp.int32, (step, 2 * rank), 1)
    for k, target in enumerate((own, to1, to2, to3)):
        there = (place[1] + side - k) & (side - 1)
        for h in range(2):
            start = pl.multiple_of(h * rows + there * step, step)
            target[h * step : (h + 1) * step, :] = sums[pl.ds(start, step), :].astype(target.dtype)
            if k == 0:
                extra = sums[pl.ds(start, step), half_kv : half_kv + 2 * rank]
                extra = jnp.where(lane == rank + 4, position[pl.ds(start, step), :], extra)
                own[h * step : (h + 1) * step, half_kv : half_kv + 2 * rank] = extra


def row_kernel(own, got1, got2, got3, b_half, bias, packed, *, half_kv, rank, width):
    total = own[...]
    for got in (got1, got2, got3):
        total = total + got[...].astype(f32)
    raw_values = total[:, :half_kv]
    raw_low = total[:, half_kv : half_kv + rank]
    at = half_kv + rank
    squares = total[:, at : at + 1] + total[:, at + 1 : at + 2] + total[:, at + 2 : at + 3]
    length = total[:, at + 3 : at + 4]
    position = total[:, at + 4 : at + 5]
    weight = jnp.where(position < length, 1.0 / length, 0.0)
    inverse = lax.rsqrt(squares / width + epsilon)
    low = (raw_low * inverse).astype(bf16)
    values_out = raw_values * inverse + bias[...] + dot(low, b_half[...])
    dvalues = ((values_out - total[:, half_kv + 2 * rank :]) * weight).astype(bf16)
    dlow = dot_nt(dvalues, b_half[...]).astype(bf16)
    centre = (
        jnp.sum(dvalues.astype(f32) * raw_values, axis=1, keepdims=True)
        + jnp.sum(dlow.astype(f32) * raw_low, axis=1, keepdims=True)
    ) / width
    factor = inverse * inverse * inverse * centre
    lane = lax.broadcasted_iota(jnp.int32, (total.shape[0], rank), 1)
    extra = jnp.zeros((total.shape[0], rank), f32)
    for i, number in enumerate((inverse, factor)):
        for j in range(3):
            part = number.astype(bf16).astype(f32)
            extra = jnp.where(lane == 3 * i + j, part, extra)
            number = number - part
    packed[:, :half_kv] = dvalues
    packed[:, half_kv:] = jnp.concatenate([low.astype(f32), extra], axis=1).astype(bf16)


def image_kernel(
    place,
    packed,
    got1,
    got2,
    got3,
    near,
    far,
    low_near,
    low_far,
    gain,
    a_part,
    w0,
    w1,
    w2,
    w3,
    b_half,
    mine,
    give,
    rows,
    *,
    block,
    half_kv,
    rank,
    step,
):
    pieces = (w0, w1, w2, w3)
    side = len(pieces)
    count = near.shape[0]
    for k, source in enumerate((packed, got1, got2, got3)):
        there = (place[1] + side - k) & (side - 1)
        for h in range(2):
            start = pl.multiple_of(h * count + there * step, step)
            rows[pl.ds(start, step), :] = source[h * step : (h + 1) * step, :]
    dvalues = rows[:, :half_kv]
    extra = rows[:, half_kv:]
    low = extra[:, :rank]
    numbers = extra[:, rank:].astype(f32)
    inverse = numbers[:, 0:1] + numbers[:, 1:2] + numbers[:, 2:3]
    factor = numbers[:, 3:4] + numbers[:, 4:5] + numbers[:, 5:6]
    dlow = dot_nt(dvalues, b_half[...]).astype(bf16)
    half = rank // 2
    grad = dot_tn(low, dvalues)
    mine[:, side * block :] = grad[:half]
    give[:, side * block :] = grad[half:]
    enc_low = jnp.concatenate([low_near[...], low_far[...]])
    for k, piece in enumerate(pieces):
        here = pl.ds(block_start(place[0], k, side, block), block)
        dnormed = dot_nt(dvalues, piece[:block, :]) + dot(dlow, a_part[:, here])
        wide = jnp.concatenate([near[:, here], far[:, here]]).astype(f32)
        dimage = (inverse * (gain[:, here] * dnormed) - wide * factor).astype(bf16)
        grad = dot_tn(enc_low, dimage)
        mine[:, here] = grad[:half]
        give[:, here] = grad[half:]


def body(
    hidden,
    enc_weight,
    enc_bias,
    enc_frozen,
    enc_adapter,
    text_rows,
    norm_gain,
    value_weight,
    value_bias,
    llm_frozen,
    llm_adapter,
    targets,
    dest_owner,
    seq_length,
):
    n_dp = lax.axis_size("dp")
    n_mp = lax.axis_size("mp")
    side = n_mp
    owners = n_dp * n_mp
    grp = lax.axis_index("grp")
    dp = lax.axis_index("dp")
    mp = lax.axis_index("mp")
    first = grp == 0
    width = text_rows.shape[1]
    part_width = enc_weight.shape[1]
    rank = enc_frozen.shape[1]
    half_rank = rank // 2
    kv = value_weight.shape[1]
    half_kv = kv // 2
    shard = value_weight.shape[0]
    block = side * shard
    block_rows = hidden.shape[0]
    mine_rows = block_rows // 2
    capacity = 2 * ENC_DEV // owners
    chunk = 2 * capacity
    area = capacity * n_dp
    slab, col = dp // side, dp & (side - 1)
    wrap = side - 1

    swap = [
        ((z * side + x) * side + y, (y * side + x) * side + z)
        for z in range(side)
        for x in range(side)
        for y in range(side)
    ]
    w_half = cut(value_weight, grp * half_kv, half_kv, 1)
    w_moved = lax.ppermute(w_half, ("dp", "mp"), swap)

    hid = lax.all_gather(cut(hidden, grp * mine_rows, mine_rows), "mp", axis=0, tiled=True)

    own_length = seq_length[0]
    t_half = cut(targets[:area], grp * half_kv, half_kv, 1)
    t_half = t_half.reshape(capacity, n_dp, half_kv).transpose(1, 0, 2)
    t_half = jnp.concatenate([t_half, jnp.full_like(t_half, own_length.astype(bf16))], axis=1)
    t_half = t_half.reshape(side, side * chunk, half_kv)
    w_line, t_line = [w_moved], [cut(t_half, slab, 1)[0]]
    for k in range(1, side):
        t_given = cut(t_half, (slab + k) & wrap, 1)[0]
        came = along(jnp.concatenate([w_moved, t_given]), k, 0, side)
        w_line.append(came[:shard])
        t_line.append(came[shard:])
    w_line = w_line[::-1]
    w_line = cut(jnp.concatenate(w_line + w_line), ((2 * side - 1 - slab) & wrap) * shard, block)
    t_line = jnp.stack(t_line).reshape(side, side, chunk, half_kv)
    pieces = []
    for k in range(side):
        t_given = cut(t_line, (col + k) & wrap, 1, 1).reshape(side * chunk, half_kv)
        piece = jnp.concatenate([w_line, t_given])
        pieces.append(along(piece, 0, k, side) if k else piece)

    a_half, _ = lax.optimization_barrier((cut(llm_frozen.T, grp * half_rank, half_rank), w_moved))
    a_mine = to_everyone(a_half, ("dp", "mp")).transpose(1, 0, 2).reshape(half_rank, width)
    a_all = jnp.concatenate([a_mine, crossed(a_mine)])
    a_part = cut(a_all, mp * part_width, part_width, 1)
    b_all = jnp.where(first, llm_adapter, jnp.roll(llm_adapter, half_rank, axis=0))
    b_half = cut(b_all, grp * half_kv, half_kv, 1)
    bias_wide = value_bias.astype(f32)[None]
    bias_half = cut(bias_wide, grp * half_kv, half_kv, 1)

    destiny = dest_owner[:, 0]
    block_dest = cut(destiny, dp * ENC_DEV, ENC_DEV)
    local = jnp.arange(ENC_DEV, dtype=jnp.int32)
    from_mp = (local % (ENC_DEV // 2)) // mine_rows
    from_grp = (grp + local // (ENC_DEV // 2)) & 1
    place = from_mp * block_rows + from_grp * mine_rows + (local & (mine_rows - 1))
    own_dest = jnp.sum(jnp.where(place[:, None] == local[None, :], block_dest[None, :], 0), axis=1)
    earlier = (own_dest[:, None] == block_dest[None, :]) & (local[None, :] < place[:, None])
    slot = jnp.sum(earlier.astype(jnp.int32), axis=1)
    own_mp, own_col, own_slab = own_dest & wrap, (own_dest // side) & wrap, own_dest // (side * side)
    line = (((col - own_col) & wrap) * side + ((slab - own_slab) & wrap)) * capacity + slot
    line = jnp.where(own_mp == mp, line, -1)
    position = (slot * n_dp + dp).astype(f32)

    gain_wide = norm_gain.astype(f32)[None]
    text_count = text_rows.shape[0] // 2
    text_wide = cut(text_rows, grp * text_count, text_count).astype(f32)
    text_inverse = lax.rsqrt(jnp.mean(text_wide * text_wide, axis=1, keepdims=True) + epsilon)
    text_normed = (text_wide * text_inverse * gain_wide).astype(bf16)
    text_low = dot_nt(text_normed, a_all).astype(bf16)
    owner_index = dp * n_mp + mp
    counts = jnp.sum((destiny.reshape(n_dp, ENC_DEV) == owner_index).astype(jnp.int32), axis=1)
    row = grp * text_count + jnp.arange(text_count, dtype=jnp.int32)
    taken = (row < area) & (
        row // n_dp
        < jnp.sum(
            jnp.where(
                (row & (n_dp - 1))[:, None] == jnp.arange(n_dp, dtype=jnp.int32)[None, :],
                counts,
                0,
            ),
            axis=1,
        )
    )
    keep = (row < own_length) & ~taken
    text_kept = jnp.where(keep[:, None], text_low, jnp.zeros_like(text_low))
    text_weight = 1.0 / own_length.astype(f32)
    text_sum = dot_tn(text_kept, text_normed) * text_weight
    own_text_targets = cut(targets, grp * text_count, text_count).astype(f32)
    rest = bias_wide + dot(text_low, b_all) - own_text_targets
    rest_high, rest_low = split_two(rest)
    rest_sum = dot_tn(
        jnp.concatenate([text_kept, text_kept]), jnp.concatenate([rest_high, rest_low])
    )
    rest_sum = rest_sum * text_weight
    both_sums = jnp.concatenate([text_sum, rest_sum], axis=1)
    both_sums = both_sums[:half_rank] + crossed(both_sums[half_rank:])
    text_parts = both_sums[:, :width].reshape(half_rank, owners, shard).transpose(1, 0, 2)
    text_parts = lax.all_to_all(text_parts.astype(bf16), ("dp", "mp"), 0, 0, tiled=True)
    text_here = jnp.sum(text_parts.astype(f32), axis=0)
    here_high, here_low = split_two(text_here)
    text_grad = dot(jnp.concatenate([here_high, here_low]), value_weight)
    text_grad = text_grad[:half_rank] + text_grad[half_rank:] + both_sums[:, width:]
    text_grad = text_grad + (
        turned(text_grad, "mp", 1) + turned(text_grad, "mp", 2) + turned(text_grad, "mp", 3)
    )

    enc_low = dot(hid, enc_frozen).astype(bf16)
    merged = dot(hid, enc_weight) + enc_bias.astype(f32) + dot(enc_low, enc_adapter)
    image = merged.astype(bf16)
    image_far = crossed(image)
    enc_low = jnp.where(first, enc_low, jnp.roll(enc_low, half_rank, axis=1))
    enc_low_far = jnp.roll(crossed(enc_low), half_rank, axis=1)
    gain_part = cut(gain_wide, mp * part_width, part_width, 1)
    where = jnp.stack([col, mp]).astype(jnp.int32)
    sizes = dict(half_kv=half_kv, rank=rank)
    lanes = kv + 2 * rank
    tokens = 2 * mine_rows
    to_one = jax.ShapeDtypeStruct((tokens, lanes), bf16)
    own, *to = pl.pallas_call(
        functools.partial(partial_kernel, chunk=chunk, block=block, step=mine_rows, **sizes),
        out_shape=(jax.ShapeDtypeStruct((tokens, lanes), f32), to_one, to_one, to_one),
        in_specs=[SMEM] + [VMEM] * 10,
        out_specs=(VMEM,) * 4,
        scratch_shapes=[pltpu.VMEM((ENC_DEV, lanes), f32)],
        compiler_params=PARAMS,
        name="partial_products",
    )(where, image, image_far, gain_part, a_part, *pieces, line[:, None], position[:, None])
    got = [turned(to[k - 1], "mp", -k) for k in range(1, n_mp)]
    packed = pl.pallas_call(
        functools.partial(row_kernel, width=float(width), **sizes),
        out_shape=jax.ShapeDtypeStruct((tokens, half_kv + 2 * rank), bf16),
        in_specs=[VMEM] * 6,
        out_specs=VMEM,
        compiler_params=PARAMS,
        name="row_work",
    )(own, *got, b_half, bias_half)
    got = [turned(packed, "mp", k) for k in range(1, n_mp)]
    mine, give = pl.pallas_call(
        functools.partial(image_kernel, block=block, step=mine_rows, **sizes),
        out_shape=(jax.ShapeDtypeStruct((half_rank, part_width + half_kv), f32),) * 2,
        in_specs=[SMEM] + [VMEM] * 15,
        out_specs=(VMEM, VMEM),
        scratch_shapes=[pltpu.VMEM((ENC_DEV, half_kv + 2 * rank), bf16)],
        compiler_params=PARAMS,
        name="image_gradients",
    )(
        where,
        packed,
        *got,
        image,
        image_far,
        enc_low,
        enc_low_far,
        gain_part,
        a_part,
        *pieces,
        b_half,
    )

    came = crossed(give)
    llm_mine, llm_came = mine[:, part_width:], came[:, part_width:]
    mine = jnp.concatenate(
        [
            mine[:, :part_width] + came[:, :part_width],
            jnp.where(first, llm_mine, llm_came) + text_grad[:, :half_kv],
            jnp.where(first, llm_came, llm_mine) + text_grad[:, half_kv:],
        ],
        axis=1,
    )
    mine = mine.reshape(n_dp, half_rank // n_dp, -1)
    mine = jnp.sum(lax.all_to_all(mine, "dp", 0, 0, tiled=True), axis=0)
    whole = to_everyone(mine, "dp").reshape(half_rank, -1)
    return whole[:, :part_width], whole[:, part_width:]


def solution(mesh):
    return jax.shard_map(
        body,
        mesh=mesh,
        in_specs=(
            P(("dp", "mp"), None),
            P(None, "mp"),
            P("mp"),
            P(),
            P(None, "mp"),
            P(("dp", "mp"), None),
            P(),
            P(("dp", "mp"), None),
            P(),
            P(("dp", "mp"), None),
            P(),
            P(("dp", "mp"), None),
            P(),
            P(("dp", "mp")),
        ),
        out_specs=(P("grp", "mp"), P("grp", None)),
        check_vma=False,
    )
```

```python
import functools

import jax
import jax.numpy as jnp
from jax import lax
from jax.experimental import pallas as pl
from jax.experimental.pallas import tpu as pltpu
from jax.sharding import PartitionSpec as P

ENC_DEV = 256
epsilon = 1e-06
f32 = jnp.float32
bf16 = jnp.bfloat16


def dot(a, b):
    return jnp.dot(a, b, preferred_element_type=f32)


def dot_tn(a, b):
    return lax.dot_general(a, b, (((0,), (0,)), ((), ())), preferred_element_type=f32)


def dot_nt(a, b):
    return lax.dot_general(a, b, (((1,), (1,)), ((), ())), preferred_element_type=f32)


def split_two(a):
    high = lax.reduce_precision(a, 8, 7)
    return high.astype(bf16), (a - high).astype(bf16)


def split_three(a):
    high = lax.reduce_precision(a, 8, 7)
    return (high.astype(bf16), *split_two(a - high))


def turned(array, axis, step):
    count = lax.axis_size(axis)
    return lax.ppermute(array, axis, [(i, (i + step) % count) for i in range(count)])


def crossed(array):
    return lax.ppermute(array, "grp", [(0, 1), (1, 0)])


def along(array, z_step, x_step, side):
    pairs = [
        (z * side + x, (z + z_step) % side * side + (x + x_step) % side)
        for z in range(side)
        for x in range(side)
    ]
    return lax.ppermute(array, "dp", pairs)


def to_everyone(array, axes):
    count = lax.axis_size(axes)
    return lax.all_to_all(
        jnp.broadcast_to(array[None], (count, *array.shape)), axes, 0, 0, tiled=True
    )


def cut(array, start, size, axis=0):
    starts = [jnp.int32(0)] * array.ndim
    starts[axis] = start
    sizes = list(array.shape)
    sizes[axis] = size
    return lax.dynamic_slice(array, starts, sizes, allow_negative_indices=False)


VMEM = pl.BlockSpec(memory_space=pltpu.VMEM)
SMEM = pl.BlockSpec(memory_space=pltpu.SMEM)
PARAMS = pltpu.CompilerParams(vmem_limit_bytes=48 * 1024 * 1024)


def block_start(col, k, side, size):
    return pl.multiple_of(((col + side - k) & (side - 1)) * size, 128)


def partial_kernel(
    place,
    near,
    far,
    gain,
    a_part,
    w0,
    w1,
    w2,
    w3,
    line,
    position,
    own,
    to1,
    to2,
    to3,
    sums,
    *,
    block,
    half_kv,
    rank,
    chunk,
    step,
):
    rows = near.shape[0]
    pieces = (w0, w1, w2, w3)
    side = len(pieces)
    per = chunk // 2
    wide_rows, lengths = [], []
    for piece in pieces:
        for z in range(side):
            both = piece[block + z * chunk : block + (z + 1) * chunk, :].astype(f32)
            wide_rows.append(both[:per])
            lengths.append(both[per:, :128])
    table = jnp.concatenate(wide_rows).astype(bf16)
    lengths = jnp.concatenate(lengths).astype(bf16)
    lane = lax.broadcasted_iota(jnp.int32, (rows, rank), 1)
    for h, source in enumerate((near, far)):
        out = slice(h * rows, (h + 1) * rows)
        values = jnp.zeros((rows, half_kv), f32)
        low = jnp.zeros((rows, rank), f32)
        squares = jnp.zeros((rows, 1), f32)
        for k, piece in enumerate(pieces):
            here = pl.ds(block_start(place[0], k, side, block), block)
            wide = source[:, here].astype(f32)
            scaled = (wide * gain[:, here]).astype(bf16)
            squares = squares + jnp.sum(wide * wide, axis=1, keepdims=True)
            values = values + dot(scaled, piece[:block, :])
            low = low + dot_nt(scaled, a_part[:, here])
        entries = lax.broadcasted_iota(jnp.int32, (rows, table.shape[0]), 1)
        pick = (line[out, :] == entries).astype(bf16)
        length = dot(pick, lengths)[:, :1]
        high = squares.astype(bf16).astype(f32)
        middle = (squares - high).astype(bf16).astype(f32)
        last = squares - high - middle
        extra = jnp.zeros((rows, rank), f32)
        for i, number in enumerate((high, middle, last, length)):
            extra = jnp.where(lane == i, number, extra)
        sums[out, :half_kv] = values
        sums[out, half_kv : half_kv + 2 * rank] = jnp.concatenate([low, extra], axis=1)
        sums[out, half_kv + 2 * rank :] = dot(pick, table)
    lane = lax.broadcasted_iota(jnp.int32, (step, 2 * rank), 1)
    for k, target in enumerate((own, to1, to2, to3)):
        for h in range(2):
            start = h * rows + k * step
            target[h * step : (h + 1) * step, :] = sums[pl.ds(start, step), :].astype(target.dtype)
            if k == 0:
                extra = sums[pl.ds(start, step), half_kv : half_kv + 2 * rank]
                extra = jnp.where(lane == rank + 4, position[pl.ds(start, step), :], extra)
                own[h * step : (h + 1) * step, half_kv : half_kv + 2 * rank] = extra


def row_kernel(own, got1, got2, got3, b_half, bias, packed, *, half_kv, rank, width):
    total = own[...]
    for got in (got1, got2, got3):
        total = total + got[...].astype(f32)
    raw_values = total[:, :half_kv]
    raw_low = total[:, half_kv : half_kv + rank]
    at = half_kv + rank
    squares = total[:, at : at + 1] + total[:, at + 1 : at + 2] + total[:, at + 2 : at + 3]
    length = total[:, at + 3 : at + 4]
    position = total[:, at + 4 : at + 5]
    weight = jnp.where(position < length, 1.0 / length, 0.0)
    inverse = lax.rsqrt(squares / width + epsilon)
    low = (raw_low * inverse).astype(bf16)
    values_out = raw_values * inverse + bias[...] + dot(low, b_half[...])
    dvalues = ((values_out - total[:, half_kv + 2 * rank :]) * weight).astype(bf16)
    dlow = dot_nt(dvalues, b_half[...]).astype(bf16)
    centre = (
        jnp.sum(dvalues.astype(f32) * raw_values, axis=1, keepdims=True)
        + jnp.sum(dlow.astype(f32) * raw_low, axis=1, keepdims=True)
    ) / width
    factor = inverse * inverse * inverse * centre
    lane = lax.broadcasted_iota(jnp.int32, (total.shape[0], rank), 1)
    extra = jnp.zeros((total.shape[0], rank), f32)
    for i, number in enumerate((inverse, factor)):
        for j in range(3):
            part = number.astype(bf16).astype(f32)
            extra = jnp.where(lane == 3 * i + j, part, extra)
            number = number - part
    packed[:, :half_kv] = dvalues
    packed[:, half_kv:] = jnp.concatenate([low.astype(f32), extra], axis=1).astype(bf16)


def image_kernel(
    place,
    packed,
    got1,
    got2,
    got3,
    near,
    far,
    low_near,
    low_far,
    gain,
    a_part,
    w0,
    w1,
    w2,
    w3,
    b_half,
    mine,
    give,
    rows,
    *,
    block,
    half_kv,
    rank,
    step,
):
    pieces = (w0, w1, w2, w3)
    side = len(pieces)
    count = near.shape[0]
    for k, source in enumerate((packed, got1, got2, got3)):
        for h in range(2):
            start = h * count + k * step
            rows[pl.ds(start, step), :] = source[h * step : (h + 1) * step, :]
    dvalues = rows[:, :half_kv]
    extra = rows[:, half_kv:]
    low = extra[:, :rank]
    numbers = extra[:, rank:].astype(f32)
    inverse = numbers[:, 0:1] + numbers[:, 1:2] + numbers[:, 2:3]
    factor = numbers[:, 3:4] + numbers[:, 4:5] + numbers[:, 5:6]
    dlow = dot_nt(dvalues, b_half[...]).astype(bf16)
    half = rank // 2
    grad = dot_tn(low, dvalues)
    mine[:, side * block :] = grad[:half]
    give[:, side * block :] = grad[half:]
    enc_low = jnp.concatenate([low_near[...], low_far[...]])
    for k, piece in enumerate(pieces):
        here = pl.ds(block_start(place[0], k, side, block), block)
        dnormed = dot_nt(dvalues, piece[:block, :]) + dot(dlow, a_part[:, here])
        wide = jnp.concatenate([near[:, here], far[:, here]]).astype(f32)
        dimage = (inverse * (gain[:, here] * dnormed) - wide * factor).astype(bf16)
        grad = dot_tn(enc_low, dimage)
        mine[:, here] = grad[:half]
        give[:, here] = grad[half:]


def body(
    hidden,
    enc_weight,
    enc_bias,
    enc_frozen,
    enc_adapter,
    text_rows,
    norm_gain,
    value_weight,
    value_bias,
    llm_frozen,
    llm_adapter,
    targets,
    dest_owner,
    seq_length,
):
    n_dp = lax.axis_size("dp")
    n_mp = lax.axis_size("mp")
    side = n_mp
    owners = n_dp * n_mp
    grp = lax.axis_index("grp")
    dp = lax.axis_index("dp")
    mp = lax.axis_index("mp")
    first = grp == 0
    width = text_rows.shape[1]
    part_width = enc_weight.shape[1]
    rank = enc_frozen.shape[1]
    half_rank = rank // 2
    kv = value_weight.shape[1]
    half_kv = kv // 2
    shard = value_weight.shape[0]
    block = side * shard
    block_rows = hidden.shape[0]
    mine_rows = block_rows // 2
    capacity = 2 * ENC_DEV // owners
    chunk = 2 * capacity
    area = capacity * n_dp
    slab, col = dp // side, dp & (side - 1)
    wrap = side - 1

    swap = [
        ((z * side + x) * side + y, (y * side + x) * side + z)
        for z in range(side)
        for x in range(side)
        for y in range(side)
    ]
    w_half = cut(value_weight, grp * half_kv, half_kv, 1)
    w_moved = lax.ppermute(w_half, ("dp", "mp"), swap)

    own_length = seq_length[0]
    t_half = cut(targets[:area], grp * half_kv, half_kv, 1)
    t_half = t_half.reshape(capacity, n_dp, half_kv).transpose(1, 0, 2)
    t_half = jnp.concatenate([t_half, jnp.full_like(t_half, own_length.astype(bf16))], axis=1)
    t_half = t_half.reshape(side, side * chunk, half_kv)
    w_line, t_line = [w_moved], [cut(t_half, slab, 1)[0]]
    for k in range(1, side):
        t_given = cut(t_half, (slab + k) & wrap, 1)[0]
        came = along(jnp.concatenate([w_moved, t_given]), k, 0, side)
        w_line.append(came[:shard])
        t_line.append(came[shard:])
    dest_owner, text_rows, hidden, _ = lax.optimization_barrier((dest_owner, text_rows, hidden, came))
    w_line = w_line[::-1]
    w_line = cut(jnp.concatenate(w_line + w_line), ((2 * side - 1 - slab) & wrap) * shard, block)
    t_line = jnp.stack(t_line).reshape(side, side, chunk, half_kv)
    pieces = []
    for k in range(side):
        t_given = cut(t_line, (col + k) & wrap, 1, 1).reshape(side * chunk, half_kv)
        piece = jnp.concatenate([w_line, t_given])
        pieces.append(along(piece, 0, k, side) if k else piece)

    own_hidden = cut(hidden, grp * mine_rows, mine_rows)
    hid_next, hid_last = turned(own_hidden, "mp", 1), turned(own_hidden, "mp", -1)
    hid = jnp.concatenate([own_hidden, hid_next, turned(hid_next, "mp", 1), hid_last])

    text_count = text_rows.shape[0] // 2
    text_wide = cut(text_rows, grp * text_count, text_count).astype(f32)
    text_inverse = lax.rsqrt(jnp.mean(text_wide * text_wide, axis=1, keepdims=True) + epsilon)

    a_half = cut(llm_frozen.T, grp * half_rank, half_rank)
    a_mine = to_everyone(a_half, ("dp", "mp")).transpose(1, 0, 2).reshape(half_rank, width)
    a_all = jnp.concatenate([a_mine, crossed(a_mine)])
    a_part = cut(a_all, mp * part_width, part_width, 1)
    b_all = jnp.where(first, llm_adapter, jnp.roll(llm_adapter, half_rank, axis=0))
    b_half = cut(b_all, grp * half_kv, half_kv, 1)
    bias_wide = value_bias.astype(f32)[None]
    bias_half = cut(bias_wide, grp * half_kv, half_kv, 1)

    destiny = dest_owner[:, 0]
    block_dest = cut(destiny, dp * ENC_DEV, ENC_DEV)
    local = jnp.arange(ENC_DEV, dtype=jnp.int32)
    from_mp = (mp - (local % (ENC_DEV // 2)) // mine_rows) & wrap
    from_grp = (grp + local // (ENC_DEV // 2)) & 1
    place = from_mp * block_rows + from_grp * mine_rows + (local & (mine_rows - 1))
    own_dest = jnp.sum(jnp.where(place[:, None] == local[None, :], block_dest[None, :], 0), axis=1)
    earlier = (own_dest[:, None] == block_dest[None, :]) & (local[None, :] < place[:, None])
    slot = jnp.sum(earlier.astype(jnp.int32), axis=1)
    own_mp, own_col, own_slab = own_dest & wrap, (own_dest // side) & wrap, own_dest // (side * side)
    line = (((col - own_col) & wrap) * side + ((slab - own_slab) & wrap)) * capacity + slot
    line = jnp.where(own_mp == mp, line, -1)
    position = (slot * n_dp + dp).astype(f32)

    enc_low = dot(hid, enc_frozen).astype(bf16)
    merged = dot(hid, enc_weight) + enc_bias.astype(f32) + dot(enc_low, enc_adapter)
    image = merged.astype(bf16)
    gain_wide = norm_gain.astype(f32)[None]
    text_normed = (text_wide * text_inverse * gain_wide).astype(bf16)
    a_text = a_all
    text_low = dot_nt(text_normed, a_text).astype(bf16)
    owner_index = dp * n_mp + mp
    counts = jnp.sum((destiny.reshape(n_dp, ENC_DEV) == owner_index).astype(jnp.int32), axis=1)
    row = grp * text_count + jnp.arange(text_count, dtype=jnp.int32)
    taken = (row < area) & (
        row // n_dp
        < jnp.sum(
            jnp.where(
                (row & (n_dp - 1))[:, None] == jnp.arange(n_dp, dtype=jnp.int32)[None, :],
                counts,
                0,
            ),
            axis=1,
        )
    )
    keep = (row < own_length) & ~taken
    text_kept = jnp.where(keep[:, None], text_low, jnp.zeros_like(text_low))
    text_weight = 1.0 / own_length.astype(f32)
    text_sum = dot_tn(text_kept, text_normed) * text_weight
    own_text_targets = cut(targets, grp * text_count, text_count).astype(f32)
    rest = bias_wide + dot(text_low, b_all) - own_text_targets
    rest_high, rest_low = split_two(rest)
    rest_sum = dot_tn(
        jnp.concatenate([text_kept, text_kept]), jnp.concatenate([rest_high, rest_low])
    )
    rest_sum = rest_sum * text_weight
    both_sums = jnp.concatenate([text_sum, rest_sum], axis=1)
    both_sums = both_sums[:half_rank] + crossed(both_sums[half_rank:])
    image_far = crossed(image)
    enc_low = jnp.where(first, enc_low, jnp.roll(enc_low, half_rank, axis=1))
    enc_low_far = jnp.roll(crossed(enc_low), half_rank, axis=1)
    gain_part = cut(gain_wide, mp * part_width, part_width, 1)
    where = col[None].astype(jnp.int32)
    sizes = dict(half_kv=half_kv, rank=rank)
    lanes = kv + 2 * rank
    tokens = 2 * mine_rows
    to_one = jax.ShapeDtypeStruct((tokens, lanes), bf16)
    own, *to = pl.pallas_call(
        functools.partial(partial_kernel, chunk=chunk, block=block, step=mine_rows, **sizes),
        out_shape=(jax.ShapeDtypeStruct((tokens, lanes), f32), to_one, to_one, to_one),
        in_specs=[SMEM] + [VMEM] * 10,
        out_specs=(VMEM,) * 4,
        scratch_shapes=[pltpu.VMEM((ENC_DEV, lanes), f32)],
        compiler_params=PARAMS,
        name="partial_products",
    )(where, image, image_far, gain_part, a_part, *pieces, line[:, None], position[:, None])
    got = [turned(to[k - 1], "mp", -k) for k in range(1, n_mp)]
    packed = pl.pallas_call(
        functools.partial(row_kernel, width=float(width), **sizes),
        out_shape=jax.ShapeDtypeStruct((tokens, half_kv + 2 * rank), bf16),
        in_specs=[VMEM] * 6,
        out_specs=VMEM,
        compiler_params=PARAMS,
        name="row_work",
    )(own, *got, b_half, bias_half)
    text_parts = both_sums[:, :width].reshape(half_rank, owners, shard).transpose(1, 0, 2)
    text_parts = lax.all_to_all(text_parts.astype(bf16), ("dp", "mp"), 0, 0, tiled=True)
    got = [turned(packed, "mp", k) for k in range(1, n_mp)]
    enc_low_far, text_parts = lax.optimization_barrier((enc_low_far, text_parts))
    mine, give = pl.pallas_call(
        functools.partial(image_kernel, block=block, step=mine_rows, **sizes),
        out_shape=(jax.ShapeDtypeStruct((half_rank, part_width + half_kv), f32),) * 2,
        in_specs=[SMEM] + [VMEM] * 15,
        out_specs=(VMEM, VMEM),
        scratch_shapes=[pltpu.VMEM((ENC_DEV, half_kv + 2 * rank), bf16)],
        compiler_params=PARAMS,
        name="image_gradients",
    )(
        where,
        packed,
        *got,
        image,
        image_far,
        enc_low,
        enc_low_far,
        gain_part,
        a_part,
        *pieces,
        b_half,
    )

    text_here = jnp.sum(text_parts.astype(f32), axis=0)
    here_high, here_low = split_two(text_here)
    text_grad = dot(jnp.concatenate([here_high, here_low]), value_weight)
    text_grad = text_grad[:half_rank] + text_grad[half_rank:] + both_sums[:, width:]
    text_grad = text_grad + (
        turned(text_grad, "mp", 1) + turned(text_grad, "mp", 2) + turned(text_grad, "mp", 3)
    )

    came = crossed(give)
    llm_mine, llm_came = mine[:, part_width:], came[:, part_width:]
    enc = (mine[:, :part_width] + came[:, :part_width]).reshape(side, 8, side, -1)
    llm = (
        jnp.concatenate(
            [jnp.where(first, llm_mine, llm_came), jnp.where(first, llm_came, llm_mine)], axis=1
        )
        + text_grad
    ).reshape(side, 8, side, -1)
    mine = jnp.concatenate([enc, llm], axis=3).transpose(0, 2, 1, 3).reshape(n_dp, 8, -1)
    mine = jnp.sum(lax.all_to_all(mine, "dp", 0, 0, tiled=True), axis=0)
    whole = to_everyone(mine, "dp").reshape(side, side, 8, -1).transpose(0, 2, 1, 3)
    at = part_width // side
    return whole[..., :at].reshape(half_rank, -1), whole[..., at:].reshape(half_rank, -1)


def solution(mesh):
    return jax.shard_map(
        body,
        mesh=mesh,
        in_specs=(
            P(("dp", "mp"), None),
            P(None, "mp"),
            P("mp"),
            P(),
            P(None, "mp"),
            P(("dp", "mp"), None),
            P(),
            P(("dp", "mp"), None),
            P(),
            P(("dp", "mp"), None),
            P(),
            P(("dp", "mp"), None),
            P(),
            P(("dp", "mp")),
        ),
        out_specs=(P("grp", "mp"), P("grp", None)),
        check_vma=False,
    )
```

```python
import functools

import jax
import jax.numpy as jnp
from jax import lax
from jax.experimental import pallas as pl
from jax.experimental.pallas import tpu as pltpu
from jax.sharding import PartitionSpec as P

ENC_DEV = 256
epsilon = 1e-06
f32 = jnp.float32
bf16 = jnp.bfloat16


def dot(a, b):
    return jnp.dot(a, b, preferred_element_type=f32)


def dot_tn(a, b):
    return lax.dot_general(a, b, (((0,), (0,)), ((), ())), preferred_element_type=f32)


def dot_nt(a, b):
    return lax.dot_general(a, b, (((1,), (1,)), ((), ())), preferred_element_type=f32)


def split_two(a):
    high = lax.reduce_precision(a, 8, 7)
    return high.astype(bf16), (a - high).astype(bf16)


def split_three(a):
    high = lax.reduce_precision(a, 8, 7)
    return (high.astype(bf16), *split_two(a - high))


def turned(array, axis, step):
    count = lax.axis_size(axis)
    return lax.ppermute(array, axis, [(i, (i + step) % count) for i in range(count)])


def crossed(array):
    return lax.ppermute(array, "grp", [(0, 1), (1, 0)])


def along(array, z_step, x_step, side):
    pairs = [
        (z * side + x, (z + z_step) % side * side + (x + x_step) % side)
        for z in range(side)
        for x in range(side)
    ]
    return lax.ppermute(array, "dp", pairs)


def to_everyone(array, axes):
    count = lax.axis_size(axes)
    return lax.all_to_all(
        jnp.broadcast_to(array[None], (count, *array.shape)), axes, 0, 0, tiled=True
    )


def cut(array, start, size, axis=0):
    starts = [jnp.int32(0)] * array.ndim
    starts[axis] = start
    sizes = list(array.shape)
    sizes[axis] = size
    return lax.dynamic_slice(array, starts, sizes, allow_negative_indices=False)


VMEM = pl.BlockSpec(memory_space=pltpu.VMEM)
SMEM = pl.BlockSpec(memory_space=pltpu.SMEM)
PARAMS = pltpu.CompilerParams(vmem_limit_bytes=48 * 1024 * 1024)


def block_start(col, k, side, size):
    return pl.multiple_of(((col + side - k) & (side - 1)) * size, 128)


def partial_kernel(
    place,
    near,
    far,
    gain,
    a_part,
    w0,
    w1,
    w2,
    w3,
    line,
    position,
    own,
    to1,
    to2,
    to3,
    sums,
    *,
    block,
    half_kv,
    rank,
    chunk,
    step,
):
    rows = near.shape[0]
    pieces = (w0, w1, w2, w3)
    side = len(pieces)
    per = chunk // 2
    wide_rows, lengths = [], []
    for piece in pieces:
        for z in range(side):
            both = piece[block + z * chunk : block + (z + 1) * chunk, :].astype(f32)
            wide_rows.append(both[:per])
            lengths.append(both[per:, :128])
    table = jnp.concatenate(wide_rows).astype(bf16)
    lengths = jnp.concatenate(lengths).astype(bf16)
    lane = lax.broadcasted_iota(jnp.int32, (rows, rank), 1)
    for h, source in enumerate((near, far)):
        out = slice(h * rows, (h + 1) * rows)
        values = jnp.zeros((rows, half_kv), f32)
        low = jnp.zeros((rows, rank), f32)
        squares = jnp.zeros((rows, 1), f32)
        for k, piece in enumerate(pieces):
            here = pl.ds(block_start(place[0], k, side, block), block)
            wide = source[:, here].astype(f32)
            scaled = (wide * gain[:, here]).astype(bf16)
            squares = squares + jnp.sum(wide * wide, axis=1, keepdims=True)
            values = values + dot(scaled, piece[:block, :])
            low = low + dot_nt(scaled, a_part[:, here])
        entries = lax.broadcasted_iota(jnp.int32, (rows, table.shape[0]), 1)
        pick = (line[out, :] == entries).astype(bf16)
        length = dot(pick, lengths)[:, :1]
        high = squares.astype(bf16).astype(f32)
        middle = (squares - high).astype(bf16).astype(f32)
        last = squares - high - middle
        extra = jnp.zeros((rows, rank), f32)
        for i, number in enumerate((high, middle, last, length)):
            extra = jnp.where(lane == i, number, extra)
        sums[out, :half_kv] = values
        sums[out, half_kv : half_kv + 2 * rank] = jnp.concatenate([low, extra], axis=1)
        sums[out, half_kv + 2 * rank :] = dot(pick, table)
    lane = lax.broadcasted_iota(jnp.int32, (step, 2 * rank), 1)
    for k, target in enumerate((own, to1, to2, to3)):
        for h in range(2):
            start = h * rows + k * step
            target[h * step : (h + 1) * step, :] = sums[pl.ds(start, step), :].astype(target.dtype)
            if k == 0:
                extra = sums[pl.ds(start, step), half_kv : half_kv + 2 * rank]
                extra = jnp.where(lane == rank + 4, position[pl.ds(start, step), :], extra)
                own[h * step : (h + 1) * step, half_kv : half_kv + 2 * rank] = extra


def row_kernel(own, got1, got2, got3, b_half, bias, packed, *, half_kv, rank, width):
    total = own[...]
    for got in (got1, got2, got3):
        total = total + got[...].astype(f32)
    raw_values = total[:, :half_kv]
    raw_low = total[:, half_kv : half_kv + rank]
    at = half_kv + rank
    squares = total[:, at : at + 1] + total[:, at + 1 : at + 2] + total[:, at + 2 : at + 3]
    length = total[:, at + 3 : at + 4]
    position = total[:, at + 4 : at + 5]
    weight = jnp.where(position < length, 1.0 / length, 0.0)
    inverse = lax.rsqrt(squares / width + epsilon)
    low = (raw_low * inverse).astype(bf16)
    values_out = raw_values * inverse + bias[...] + dot(low, b_half[...])
    dvalues = ((values_out - total[:, half_kv + 2 * rank :]) * weight).astype(bf16)
    dlow = dot_nt(dvalues, b_half[...]).astype(bf16)
    centre = (
        jnp.sum(dvalues.astype(f32) * raw_values, axis=1, keepdims=True)
        + jnp.sum(dlow.astype(f32) * raw_low, axis=1, keepdims=True)
    ) / width
    factor = inverse * inverse * inverse * centre
    lane = lax.broadcasted_iota(jnp.int32, (total.shape[0], rank), 1)
    extra = jnp.zeros((total.shape[0], rank), f32)
    for i, number in enumerate((inverse, factor)):
        for j in range(3):
            part = number.astype(bf16).astype(f32)
            extra = jnp.where(lane == 3 * i + j, part, extra)
            number = number - part
    packed[:, :half_kv] = dvalues
    packed[:, half_kv:] = jnp.concatenate([low.astype(f32), extra], axis=1).astype(bf16)


def image_kernel(
    place,
    packed,
    got1,
    got2,
    got3,
    near,
    far,
    low_near,
    low_far,
    gain,
    a_part,
    w0,
    w1,
    w2,
    w3,
    b_half,
    mine,
    give,
    rows,
    *,
    block,
    half_kv,
    rank,
    step,
):
    pieces = (w0, w1, w2, w3)
    side = len(pieces)
    count = near.shape[0]
    for k, source in enumerate((packed, got1, got2, got3)):
        for h in range(2):
            start = h * count + k * step
            rows[pl.ds(start, step), :] = source[h * step : (h + 1) * step, :]
    dvalues = rows[:, :half_kv]
    extra = rows[:, half_kv:]
    low = extra[:, :rank]
    numbers = extra[:, rank:].astype(f32)
    inverse = numbers[:, 0:1] + numbers[:, 1:2] + numbers[:, 2:3]
    factor = numbers[:, 3:4] + numbers[:, 4:5] + numbers[:, 5:6]
    dlow = dot_nt(dvalues, b_half[...]).astype(bf16)
    half = rank // 2
    grad = dot_tn(low, dvalues)
    mine[:, side * block :] = grad[:half]
    give[:, side * block :] = grad[half:]
    enc_low = jnp.concatenate([low_near[...], low_far[...]])
    for k, piece in enumerate(pieces):
        here = pl.ds(block_start(place[0], k, side, block), block)
        dnormed = dot_nt(dvalues, piece[:block, :]) + dot(dlow, a_part[:, here])
        wide = jnp.concatenate([near[:, here], far[:, here]]).astype(f32)
        dimage = (inverse * (gain[:, here] * dnormed) - wide * factor).astype(bf16)
        grad = dot_tn(enc_low, dimage)
        mine[:, here] = grad[:half]
        give[:, here] = grad[half:]


def body(
    hidden,
    enc_weight,
    enc_bias,
    enc_frozen,
    enc_adapter,
    text_rows,
    norm_gain,
    value_weight,
    value_bias,
    llm_frozen,
    llm_adapter,
    targets,
    dest_owner,
    seq_length,
):
    n_dp = lax.axis_size("dp")
    n_mp = lax.axis_size("mp")
    side = n_mp
    owners = n_dp * n_mp
    grp = lax.axis_index("grp")
    dp = lax.axis_index("dp")
    mp = lax.axis_index("mp")
    first = grp == 0
    width = text_rows.shape[1]
    part_width = enc_weight.shape[1]
    rank = enc_frozen.shape[1]
    half_rank = rank // 2
    kv = value_weight.shape[1]
    half_kv = kv // 2
    shard = value_weight.shape[0]
    block = side * shard
    block_rows = hidden.shape[0]
    mine_rows = block_rows // 2
    capacity = 2 * ENC_DEV // owners
    chunk = 2 * capacity
    area = capacity * n_dp
    slab, col = dp // side, dp & (side - 1)
    wrap = side - 1

    swap = [
        ((z * side + x) * side + y, (y * side + x) * side + z)
        for z in range(side)
        for x in range(side)
        for y in range(side)
    ]
    w_half = cut(value_weight, grp * half_kv, half_kv, 1)
    w_moved = lax.ppermute(w_half, ("dp", "mp"), swap)

    own_length = seq_length[0]
    t_half = cut(targets[:area], grp * half_kv, half_kv, 1)
    t_half = t_half.reshape(capacity, n_dp, half_kv).transpose(1, 0, 2)
    t_half = jnp.concatenate([t_half, jnp.full_like(t_half, own_length.astype(bf16))], axis=1)
    t_half = t_half.reshape(side, side * chunk, half_kv)
    w_line, t_line = [w_moved], [cut(t_half, slab, 1)[0]]
    for k in range(1, side):
        t_given = cut(t_half, (slab + k) & wrap, 1)[0]
        came = along(jnp.concatenate([w_moved, t_given]), k, 0, side)
        w_line.append(came[:shard])
        t_line.append(came[shard:])
    dest_owner, text_rows, _ = lax.optimization_barrier((dest_owner, text_rows, came))
    w_line = w_line[::-1]
    w_line = cut(jnp.concatenate(w_line + w_line), ((2 * side - 1 - slab) & wrap) * shard, block)
    t_line = jnp.stack(t_line).reshape(side, side, chunk, half_kv)
    pieces = []
    for k in range(side):
        t_given = cut(t_line, (col + k) & wrap, 1, 1).reshape(side * chunk, half_kv)
        piece = jnp.concatenate([w_line, t_given])
        pieces.append(along(piece, 0, k, side) if k else piece)

    own_hidden = cut(hidden, grp * mine_rows, mine_rows)
    hid_next, hid_last = turned(own_hidden, "mp", 1), turned(own_hidden, "mp", -1)
    hid = jnp.concatenate([own_hidden, hid_next, turned(hid_next, "mp", 1), hid_last])

    text_count = text_rows.shape[0] // 2
    text_wide = cut(text_rows, grp * text_count, text_count).astype(f32)
    text_inverse = lax.rsqrt(jnp.mean(text_wide * text_wide, axis=1, keepdims=True) + epsilon)

    a_half = cut(llm_frozen.T, grp * half_rank, half_rank)
    a_mine = to_everyone(a_half, ("dp", "mp")).transpose(1, 0, 2).reshape(half_rank, width)
    a_all = jnp.concatenate([a_mine, crossed(a_mine)])
    a_part = cut(a_all, mp * part_width, part_width, 1)
    b_all = jnp.where(first, llm_adapter, jnp.roll(llm_adapter, half_rank, axis=0))
    b_half = cut(b_all, grp * half_kv, half_kv, 1)
    bias_wide = value_bias.astype(f32)[None]
    bias_half = cut(bias_wide, grp * half_kv, half_kv, 1)

    destiny = dest_owner[:, 0]
    block_dest = cut(destiny, dp * ENC_DEV, ENC_DEV)
    local = jnp.arange(ENC_DEV, dtype=jnp.int32)
    from_mp = (mp - (local % (ENC_DEV // 2)) // mine_rows) & wrap
    from_grp = (grp + local // (ENC_DEV // 2)) & 1
    place = from_mp * block_rows + from_grp * mine_rows + (local & (mine_rows - 1))
    own_dest = jnp.sum(jnp.where(place[:, None] == local[None, :], block_dest[None, :], 0), axis=1)
    earlier = (own_dest[:, None] == block_dest[None, :]) & (local[None, :] < place[:, None])
    slot = jnp.sum(earlier.astype(jnp.int32), axis=1)
    own_mp, own_col, own_slab = own_dest & wrap, (own_dest // side) & wrap, own_dest // (side * side)
    line = (((col - own_col) & wrap) * side + ((slab - own_slab) & wrap)) * capacity + slot
    line = jnp.where(own_mp == mp, line, -1)
    position = (slot * n_dp + dp).astype(f32)

    enc_low = dot(hid, enc_frozen).astype(bf16)
    merged = dot(hid, enc_weight) + enc_bias.astype(f32) + dot(enc_low, enc_adapter)
    image = merged.astype(bf16)
    gain_wide = norm_gain.astype(f32)[None]
    text_normed = (text_wide * text_inverse * gain_wide).astype(bf16)
    a_text = a_all
    text_low = dot_nt(text_normed, a_text).astype(bf16)
    owner_index = dp * n_mp + mp
    counts = jnp.sum((destiny.reshape(n_dp, ENC_DEV) == owner_index).astype(jnp.int32), axis=1)
    row = grp * text_count + jnp.arange(text_count, dtype=jnp.int32)
    taken = (row < area) & (
        row // n_dp
        < jnp.sum(
            jnp.where(
                (row & (n_dp - 1))[:, None] == jnp.arange(n_dp, dtype=jnp.int32)[None, :],
                counts,
                0,
            ),
            axis=1,
        )
    )
    keep = (row < own_length) & ~taken
    text_kept = jnp.where(keep[:, None], text_low, jnp.zeros_like(text_low))
    text_weight = 1.0 / own_length.astype(f32)
    text_sum = dot_tn(text_kept, text_normed) * text_weight
    own_text_targets = cut(targets, grp * text_count, text_count).astype(f32)
    rest = bias_wide + dot(text_low, b_all) - own_text_targets
    rest_high, rest_low = split_two(rest)
    rest_sum = dot_tn(
        jnp.concatenate([text_kept, text_kept]), jnp.concatenate([rest_high, rest_low])
    )
    rest_sum = rest_sum * text_weight
    both_sums = jnp.concatenate([text_sum, rest_sum], axis=1)
    both_sums = both_sums[:half_rank] + crossed(both_sums[half_rank:])
    image_far = crossed(image)
    enc_low = jnp.where(first, enc_low, jnp.roll(enc_low, half_rank, axis=1))
    enc_low_far = jnp.roll(crossed(enc_low), half_rank, axis=1)
    gain_part = cut(gain_wide, mp * part_width, part_width, 1)
    where = col[None].astype(jnp.int32)
    sizes = dict(half_kv=half_kv, rank=rank)
    lanes = kv + 2 * rank
    tokens = 2 * mine_rows
    to_one = jax.ShapeDtypeStruct((tokens, lanes), bf16)
    own, *to = pl.pallas_call(
        functools.partial(partial_kernel, chunk=chunk, block=block, step=mine_rows, **sizes),
        out_shape=(jax.ShapeDtypeStruct((tokens, lanes), f32), to_one, to_one, to_one),
        in_specs=[SMEM] + [VMEM] * 10,
        out_specs=(VMEM,) * 4,
        scratch_shapes=[pltpu.VMEM((ENC_DEV, lanes), f32)],
        compiler_params=PARAMS,
        name="partial_products",
    )(where, image, image_far, gain_part, a_part, *pieces, line[:, None], position[:, None])
    got = [turned(to[k - 1], "mp", -k) for k in range(1, n_mp)]
    packed = pl.pallas_call(
        functools.partial(row_kernel, width=float(width), **sizes),
        out_shape=jax.ShapeDtypeStruct((tokens, half_kv + 2 * rank), bf16),
        in_specs=[VMEM] * 6,
        out_specs=VMEM,
        compiler_params=PARAMS,
        name="row_work",
    )(own, *got, b_half, bias_half)
    text_parts = both_sums[:, :width].reshape(half_rank, owners, shard).transpose(1, 0, 2)
    text_parts = lax.all_to_all(text_parts.astype(bf16), ("dp", "mp"), 0, 0, tiled=True)
    got = [turned(packed, "mp", k) for k in range(1, n_mp)]
    text_here = jnp.sum(text_parts.astype(f32), axis=0)
    here_high, here_low = split_two(text_here)
    text_grad = dot(jnp.concatenate([here_high, here_low]), value_weight)
    text_grad = text_grad[:half_rank] + text_grad[half_rank:] + both_sums[:, width:]
    text_grad = text_grad + (
        turned(text_grad, "mp", 1) + turned(text_grad, "mp", 2) + turned(text_grad, "mp", 3)
    )
    enc_low_far, text_grad = lax.optimization_barrier((enc_low_far, text_grad))
    mine, give = pl.pallas_call(
        functools.partial(image_kernel, block=block, step=mine_rows, **sizes),
        out_shape=(jax.ShapeDtypeStruct((half_rank, part_width + half_kv), f32),) * 2,
        in_specs=[SMEM] + [VMEM] * 15,
        out_specs=(VMEM, VMEM),
        scratch_shapes=[pltpu.VMEM((ENC_DEV, half_kv + 2 * rank), bf16)],
        compiler_params=PARAMS,
        name="image_gradients",
    )(
        where,
        packed,
        *got,
        image,
        image_far,
        enc_low,
        enc_low_far,
        gain_part,
        a_part,
        *pieces,
        b_half,
    )

    came = crossed(give)
    llm_mine, llm_came = mine[:, part_width:], came[:, part_width:]
    enc = (mine[:, :part_width] + came[:, :part_width]).reshape(side, 8, side, -1)
    llm = (
        jnp.concatenate(
            [jnp.where(first, llm_mine, llm_came), jnp.where(first, llm_came, llm_mine)], axis=1
        )
        + text_grad
    ).reshape(side, 8, side, -1)
    mine = jnp.concatenate([enc, llm], axis=3).transpose(0, 2, 1, 3).reshape(n_dp, 8, -1)
    mine = jnp.sum(lax.all_to_all(mine, "dp", 0, 0, tiled=True), axis=0)
    whole = to_everyone(mine, "dp").reshape(side, side, 8, -1).transpose(0, 2, 1, 3)
    at = part_width // side
    return whole[..., :at].reshape(half_rank, -1), whole[..., at:].reshape(half_rank, -1)


def solution(mesh):
    return jax.shard_map(
        body,
        mesh=mesh,
        in_specs=(
            P(("dp", "mp"), None),
            P(None, "mp"),
            P("mp"),
            P(),
            P(None, "mp"),
            P(("dp", "mp"), None),
            P(),
            P(("dp", "mp"), None),
            P(),
            P(("dp", "mp"), None),
            P(),
            P(("dp", "mp"), None),
            P(),
            P(("dp", "mp")),
        ),
        out_specs=(P("grp", "mp"), P("grp", None)),
        check_vma=False,
    )
```

```python
import functools

import jax
import jax.numpy as jnp
from jax import lax
from jax.experimental import pallas as pl
from jax.experimental.pallas import tpu as pltpu
from jax.sharding import PartitionSpec as P

ENC_DEV = 256
epsilon = 1e-06
f32 = jnp.float32
bf16 = jnp.bfloat16


def dot(a, b):
    return jnp.dot(a, b, preferred_element_type=f32)


def dot_tn(a, b):
    return lax.dot_general(a, b, (((0,), (0,)), ((), ())), preferred_element_type=f32)


def dot_nt(a, b):
    return lax.dot_general(a, b, (((1,), (1,)), ((), ())), preferred_element_type=f32)


def split_two(a):
    high = lax.reduce_precision(a, 8, 7)
    return high.astype(bf16), (a - high).astype(bf16)


def split_three(a):
    high = lax.reduce_precision(a, 8, 7)
    return (high.astype(bf16), *split_two(a - high))


def turned(array, axis, step):
    count = lax.axis_size(axis)
    return lax.ppermute(array, axis, [(i, (i + step) % count) for i in range(count)])


def crossed(array):
    return lax.ppermute(array, "grp", [(0, 1), (1, 0)])


def along(array, z_step, x_step, side):
    pairs = [
        (z * side + x, (z + z_step) % side * side + (x + x_step) % side)
        for z in range(side)
        for x in range(side)
    ]
    return lax.ppermute(array, "dp", pairs)


def to_everyone(array, axes):
    count = lax.axis_size(axes)
    return lax.all_to_all(
        jnp.broadcast_to(array[None], (count, *array.shape)), axes, 0, 0, tiled=True
    )


def cut(array, start, size, axis=0):
    starts = [jnp.int32(0)] * array.ndim
    starts[axis] = start
    sizes = list(array.shape)
    sizes[axis] = size
    return lax.dynamic_slice(array, starts, sizes, allow_negative_indices=False)


VMEM = pl.BlockSpec(memory_space=pltpu.VMEM)
SMEM = pl.BlockSpec(memory_space=pltpu.SMEM)
PARAMS = pltpu.CompilerParams(vmem_limit_bytes=48 * 1024 * 1024)


def block_start(col, k, side, size):
    return pl.multiple_of(((col + side - k) & (side - 1)) * size, 128)


def partial_kernel(
    place,
    near,
    far,
    gain,
    a_part,
    w0,
    w1,
    w2,
    w3,
    line,
    position,
    own,
    to1,
    to2,
    to3,
    sums,
    *,
    block,
    half_kv,
    rank,
    chunk,
    step,
):
    rows = near.shape[0]
    pieces = (w0, w1, w2, w3)
    side = len(pieces)
    per = chunk // 2
    wide_rows, lengths = [], []
    for piece in pieces:
        for z in range(side):
            both = piece[block + z * chunk : block + (z + 1) * chunk, :].astype(f32)
            wide_rows.append(both[:per])
            lengths.append(both[per:, :128])
    table = jnp.concatenate(wide_rows).astype(bf16)
    lengths = jnp.concatenate(lengths).astype(bf16)
    lane = lax.broadcasted_iota(jnp.int32, (rows, rank), 1)
    for h, source in enumerate((near, far)):
        out = slice(h * rows, (h + 1) * rows)
        values = jnp.zeros((rows, half_kv), f32)
        low = jnp.zeros((rows, rank), f32)
        squares = jnp.zeros((rows, 1), f32)
        for k, piece in enumerate(pieces):
            here = pl.ds(block_start(place[0], k, side, block), block)
            wide = source[:, here].astype(f32)
            scaled = (wide * gain[:, here]).astype(bf16)
            squares = squares + jnp.sum(wide * wide, axis=1, keepdims=True)
            values = values + dot(scaled, piece[:block, :])
            low = low + dot_nt(scaled, a_part[:, here])
        entries = lax.broadcasted_iota(jnp.int32, (rows, table.shape[0]), 1)
        pick = (line[out, :] == entries).astype(bf16)
        length = dot(pick, lengths)[:, :1]
        high = squares.astype(bf16).astype(f32)
        middle = (squares - high).astype(bf16).astype(f32)
        last = squares - high - middle
        extra = jnp.zeros((rows, rank), f32)
        for i, number in enumerate((high, middle, last, length)):
            extra = jnp.where(lane == i, number, extra)
        sums[out, :half_kv] = values
        sums[out, half_kv : half_kv + 2 * rank] = jnp.concatenate([low, extra], axis=1)
        sums[out, half_kv + 2 * rank :] = dot(pick, table)
    lane = lax.broadcasted_iota(jnp.int32, (step, 2 * rank), 1)
    for k, target in enumerate((own, to1, to2, to3)):
        for h in range(2):
            start = h * rows + k * step
            target[h * step : (h + 1) * step, :] = sums[pl.ds(start, step), :].astype(target.dtype)
            if k == 0:
                extra = sums[pl.ds(start, step), half_kv : half_kv + 2 * rank]
                extra = jnp.where(lane == rank + 4, position[pl.ds(start, step), :], extra)
                own[h * step : (h + 1) * step, half_kv : half_kv + 2 * rank] = extra


def row_kernel(own, got1, got2, got3, b_half, bias, packed, *, half_kv, rank, width):
    total = own[...]
    for got in (got1, got2, got3):
        total = total + got[...].astype(f32)
    raw_values = total[:, :half_kv]
    raw_low = total[:, half_kv : half_kv + rank]
    at = half_kv + rank
    squares = total[:, at : at + 1] + total[:, at + 1 : at + 2] + total[:, at + 2 : at + 3]
    length = total[:, at + 3 : at + 4]
    position = total[:, at + 4 : at + 5]
    weight = jnp.where(position < length, 1.0 / length, 0.0)
    inverse = lax.rsqrt(squares / width + epsilon)
    low = (raw_low * inverse).astype(bf16)
    values_out = raw_values * inverse + bias[...] + dot(low, b_half[...])
    dvalues = ((values_out - total[:, half_kv + 2 * rank :]) * weight).astype(bf16)
    dlow = dot_nt(dvalues, b_half[...]).astype(bf16)
    centre = (
        jnp.sum(dvalues.astype(f32) * raw_values, axis=1, keepdims=True)
        + jnp.sum(dlow.astype(f32) * raw_low, axis=1, keepdims=True)
    ) / width
    factor = inverse * inverse * inverse * centre
    lane = lax.broadcasted_iota(jnp.int32, (total.shape[0], rank), 1)
    extra = jnp.zeros((total.shape[0], rank), f32)
    for i, number in enumerate((inverse, factor)):
        for j in range(3):
            part = number.astype(bf16).astype(f32)
            extra = jnp.where(lane == 3 * i + j, part, extra)
            number = number - part
    packed[:, :half_kv] = dvalues
    packed[:, half_kv:] = jnp.concatenate([low.astype(f32), extra], axis=1).astype(bf16)


def image_kernel(
    place,
    packed,
    got1,
    got2,
    got3,
    near,
    far,
    low_near,
    low_far,
    gain,
    a_part,
    w0,
    w1,
    w2,
    w3,
    b_half,
    mine,
    give,
    rows,
    ranks,
    *,
    block,
    half_kv,
    rank,
    step,
):
    pieces = (w0, w1, w2, w3)
    side = len(pieces)
    count = near.shape[0]
    for k, source in enumerate((packed, got1, got2, got3)):
        for h in range(2):
            start = h * count + k * step
            rows[pl.ds(start, step), :] = source[h * step : (h + 1) * step, :]
    dvalues = rows[:, :half_kv]
    extra = rows[:, half_kv:]
    low = extra[:, :rank]
    numbers = extra[:, rank:].astype(f32)
    inverse = numbers[:, 0:1] + numbers[:, 1:2] + numbers[:, 2:3]
    factor = numbers[:, 3:4] + numbers[:, 4:5] + numbers[:, 5:6]
    dlow = dot_nt(dvalues, b_half[...]).astype(bf16)
    half = rank // 2
    grad = dot_tn(low, dvalues)
    mine[:, side * block :] = grad[:half]
    give[:, side * block :] = grad[half:]
    enc_low = jnp.concatenate([low_near[...], low_far[...]])
    for k, piece in enumerate(pieces):
        here = pl.ds(block_start(place[0], k, side, block), block)
        dnormed = dot_nt(dvalues, piece[:block, :]) + dot(dlow, a_part[:, here])
        wide = jnp.concatenate([near[:, here], far[:, here]]).astype(f32)
        dimage = (inverse * (gain[:, here] * dnormed) - wide * factor).astype(bf16)
        ranks[...] = dot_tn(enc_low, dimage)
        mine[:, here] = ranks[pl.ds(pl.multiple_of(place[1] * half, half), half), :]
        give[:, here] = ranks[pl.ds(pl.multiple_of((1 - place[1]) * half, half), half), :]


def body(
    hidden,
    enc_weight,
    enc_bias,
    enc_frozen,
    enc_adapter,
    text_rows,
    norm_gain,
    value_weight,
    value_bias,
    llm_frozen,
    llm_adapter,
    targets,
    dest_owner,
    seq_length,
):
    n_dp = lax.axis_size("dp")
    n_mp = lax.axis_size("mp")
    side = n_mp
    owners = n_dp * n_mp
    grp = lax.axis_index("grp")
    dp = lax.axis_index("dp")
    mp = lax.axis_index("mp")
    first = grp == 0
    width = text_rows.shape[1]
    part_width = enc_weight.shape[1]
    rank = enc_frozen.shape[1]
    half_rank = rank // 2
    kv = value_weight.shape[1]
    half_kv = kv // 2
    shard = value_weight.shape[0]
    block = side * shard
    block_rows = hidden.shape[0]
    mine_rows = block_rows // 2
    capacity = 2 * ENC_DEV // owners
    chunk = 2 * capacity
    area = capacity * n_dp
    slab, col = dp // side, dp & (side - 1)
    wrap = side - 1

    swap = [
        ((z * side + x) * side + y, (y * side + x) * side + z)
        for z in range(side)
        for x in range(side)
        for y in range(side)
    ]
    w_half = cut(value_weight, grp * half_kv, half_kv, 1)
    w_moved = lax.ppermute(w_half, ("dp", "mp"), swap)

    own_length = seq_length[0]
    t_half = cut(targets[:area], grp * half_kv, half_kv, 1)
    t_half = t_half.reshape(capacity, n_dp, half_kv).transpose(1, 0, 2)
    t_half = jnp.concatenate([t_half, jnp.full_like(t_half, own_length.astype(bf16))], axis=1)
    t_half = t_half.reshape(side, side * chunk, half_kv)
    w_line, t_line = [w_moved], [cut(t_half, slab, 1)[0]]
    for k in range(1, side):
        t_given = cut(t_half, (slab + k) & wrap, 1)[0]
        came = along(jnp.concatenate([w_moved, t_given]), k, 0, side)
        w_line.append(came[:shard])
        t_line.append(came[shard:])
    dest_owner, text_rows, _ = lax.optimization_barrier((dest_owner, text_rows, came))
    w_line = w_line[::-1]
    w_line = cut(jnp.concatenate(w_line + w_line), ((2 * side - 1 - slab) & wrap) * shard, block)
    t_line = jnp.stack(t_line).reshape(side, side, chunk, half_kv)
    pieces = []
    for k in range(side):
        t_given = cut(t_line, (col + k) & wrap, 1, 1).reshape(side * chunk, half_kv)
        piece = jnp.concatenate([w_line, t_given])
        pieces.append(along(piece, 0, k, side) if k else piece)

    own_hidden = cut(hidden, grp * mine_rows, mine_rows)
    hid_next, hid_last = turned(own_hidden, "mp", 1), turned(own_hidden, "mp", -1)
    hid = jnp.concatenate([own_hidden, hid_next, turned(hid_next, "mp", 1), hid_last])

    text_count = text_rows.shape[0] // 2
    text_wide = cut(text_rows, grp * text_count, text_count).astype(f32)
    text_inverse = lax.rsqrt(jnp.mean(text_wide * text_wide, axis=1, keepdims=True) + epsilon)

    a_half = cut(llm_frozen.T, grp * half_rank, half_rank)
    a_mine = to_everyone(a_half, ("dp", "mp")).transpose(1, 0, 2).reshape(half_rank, width)
    a_all = jnp.concatenate([a_mine, crossed(a_mine)])
    a_part = cut(a_all, mp * part_width, part_width, 1)
    b_all = jnp.where(first, llm_adapter, jnp.roll(llm_adapter, half_rank, axis=0))
    b_half = cut(b_all, grp * half_kv, half_kv, 1)
    bias_wide = value_bias.astype(f32)[None]
    bias_half = cut(bias_wide, grp * half_kv, half_kv, 1)

    destiny = dest_owner[:, 0]
    block_dest = cut(destiny, dp * ENC_DEV, ENC_DEV)
    local = jnp.arange(ENC_DEV, dtype=jnp.int32)
    from_mp = (mp - (local % (ENC_DEV // 2)) // mine_rows) & wrap
    from_grp = (grp + local // (ENC_DEV // 2)) & 1
    place = from_mp * block_rows + from_grp * mine_rows + (local & (mine_rows - 1))
    own_dest = jnp.sum(jnp.where(place[:, None] == local[None, :], block_dest[None, :], 0), axis=1)
    earlier = (own_dest[:, None] == block_dest[None, :]) & (local[None, :] < place[:, None])
    slot = jnp.sum(earlier.astype(jnp.int32), axis=1)
    own_mp, own_col, own_slab = own_dest & wrap, (own_dest // side) & wrap, own_dest // (side * side)
    line = (((col - own_col) & wrap) * side + ((slab - own_slab) & wrap)) * capacity + slot
    line = jnp.where(own_mp == mp, line, -1)
    position = (slot * n_dp + dp).astype(f32)

    enc_low = dot(hid, enc_frozen).astype(bf16)
    merged = dot(hid, enc_weight) + enc_bias.astype(f32) + dot(enc_low, enc_adapter)
    image = merged.astype(bf16)
    gain_wide = norm_gain.astype(f32)[None]
    text_normed = (text_wide * text_inverse * gain_wide).astype(bf16)
    a_text = a_all
    text_low = dot_nt(text_normed, a_text).astype(bf16)
    owner_index = dp * n_mp + mp
    counts = jnp.sum((destiny.reshape(n_dp, ENC_DEV) == owner_index).astype(jnp.int32), axis=1)
    row = grp * text_count + jnp.arange(text_count, dtype=jnp.int32)
    taken = (row < area) & (
        row // n_dp
        < jnp.sum(
            jnp.where(
                (row & (n_dp - 1))[:, None] == jnp.arange(n_dp, dtype=jnp.int32)[None, :],
                counts,
                0,
            ),
            axis=1,
        )
    )
    keep = (row < own_length) & ~taken
    text_kept = jnp.where(keep[:, None], text_low, jnp.zeros_like(text_low))
    text_weight = 1.0 / own_length.astype(f32)
    text_sum = dot_tn(text_kept, text_normed) * text_weight
    own_text_targets = cut(targets, grp * text_count, text_count).astype(f32)
    rest = bias_wide + dot(text_low, b_all) - own_text_targets
    rest_high, rest_low = split_two(rest)
    rest_sum = dot_tn(
        jnp.concatenate([text_kept, text_kept]), jnp.concatenate([rest_high, rest_low])
    )
    rest_sum = rest_sum * text_weight
    both_sums = jnp.concatenate([text_sum, rest_sum], axis=1)
    both_sums = both_sums[:half_rank] + crossed(both_sums[half_rank:])
    image_far = crossed(image)
    enc_low_far = crossed(enc_low)
    gain_part = cut(gain_wide, mp * part_width, part_width, 1)
    where = jnp.stack([col, grp]).astype(jnp.int32)
    sizes = dict(half_kv=half_kv, rank=rank)
    lanes = kv + 2 * rank
    tokens = 2 * mine_rows
    to_one = jax.ShapeDtypeStruct((tokens, lanes), bf16)
    own, *to = pl.pallas_call(
        functools.partial(partial_kernel, chunk=chunk, block=block, step=mine_rows, **sizes),
        out_shape=(jax.ShapeDtypeStruct((tokens, lanes), f32), to_one, to_one, to_one),
        in_specs=[SMEM] + [VMEM] * 10,
        out_specs=(VMEM,) * 4,
        scratch_shapes=[pltpu.VMEM((ENC_DEV, lanes), f32)],
        compiler_params=PARAMS,
        name="partial_products",
    )(where, image, image_far, gain_part, a_part, *pieces, line[:, None], position[:, None])
    got = [turned(to[k - 1], "mp", -k) for k in range(1, n_mp)]
    packed = pl.pallas_call(
        functools.partial(row_kernel, width=float(width), **sizes),
        out_shape=jax.ShapeDtypeStruct((tokens, half_kv + 2 * rank), bf16),
        in_specs=[VMEM] * 6,
        out_specs=VMEM,
        compiler_params=PARAMS,
        name="row_work",
    )(own, *got, b_half, bias_half)
    text_parts = both_sums[:, :width].reshape(half_rank, owners, shard).transpose(1, 0, 2)
    text_parts = lax.all_to_all(text_parts.astype(bf16), ("dp", "mp"), 0, 0, tiled=True)
    got = [turned(packed, "mp", k) for k in range(1, n_mp)]
    text_here = jnp.sum(text_parts.astype(f32), axis=0)
    here_high, here_low = split_two(text_here)
    text_grad = dot(jnp.concatenate([here_high, here_low]), value_weight)
    text_grad = text_grad[:half_rank] + text_grad[half_rank:] + both_sums[:, width:]
    text_grad = text_grad + (
        turned(text_grad, "mp", 1) + turned(text_grad, "mp", 2) + turned(text_grad, "mp", 3)
    )
    enc_low_far, text_grad = lax.optimization_barrier((enc_low_far, text_grad))
    mine, give = pl.pallas_call(
        functools.partial(image_kernel, block=block, step=mine_rows, **sizes),
        out_shape=(jax.ShapeDtypeStruct((half_rank, part_width + half_kv), f32),) * 2,
        in_specs=[SMEM] + [VMEM] * 15,
        out_specs=(VMEM, VMEM),
        scratch_shapes=[
            pltpu.VMEM((ENC_DEV, half_kv + 2 * rank), bf16),
            pltpu.VMEM((rank, block), f32),
        ],
        compiler_params=PARAMS,
        name="image_gradients",
    )(
        where,
        packed,
        *got,
        image,
        image_far,
        enc_low,
        enc_low_far,
        gain_part,
        a_part,
        *pieces,
        b_half,
    )

    came = crossed(give)
    llm_mine, llm_came = mine[:, part_width:], came[:, part_width:]
    enc = (mine[:, :part_width] + came[:, :part_width]).reshape(side, 8, side, -1)
    llm = (
        jnp.concatenate(
            [jnp.where(first, llm_mine, llm_came), jnp.where(first, llm_came, llm_mine)], axis=1
        )
        + text_grad
    ).reshape(side, 8, side, -1)
    mine = jnp.concatenate([enc, llm], axis=3).transpose(0, 2, 1, 3).reshape(n_dp, 8, -1)
    mine = jnp.sum(lax.all_to_all(mine, "dp", 0, 0, tiled=True), axis=0)
    whole = to_everyone(mine, "dp").reshape(side, side, 8, -1).transpose(0, 2, 1, 3)
    at = part_width // side
    return whole[..., :at].reshape(half_rank, -1), whole[..., at:].reshape(half_rank, -1)


def solution(mesh):
    return jax.shard_map(
        body,
        mesh=mesh,
        in_specs=(
            P(("dp", "mp"), None),
            P(None, "mp"),
            P("mp"),
            P(),
            P(None, "mp"),
            P(("dp", "mp"), None),
            P(),
            P(("dp", "mp"), None),
            P(),
            P(("dp", "mp"), None),
            P(),
            P(("dp", "mp"), None),
            P(),
            P(("dp", "mp")),
        ),
        out_specs=(P("grp", "mp"), P("grp", None)),
        check_vma=False,
    )
```

```python
import functools

import jax
import jax.numpy as jnp
from jax import lax
from jax.experimental import pallas as pl
from jax.experimental.pallas import tpu as pltpu
from jax.sharding import PartitionSpec as P

ENC_DEV = 256
epsilon = 1e-06
f32 = jnp.float32
bf16 = jnp.bfloat16


def dot(a, b):
    return jnp.dot(a, b, preferred_element_type=f32)


def dot_tn(a, b):
    return lax.dot_general(a, b, (((0,), (0,)), ((), ())), preferred_element_type=f32)


def dot_nt(a, b):
    return lax.dot_general(a, b, (((1,), (1,)), ((), ())), preferred_element_type=f32)


def split_two(a):
    high = lax.reduce_precision(a, 8, 7)
    return high.astype(bf16), (a - high).astype(bf16)


def split_three(a):
    high = lax.reduce_precision(a, 8, 7)
    return (high.astype(bf16), *split_two(a - high))


def turned(array, axis, step):
    count = lax.axis_size(axis)
    return lax.ppermute(array, axis, [(i, (i + step) % count) for i in range(count)])


def crossed(array):
    return lax.ppermute(array, "grp", [(0, 1), (1, 0)])


def along(array, z_step, x_step, side):
    pairs = [
        (z * side + x, (z + z_step) % side * side + (x + x_step) % side)
        for z in range(side)
        for x in range(side)
    ]
    return lax.ppermute(array, "dp", pairs)


def to_everyone(array, axes):
    count = lax.axis_size(axes)
    return lax.all_to_all(
        jnp.broadcast_to(array[None], (count, *array.shape)), axes, 0, 0, tiled=True
    )


def cut(array, start, size, axis=0):
    starts = [jnp.int32(0)] * array.ndim
    starts[axis] = start
    sizes = list(array.shape)
    sizes[axis] = size
    return lax.dynamic_slice(array, starts, sizes, allow_negative_indices=False)


VMEM = pl.BlockSpec(memory_space=pltpu.VMEM)
SMEM = pl.BlockSpec(memory_space=pltpu.SMEM)
PARAMS = pltpu.CompilerParams(vmem_limit_bytes=48 * 1024 * 1024)


def block_start(col, k, side, size):
    return pl.multiple_of(((col + side - k) & (side - 1)) * size, 128)


def partial_kernel(
    place,
    near,
    far,
    gain,
    a_part,
    w0,
    w1,
    w2,
    w3,
    line,
    position,
    own,
    to1,
    to2,
    to3,
    sums,
    *,
    block,
    half_kv,
    rank,
    chunk,
    step,
):
    rows = near.shape[0]
    pieces = (w0, w1, w2, w3)
    side = len(pieces)
    per = chunk // 2
    wide_rows, lengths = [], []
    for piece in pieces:
        for z in range(side):
            both = piece[block + z * chunk : block + (z + 1) * chunk, :].astype(f32)
            wide_rows.append(both[:per])
            lengths.append(both[per:, :128])
    table = jnp.concatenate(wide_rows).astype(bf16)
    lengths = jnp.concatenate(lengths).astype(bf16)
    lane = lax.broadcasted_iota(jnp.int32, (rows, rank), 1)
    for h, source in enumerate((near, far)):
        out = slice(h * rows, (h + 1) * rows)
        values = jnp.zeros((rows, half_kv), f32)
        low = jnp.zeros((rows, rank), f32)
        squares = jnp.zeros((rows, 1), f32)
        for k, piece in enumerate(pieces):
            here = pl.ds(block_start(place[0], k, side, block), block)
            wide = source[:, here].astype(f32)
            scaled = (wide * gain[:, here]).astype(bf16)
            squares = squares + jnp.sum(wide * wide, axis=1, keepdims=True)
            values = values + dot(scaled, piece[:block, :])
            low = low + dot_nt(scaled, a_part[:, here])
        entries = lax.broadcasted_iota(jnp.int32, (rows, table.shape[0]), 1)
        pick = (line[out, :] == entries).astype(bf16)
        length = dot(pick, lengths)[:, :1]
        high = squares.astype(bf16).astype(f32)
        middle = (squares - high).astype(bf16).astype(f32)
        last = squares - high - middle
        extra = jnp.zeros((rows, rank), f32)
        for i, number in enumerate((high, middle, last, length)):
            extra = jnp.where(lane == i, number, extra)
        sums[out, :half_kv] = values
        sums[out, half_kv : half_kv + 2 * rank] = jnp.concatenate([low, extra], axis=1)
        sums[out, half_kv + 2 * rank :] = dot(pick, table)
    lane = lax.broadcasted_iota(jnp.int32, (step, 2 * rank), 1)
    for k, target in enumerate((own, to1, to2, to3)):
        for h in range(2):
            start = h * rows + k * step
            target[h * step : (h + 1) * step, :] = sums[pl.ds(start, step), :].astype(target.dtype)
            if k == 0:
                extra = sums[pl.ds(start, step), half_kv : half_kv + 2 * rank]
                extra = jnp.where(lane == rank + 4, position[pl.ds(start, step), :], extra)
                own[h * step : (h + 1) * step, half_kv : half_kv + 2 * rank] = extra


def row_kernel(own, got1, got2, got3, b_half, bias, packed, *, half_kv, rank, width):
    total = own[...]
    for got in (got1, got2, got3):
        total = total + got[...].astype(f32)
    raw_values = total[:, :half_kv]
    raw_low = total[:, half_kv : half_kv + rank]
    at = half_kv + rank
    squares = total[:, at : at + 1] + total[:, at + 1 : at + 2] + total[:, at + 2 : at + 3]
    length = total[:, at + 3 : at + 4]
    position = total[:, at + 4 : at + 5]
    weight = jnp.where(position < length, 1.0 / length, 0.0)
    inverse = lax.rsqrt(squares / width + epsilon)
    low = (raw_low * inverse).astype(bf16)
    values_out = raw_values * inverse + bias[...] + dot(low, b_half[...])
    dvalues = ((values_out - total[:, half_kv + 2 * rank :]) * weight).astype(bf16)
    dlow = dot_nt(dvalues, b_half[...]).astype(bf16)
    centre = (
        jnp.sum(dvalues.astype(f32) * raw_values, axis=1, keepdims=True)
        + jnp.sum(dlow.astype(f32) * raw_low, axis=1, keepdims=True)
    ) / width
    factor = inverse * inverse * inverse * centre
    lane = lax.broadcasted_iota(jnp.int32, (total.shape[0], rank), 1)
    extra = jnp.zeros((total.shape[0], rank), f32)
    for i, number in enumerate((inverse, factor)):
        for j in range(3):
            part = number.astype(bf16).astype(f32)
            extra = jnp.where(lane == 3 * i + j, part, extra)
            number = number - part
    packed[:, :half_kv] = dvalues
    packed[:, half_kv:] = jnp.concatenate([low.astype(f32), extra], axis=1).astype(bf16)


def image_kernel(
    place,
    packed,
    got1,
    got2,
    got3,
    near,
    far,
    low_near,
    low_far,
    gain,
    a_part,
    w0,
    w1,
    w2,
    w3,
    b_half,
    mine,
    give,
    rows,
    ranks,
    *,
    block,
    half_kv,
    rank,
    step,
):
    pieces = (w0, w1, w2, w3)
    side = len(pieces)
    count = near.shape[0]
    for k, source in enumerate((packed, got1, got2, got3)):
        for h in range(2):
            start = h * count + k * step
            rows[pl.ds(start, step), :] = source[h * step : (h + 1) * step, :]
    dvalues = rows[:, :half_kv]
    extra = rows[:, half_kv:]
    low = extra[:, :rank]
    numbers = extra[:, rank:].astype(f32)
    inverse = numbers[:, 0:1] + numbers[:, 1:2] + numbers[:, 2:3]
    factor = numbers[:, 3:4] + numbers[:, 4:5] + numbers[:, 5:6]
    dlow = dot_nt(dvalues, b_half[...]).astype(bf16)
    half = rank // 2
    grad = dot_tn(low, dvalues)
    mine[:, side * block :] = grad[:half]
    give[:, side * block :] = grad[half:]
    enc_low = jnp.concatenate([low_near[...], low_far[...]])
    for k, piece in enumerate(pieces):
        here = pl.ds(block_start(place[0], k, side, block), block)
        dnormed = dot_nt(dvalues, piece[:block, :]) + dot(dlow, a_part[:, here])
        wide = jnp.concatenate([near[:, here], far[:, here]]).astype(f32)
        dimage = (inverse * (gain[:, here] * dnormed) - wide * factor).astype(bf16)
        ranks[...] = dot_tn(enc_low, dimage)
        mine[:, here] = ranks[pl.ds(pl.multiple_of(place[1] * half, half), half), :]
        give[:, here] = ranks[pl.ds(pl.multiple_of((1 - place[1]) * half, half), half), :]


def place_kernel(whole, enc, llm, *, side):
    rows = whole.shape[1]
    enc_step, llm_step = enc.shape[1] // side, llm.shape[1] // side
    for i in range(side):
        for j in range(side):
            here = slice(i * rows, (i + 1) * rows)
            part = whole[i * side + j]
            enc[here, j * enc_step : (j + 1) * enc_step] = part[:, :enc_step]
            llm[here, j * llm_step : (j + 1) * llm_step] = part[:, enc_step:]


def body(
    hidden,
    enc_weight,
    enc_bias,
    enc_frozen,
    enc_adapter,
    text_rows,
    norm_gain,
    value_weight,
    value_bias,
    llm_frozen,
    llm_adapter,
    targets,
    dest_owner,
    seq_length,
):
    n_dp = lax.axis_size("dp")
    n_mp = lax.axis_size("mp")
    side = n_mp
    owners = n_dp * n_mp
    grp = lax.axis_index("grp")
    dp = lax.axis_index("dp")
    mp = lax.axis_index("mp")
    first = grp == 0
    width = text_rows.shape[1]
    part_width = enc_weight.shape[1]
    rank = enc_frozen.shape[1]
    half_rank = rank // 2
    kv = value_weight.shape[1]
    half_kv = kv // 2
    shard = value_weight.shape[0]
    block = side * shard
    block_rows = hidden.shape[0]
    mine_rows = block_rows // 2
    capacity = 2 * ENC_DEV // owners
    chunk = 2 * capacity
    area = capacity * n_dp
    slab, col = dp // side, dp & (side - 1)
    wrap = side - 1

    swap = [
        ((z * side + x) * side + y, (y * side + x) * side + z)
        for z in range(side)
        for x in range(side)
        for y in range(side)
    ]
    w_half = cut(value_weight, grp * half_kv, half_kv, 1)
    w_moved = lax.ppermute(w_half, ("dp", "mp"), swap)

    own_length = seq_length[0]
    t_half = cut(targets[:area], grp * half_kv, half_kv, 1)
    t_half = t_half.reshape(capacity, n_dp, half_kv).transpose(1, 0, 2)
    t_half = jnp.concatenate([t_half, jnp.full_like(t_half, own_length.astype(bf16))], axis=1)
    t_half = t_half.reshape(side, side * chunk, half_kv)
    w_line, t_line = [w_moved], [cut(t_half, slab, 1)[0]]
    for k in range(1, side):
        t_given = cut(t_half, (slab + k) & wrap, 1)[0]
        came = along(jnp.concatenate([w_moved, t_given]), k, 0, side)
        w_line.append(came[:shard])
        t_line.append(came[shard:])
    dest_owner, text_rows, _ = lax.optimization_barrier((dest_owner, text_rows, came))
    w_line = w_line[::-1]
    w_line = cut(jnp.concatenate(w_line + w_line), ((2 * side - 1 - slab) & wrap) * shard, block)
    t_line = jnp.stack(t_line).reshape(side, side, chunk, half_kv)
    pieces = []
    for k in range(side):
        t_given = cut(t_line, (col + k) & wrap, 1, 1).reshape(side * chunk, half_kv)
        piece = jnp.concatenate([w_line, t_given])
        pieces.append(along(piece, 0, k, side) if k else piece)

    own_hidden = cut(hidden, grp * mine_rows, mine_rows)
    hid_next, hid_last = turned(own_hidden, "mp", 1), turned(own_hidden, "mp", -1)
    hid = jnp.concatenate([own_hidden, hid_next, turned(hid_next, "mp", 1), hid_last])

    text_count = text_rows.shape[0] // 2
    text_wide = cut(text_rows, grp * text_count, text_count).astype(f32)
    text_inverse = lax.rsqrt(jnp.mean(text_wide * text_wide, axis=1, keepdims=True) + epsilon)

    a_half = cut(llm_frozen.T, grp * half_rank, half_rank)
    a_mine = to_everyone(a_half, ("dp", "mp"))
    a_both = [a.transpose(1, 0, 2).reshape(half_rank, width) for a in (a_mine, crossed(a_mine))]
    a_all = jnp.concatenate(a_both)
    a_part = cut(a_all, mp * part_width, part_width, 1)
    b_all = jnp.where(first, llm_adapter, jnp.roll(llm_adapter, half_rank, axis=0))
    b_half = cut(b_all, grp * half_kv, half_kv, 1)
    bias_wide = value_bias.astype(f32)[None]
    bias_half = cut(bias_wide, grp * half_kv, half_kv, 1)

    destiny = dest_owner[:, 0]
    block_dest = cut(destiny, dp * ENC_DEV, ENC_DEV)
    local = jnp.arange(ENC_DEV, dtype=jnp.int32)
    from_mp = (mp - (local % (ENC_DEV // 2)) // mine_rows) & wrap
    from_grp = (grp + local // (ENC_DEV // 2)) & 1
    place = from_mp * block_rows + from_grp * mine_rows + (local & (mine_rows - 1))
    own_dest = jnp.sum(jnp.where(place[:, None] == local[None, :], block_dest[None, :], 0), axis=1)
    earlier = (own_dest[:, None] == block_dest[None, :]) & (local[None, :] < place[:, None])
    slot = jnp.sum(earlier.astype(jnp.int32), axis=1)
    own_mp, own_col, own_slab = own_dest & wrap, (own_dest // side) & wrap, own_dest // (side * side)
    line = (((col - own_col) & wrap) * side + ((slab - own_slab) & wrap)) * capacity + slot
    line = jnp.where(own_mp == mp, line, -1)
    position = (slot * n_dp + dp).astype(f32)

    enc_low = dot(hid, enc_frozen).astype(bf16)
    merged = dot(hid, enc_weight) + enc_bias.astype(f32) + dot(enc_low, enc_adapter)
    image = merged.astype(bf16)
    gain_wide = norm_gain.astype(f32)[None]
    text_normed = (text_wide * text_inverse * gain_wide).astype(bf16)
    a_text = a_all
    text_low = dot_nt(text_normed, a_text).astype(bf16)
    owner_index = dp * n_mp + mp
    counts = jnp.sum((destiny.reshape(n_dp, ENC_DEV) == owner_index).astype(jnp.int32), axis=1)
    row = grp * text_count + jnp.arange(text_count, dtype=jnp.int32)
    taken = (row < area) & (
        row // n_dp
        < jnp.sum(
            jnp.where(
                (row & (n_dp - 1))[:, None] == jnp.arange(n_dp, dtype=jnp.int32)[None, :],
                counts,
                0,
            ),
            axis=1,
        )
    )
    keep = (row < own_length) & ~taken
    text_kept = jnp.where(keep[:, None], text_low, jnp.zeros_like(text_low))
    text_weight = 1.0 / own_length.astype(f32)
    text_sum = dot_tn(text_kept, text_normed) * text_weight
    own_text_targets = cut(targets, grp * text_count, text_count).astype(f32)
    rest = bias_wide + dot(text_low, b_all) - own_text_targets
    rest_high, rest_low = split_two(rest)
    rest_sum = dot_tn(
        jnp.concatenate([text_kept, text_kept]), jnp.concatenate([rest_high, rest_low])
    )
    rest_sum = rest_sum * text_weight
    both_sums = jnp.concatenate([text_sum, rest_sum], axis=1)
    both_sums = both_sums[:half_rank] + crossed(both_sums[half_rank:])
    image_far = crossed(image)
    enc_low_far = crossed(enc_low)
    gain_part = cut(gain_wide, mp * part_width, part_width, 1)
    where = jnp.stack([col, grp]).astype(jnp.int32)
    sizes = dict(half_kv=half_kv, rank=rank)
    lanes = kv + 2 * rank
    tokens = 2 * mine_rows
    to_one = jax.ShapeDtypeStruct((tokens, lanes), bf16)
    own, *to = pl.pallas_call(
        functools.partial(partial_kernel, chunk=chunk, block=block, step=mine_rows, **sizes),
        out_shape=(jax.ShapeDtypeStruct((tokens, lanes), f32), to_one, to_one, to_one),
        in_specs=[SMEM] + [VMEM] * 10,
        out_specs=(VMEM,) * 4,
        scratch_shapes=[pltpu.VMEM((ENC_DEV, lanes), f32)],
        compiler_params=PARAMS,
        name="partial_products",
    )(where, image, image_far, gain_part, a_part, *pieces, line[:, None], position[:, None])
    got = [turned(to[k - 1], "mp", -k) for k in range(1, n_mp)]
    packed = pl.pallas_call(
        functools.partial(row_kernel, width=float(width), **sizes),
        out_shape=jax.ShapeDtypeStruct((tokens, half_kv + 2 * rank), bf16),
        in_specs=[VMEM] * 6,
        out_specs=VMEM,
        compiler_params=PARAMS,
        name="row_work",
    )(own, *got, b_half, bias_half)
    text_parts = both_sums[:, :width].reshape(half_rank, owners, shard).transpose(1, 0, 2)
    text_parts = lax.all_to_all(text_parts.astype(bf16), ("dp", "mp"), 0, 0, tiled=True)
    got = [turned(packed, "mp", k) for k in range(1, n_mp)]
    text_here = jnp.sum(text_parts.astype(f32), axis=0)
    here_high, here_low = split_two(text_here)
    text_grad = dot(jnp.concatenate([here_high, here_low]), value_weight)
    text_grad = text_grad[:half_rank] + text_grad[half_rank:] + both_sums[:, width:]
    text_grad = text_grad + (
        turned(text_grad, "mp", 1) + turned(text_grad, "mp", 2) + turned(text_grad, "mp", 3)
    )
    enc_low_far, text_grad = lax.optimization_barrier((enc_low_far, text_grad))
    mine, give = pl.pallas_call(
        functools.partial(image_kernel, block=block, step=mine_rows, **sizes),
        out_shape=(jax.ShapeDtypeStruct((half_rank, part_width + half_kv), f32),) * 2,
        in_specs=[SMEM] + [VMEM] * 15,
        out_specs=(VMEM, VMEM),
        scratch_shapes=[
            pltpu.VMEM((ENC_DEV, half_kv + 2 * rank), bf16),
            pltpu.VMEM((rank, block), f32),
        ],
        compiler_params=PARAMS,
        name="image_gradients",
    )(
        where,
        packed,
        *got,
        image,
        image_far,
        enc_low,
        enc_low_far,
        gain_part,
        a_part,
        *pieces,
        b_half,
    )

    came = crossed(give)
    llm_mine, llm_came = mine[:, part_width:], came[:, part_width:]
    enc = (mine[:, :part_width] + came[:, :part_width]).reshape(side, 8, side, -1)
    llm = (
        jnp.concatenate(
            [jnp.where(first, llm_mine, llm_came), jnp.where(first, llm_came, llm_mine)], axis=1
        )
        + text_grad
    ).reshape(side, 8, side, -1)
    mine = jnp.concatenate([enc, llm], axis=3).transpose(0, 2, 1, 3).reshape(n_dp, 8, -1)
    mine = jnp.sum(lax.all_to_all(mine, "dp", 0, 0, tiled=True), axis=0)
    whole = to_everyone(mine, "dp")
    return pl.pallas_call(
        functools.partial(place_kernel, side=side),
        out_shape=(
            jax.ShapeDtypeStruct((half_rank, part_width), f32),
            jax.ShapeDtypeStruct((half_rank, kv), f32),
        ),
        in_specs=[VMEM],
        out_specs=(VMEM, VMEM),
        compiler_params=PARAMS,
        name="placed",
    )(whole)


def solution(mesh):
    return jax.shard_map(
        body,
        mesh=mesh,
        in_specs=(
            P(("dp", "mp"), None),
            P(None, "mp"),
            P("mp"),
            P(),
            P(None, "mp"),
            P(("dp", "mp"), None),
            P(),
            P(("dp", "mp"), None),
            P(),
            P(("dp", "mp"), None),
            P(),
            P(("dp", "mp"), None),
            P(),
            P(("dp", "mp")),
        ),
        out_specs=(P("grp", "mp"), P("grp", None)),
        check_vma=False,
    )
```

```python
import functools

import jax
import jax.numpy as jnp
from jax import lax
from jax.experimental import pallas as pl
from jax.experimental.pallas import tpu as pltpu
from jax.sharding import PartitionSpec as P

ENC_DEV = 256
epsilon = 1e-06
f32 = jnp.float32
bf16 = jnp.bfloat16


def dot(a, b):
    return jnp.dot(a, b, preferred_element_type=f32)


def dot_tn(a, b):
    return lax.dot_general(a, b, (((0,), (0,)), ((), ())), preferred_element_type=f32)


def dot_nt(a, b):
    return lax.dot_general(a, b, (((1,), (1,)), ((), ())), preferred_element_type=f32)


def split_two(a):
    high = lax.reduce_precision(a, 8, 7)
    return high.astype(bf16), (a - high).astype(bf16)


def split_three(a):
    high = lax.reduce_precision(a, 8, 7)
    return (high.astype(bf16), *split_two(a - high))


def turned(array, axis, step):
    count = lax.axis_size(axis)
    return lax.ppermute(array, axis, [(i, (i + step) % count) for i in range(count)])


def crossed(array):
    return lax.ppermute(array, "grp", [(0, 1), (1, 0)])


def along(array, z_step, x_step, side):
    pairs = [
        (z * side + x, (z + z_step) % side * side + (x + x_step) % side)
        for z in range(side)
        for x in range(side)
    ]
    return lax.ppermute(array, "dp", pairs)


def to_everyone(array, axes):
    count = lax.axis_size(axes)
    return lax.all_to_all(
        jnp.broadcast_to(array[None], (count, *array.shape)), axes, 0, 0, tiled=True
    )


def cut(array, start, size, axis=0):
    starts = [jnp.int32(0)] * array.ndim
    starts[axis] = start
    sizes = list(array.shape)
    sizes[axis] = size
    return lax.dynamic_slice(array, starts, sizes, allow_negative_indices=False)


VMEM = pl.BlockSpec(memory_space=pltpu.VMEM)
SMEM = pl.BlockSpec(memory_space=pltpu.SMEM)
PARAMS = pltpu.CompilerParams(vmem_limit_bytes=48 * 1024 * 1024)


def block_start(col, k, side, size):
    return pl.multiple_of(((col + side - k) & (side - 1)) * size, 128)


def partial_kernel(
    place,
    near,
    far,
    gain,
    a_part,
    w0,
    w1,
    w2,
    w3,
    line,
    position,
    own,
    to1,
    to2,
    to3,
    sums,
    *,
    block,
    half_kv,
    rank,
    chunk,
    step,
):
    rows = near.shape[0]
    pieces = (w0, w1, w2, w3)
    side = len(pieces)
    per = chunk // 2
    wide_rows, lengths = [], []
    for piece in pieces:
        for z in range(side):
            both = piece[block + z * chunk : block + (z + 1) * chunk, :].astype(f32)
            wide_rows.append(both[:per])
            lengths.append(both[per:, :128])
    table = jnp.concatenate(wide_rows).astype(bf16)
    lengths = jnp.concatenate(lengths).astype(bf16)
    lane = lax.broadcasted_iota(jnp.int32, (rows, rank), 1)
    for h, source in enumerate((near, far)):
        out = slice(h * rows, (h + 1) * rows)
        values = jnp.zeros((rows, half_kv), f32)
        low = jnp.zeros((rows, rank), f32)
        squares = jnp.zeros((rows, 1), f32)
        for k, piece in enumerate(pieces):
            here = pl.ds(block_start(place[0], k, side, block), block)
            wide = source[:, here].astype(f32)
            scaled = (wide * gain[:, here]).astype(bf16)
            squares = squares + jnp.sum(wide * wide, axis=1, keepdims=True)
            values = values + dot(scaled, piece[:block, :])
            low = low + dot_nt(scaled, a_part[:, here])
        entries = lax.broadcasted_iota(jnp.int32, (rows, table.shape[0]), 1)
        pick = (line[out, :] == entries).astype(bf16)
        length = dot(pick, lengths)[:, :1]
        high = squares.astype(bf16).astype(f32)
        middle = (squares - high).astype(bf16).astype(f32)
        last = squares - high - middle
        extra = jnp.zeros((rows, rank), f32)
        for i, number in enumerate((high, middle, last, length)):
            extra = jnp.where(lane == i, number, extra)
        sums[out, :half_kv] = values
        sums[out, half_kv : half_kv + 2 * rank] = jnp.concatenate([low, extra], axis=1)
        sums[out, half_kv + 2 * rank :] = dot(pick, table)
    lane = lax.broadcasted_iota(jnp.int32, (step, 2 * rank), 1)
    for k, target in enumerate((own, to1, to2, to3)):
        for h in range(2):
            start = h * rows + k * step
            target[h * step : (h + 1) * step, :] = sums[pl.ds(start, step), :].astype(target.dtype)
            if k == 0:
                extra = sums[pl.ds(start, step), half_kv : half_kv + 2 * rank]
                extra = jnp.where(lane == rank + 4, position[pl.ds(start, step), :], extra)
                own[h * step : (h + 1) * step, half_kv : half_kv + 2 * rank] = extra


def row_kernel(own, got1, got2, got3, b_half, bias, text, packed, *, half_kv, rank, width):
    total = own[...]
    for got in (got1, got2, got3):
        total = total + got[...].astype(f32)
    raw_values = total[:, :half_kv]
    raw_low = total[:, half_kv : half_kv + rank]
    at = half_kv + rank
    squares = total[:, at : at + 1] + total[:, at + 1 : at + 2] + total[:, at + 2 : at + 3]
    length = total[:, at + 3 : at + 4]
    position = total[:, at + 4 : at + 5]
    weight = jnp.where(position < length, 1.0 / length, 0.0)
    inverse = lax.rsqrt(squares / width + epsilon)
    low = (raw_low * inverse).astype(bf16)
    values_out = raw_values * inverse + bias[...] + dot(low, b_half[...])
    dvalues = ((values_out - total[:, half_kv + 2 * rank :]) * weight).astype(bf16)
    dlow = dot_nt(dvalues, b_half[...]).astype(bf16)
    centre = (
        jnp.sum(dvalues.astype(f32) * raw_values, axis=1, keepdims=True)
        + jnp.sum(dlow.astype(f32) * raw_low, axis=1, keepdims=True)
    ) / width
    factor = inverse * inverse * inverse * centre
    lane = lax.broadcasted_iota(jnp.int32, (total.shape[0], rank), 1)
    extra = jnp.zeros((total.shape[0], rank), f32)
    for i, number in enumerate((inverse, factor)):
        for j in range(3):
            part = number.astype(bf16).astype(f32)
            extra = jnp.where(lane == 3 * i + j, part, extra)
            number = number - part
    packed[:, :half_kv] = dvalues
    at = half_kv + 2 * rank
    packed[:, half_kv:at] = jnp.concatenate([low.astype(f32), extra], axis=1).astype(bf16)
    half = text.shape[0]
    packed[:half, at:] = text[:, :half_kv].astype(bf16)
    packed[half:, at:] = text[:, half_kv:].astype(bf16)


def image_kernel(
    place,
    packed,
    got1,
    got2,
    got3,
    near,
    far,
    low_near,
    low_far,
    gain,
    a_part,
    w0,
    w1,
    w2,
    w3,
    b_half,
    mine,
    give,
    text,
    rows,
    ranks,
    *,
    block,
    half_kv,
    rank,
    step,
):
    pieces = (w0, w1, w2, w3)
    side = len(pieces)
    count = near.shape[0]
    for k, source in enumerate((packed, got1, got2, got3)):
        for h in range(2):
            start = h * count + k * step
            rows[pl.ds(start, step), :] = source[h * step : (h + 1) * step, :half_kv + 2 * rank]
    total = packed[:, half_kv + 2 * rank :].astype(f32)
    for source in (got1, got2, got3):
        total = total + source[:, half_kv + 2 * rank :].astype(f32)
    text[:, :half_kv] = total[:step]
    text[:, half_kv:] = total[step:]
    dvalues = rows[:, :half_kv]
    extra = rows[:, half_kv:]
    low = extra[:, :rank]
    numbers = extra[:, rank:].astype(f32)
    inverse = numbers[:, 0:1] + numbers[:, 1:2] + numbers[:, 2:3]
    factor = numbers[:, 3:4] + numbers[:, 4:5] + numbers[:, 5:6]
    dlow = dot_nt(dvalues, b_half[...]).astype(bf16)
    half = rank // 2
    grad = dot_tn(low, dvalues)
    mine[:, side * block :] = grad[:half]
    give[:, side * block :] = grad[half:]
    enc_low = jnp.concatenate([low_near[...], low_far[...]])
    for k, piece in enumerate(pieces):
        here = pl.ds(block_start(place[0], k, side, block), block)
        dnormed = dot_nt(dvalues, piece[:block, :]) + dot(dlow, a_part[:, here])
        wide = jnp.concatenate([near[:, here], far[:, here]]).astype(f32)
        dimage = (inverse * (gain[:, here] * dnormed) - wide * factor).astype(bf16)
        ranks[...] = dot_tn(enc_low, dimage)
        mine[:, here] = ranks[pl.ds(pl.multiple_of(place[1] * half, half), half), :]
        give[:, here] = ranks[pl.ds(pl.multiple_of((1 - place[1]) * half, half), half), :]


def place_kernel(whole, enc, llm, *, side):
    rows = whole.shape[1]
    enc_step, llm_step = enc.shape[1] // side, llm.shape[1] // side
    for i in range(side):
        for j in range(side):
            here = slice(i * rows, (i + 1) * rows)
            part = whole[i * side + j]
            enc[here, j * enc_step : (j + 1) * enc_step] = part[:, :enc_step]
            llm[here, j * llm_step : (j + 1) * llm_step] = part[:, enc_step:]


def body(
    hidden,
    enc_weight,
    enc_bias,
    enc_frozen,
    enc_adapter,
    text_rows,
    norm_gain,
    value_weight,
    value_bias,
    llm_frozen,
    llm_adapter,
    targets,
    dest_owner,
    seq_length,
):
    n_dp = lax.axis_size("dp")
    n_mp = lax.axis_size("mp")
    side = n_mp
    owners = n_dp * n_mp
    grp = lax.axis_index("grp")
    dp = lax.axis_index("dp")
    mp = lax.axis_index("mp")
    first = grp == 0
    width = text_rows.shape[1]
    part_width = enc_weight.shape[1]
    rank = enc_frozen.shape[1]
    half_rank = rank // 2
    kv = value_weight.shape[1]
    half_kv = kv // 2
    shard = value_weight.shape[0]
    block = side * shard
    block_rows = hidden.shape[0]
    mine_rows = block_rows // 2
    capacity = 2 * ENC_DEV // owners
    chunk = 2 * capacity
    area = capacity * n_dp
    slab, col = dp // side, dp & (side - 1)
    wrap = side - 1

    swap = [
        ((z * side + x) * side + y, (y * side + x) * side + z)
        for z in range(side)
        for x in range(side)
        for y in range(side)
    ]
    w_half = cut(value_weight, grp * half_kv, half_kv, 1)
    w_moved = lax.ppermute(w_half, ("dp", "mp"), swap)

    own_length = seq_length[0]
    t_half = cut(targets[:area], grp * half_kv, half_kv, 1)
    t_half = t_half.reshape(capacity, n_dp, half_kv).transpose(1, 0, 2)
    t_half = jnp.concatenate([t_half, jnp.full_like(t_half, own_length.astype(bf16))], axis=1)
    t_half = t_half.reshape(side, side * chunk, half_kv)
    w_line, t_line = [w_moved], [cut(t_half, slab, 1)[0]]
    for k in range(1, side):
        t_given = cut(t_half, (slab + k) & wrap, 1)[0]
        came = along(jnp.concatenate([w_moved, t_given]), k, 0, side)
        w_line.append(came[:shard])
        t_line.append(came[shard:])
    dest_owner, text_rows, _ = lax.optimization_barrier((dest_owner, text_rows, came))
    w_line = w_line[::-1]
    w_line = cut(jnp.concatenate(w_line + w_line), ((2 * side - 1 - slab) & wrap) * shard, block)
    t_line = jnp.stack(t_line).reshape(side, side, chunk, half_kv)
    pieces = []
    for k in range(side):
        t_given = cut(t_line, (col + k) & wrap, 1, 1).reshape(side * chunk, half_kv)
        piece = jnp.concatenate([w_line, t_given])
        pieces.append(along(piece, 0, k, side) if k else piece)

    own_hidden = cut(hidden, grp * mine_rows, mine_rows)
    hid_next, hid_last = turned(own_hidden, "mp", 1), turned(own_hidden, "mp", -1)
    hid = jnp.concatenate([own_hidden, hid_next, turned(hid_next, "mp", 1), hid_last])

    text_count = text_rows.shape[0] // 2
    text_wide = cut(text_rows, grp * text_count, text_count).astype(f32)
    text_inverse = lax.rsqrt(jnp.mean(text_wide * text_wide, axis=1, keepdims=True) + epsilon)

    a_half = cut(llm_frozen.T, grp * half_rank, half_rank)
    a_mine = to_everyone(a_half, ("dp", "mp"))
    a_both = [a.transpose(1, 0, 2).reshape(half_rank, width) for a in (a_mine, crossed(a_mine))]
    a_all = jnp.concatenate(a_both)
    a_part = cut(a_all, mp * part_width, part_width, 1)
    b_all = jnp.where(first, llm_adapter, jnp.roll(llm_adapter, half_rank, axis=0))
    b_half = cut(b_all, grp * half_kv, half_kv, 1)
    bias_wide = value_bias.astype(f32)[None]
    bias_half = cut(bias_wide, grp * half_kv, half_kv, 1)

    destiny = dest_owner[:, 0]
    block_dest = cut(destiny, dp * ENC_DEV, ENC_DEV)
    local = jnp.arange(ENC_DEV, dtype=jnp.int32)
    from_mp = (mp - (local % (ENC_DEV // 2)) // mine_rows) & wrap
    from_grp = (grp + local // (ENC_DEV // 2)) & 1
    place = from_mp * block_rows + from_grp * mine_rows + (local & (mine_rows - 1))
    own_dest = jnp.sum(jnp.where(place[:, None] == local[None, :], block_dest[None, :], 0), axis=1)
    earlier = (own_dest[:, None] == block_dest[None, :]) & (local[None, :] < place[:, None])
    slot = jnp.sum(earlier.astype(jnp.int32), axis=1)
    own_mp, own_col, own_slab = own_dest & wrap, (own_dest // side) & wrap, own_dest // (side * side)
    line = (((col - own_col) & wrap) * side + ((slab - own_slab) & wrap)) * capacity + slot
    line = jnp.where(own_mp == mp, line, -1)
    position = (slot * n_dp + dp).astype(f32)

    enc_low = dot(hid, enc_frozen).astype(bf16)
    merged = dot(hid, enc_weight) + enc_bias.astype(f32) + dot(enc_low, enc_adapter)
    image = merged.astype(bf16)
    gain_wide = norm_gain.astype(f32)[None]
    text_normed = (text_wide * text_inverse * gain_wide).astype(bf16)
    a_text = a_all
    text_low = dot_nt(text_normed, a_text).astype(bf16)
    owner_index = dp * n_mp + mp
    counts = jnp.sum((destiny.reshape(n_dp, ENC_DEV) == owner_index).astype(jnp.int32), axis=1)
    row = grp * text_count + jnp.arange(text_count, dtype=jnp.int32)
    taken = (row < area) & (
        row // n_dp
        < jnp.sum(
            jnp.where(
                (row & (n_dp - 1))[:, None] == jnp.arange(n_dp, dtype=jnp.int32)[None, :],
                counts,
                0,
            ),
            axis=1,
        )
    )
    keep = (row < own_length) & ~taken
    text_kept = jnp.where(keep[:, None], text_low, jnp.zeros_like(text_low))
    text_weight = 1.0 / own_length.astype(f32)
    text_sum = dot_tn(text_kept, text_normed) * text_weight
    own_text_targets = cut(targets, grp * text_count, text_count).astype(f32)
    rest = bias_wide + dot(text_low, b_all) - own_text_targets
    rest_high, rest_low = split_two(rest)
    rest_sum = dot_tn(
        jnp.concatenate([text_kept, text_kept]), jnp.concatenate([rest_high, rest_low])
    )
    rest_sum = rest_sum * text_weight
    both_sums = jnp.concatenate([text_sum, rest_sum], axis=1)
    both_sums = both_sums[:half_rank] + crossed(both_sums[half_rank:])
    image_far = crossed(image)
    enc_low_far = crossed(enc_low)
    gain_part = cut(gain_wide, mp * part_width, part_width, 1)
    where = jnp.stack([col, grp]).astype(jnp.int32)
    sizes = dict(half_kv=half_kv, rank=rank)
    lanes = kv + 2 * rank
    tokens = 2 * mine_rows
    to_one = jax.ShapeDtypeStruct((tokens, lanes), bf16)
    own, *to = pl.pallas_call(
        functools.partial(partial_kernel, chunk=chunk, block=block, step=mine_rows, **sizes),
        out_shape=(jax.ShapeDtypeStruct((tokens, lanes), f32), to_one, to_one, to_one),
        in_specs=[SMEM] + [VMEM] * 10,
        out_specs=(VMEM,) * 4,
        scratch_shapes=[pltpu.VMEM((ENC_DEV, lanes), f32)],
        compiler_params=PARAMS,
        name="partial_products",
    )(where, image, image_far, gain_part, a_part, *pieces, line[:, None], position[:, None])
    got = [turned(to[k - 1], "mp", -k) for k in range(1, n_mp)]
    text_parts = both_sums[:, :width].reshape(half_rank, owners, shard).transpose(1, 0, 2)
    text_parts = lax.all_to_all(text_parts.astype(bf16), ("dp", "mp"), 0, 0, tiled=True)
    text_here = jnp.sum(text_parts.astype(f32), axis=0)
    here_high, here_low = split_two(text_here)
    text_grad = dot(jnp.concatenate([here_high, here_low]), value_weight)
    text_grad = text_grad[:half_rank] + text_grad[half_rank:] + both_sums[:, width:]
    packed = pl.pallas_call(
        functools.partial(row_kernel, width=float(width), **sizes),
        out_shape=jax.ShapeDtypeStruct((tokens, kv + 2 * rank), bf16),
        in_specs=[VMEM] * 7,
        out_specs=VMEM,
        compiler_params=PARAMS,
        name="row_work",
    )(own, *got, b_half, bias_half, text_grad)
    got = [turned(packed, "mp", k) for k in range(1, n_mp)]
    mine, give, text_grad = pl.pallas_call(
        functools.partial(image_kernel, block=block, step=mine_rows, **sizes),
        out_shape=(jax.ShapeDtypeStruct((half_rank, part_width + half_kv), f32),) * 2
        + (jax.ShapeDtypeStruct((half_rank, kv), f32),),
        in_specs=[SMEM] + [VMEM] * 15,
        out_specs=(VMEM, VMEM, VMEM),
        scratch_shapes=[
            pltpu.VMEM((ENC_DEV, half_kv + 2 * rank), bf16),
            pltpu.VMEM((rank, block), f32),
        ],
        compiler_params=PARAMS,
        name="image_gradients",
    )(
        where,
        packed,
        *got,
        image,
        image_far,
        enc_low,
        enc_low_far,
        gain_part,
        a_part,
        *pieces,
        b_half,
    )

    came = crossed(give)
    llm_mine, llm_came = mine[:, part_width:], came[:, part_width:]
    enc = (mine[:, :part_width] + came[:, :part_width]).reshape(side, 8, side, -1)
    llm = (
        jnp.concatenate(
            [jnp.where(first, llm_mine, llm_came), jnp.where(first, llm_came, llm_mine)], axis=1
        )
        + text_grad
    ).reshape(side, 8, side, -1)
    mine = jnp.concatenate([enc, llm], axis=3).transpose(0, 2, 1, 3).reshape(n_dp, 8, -1)
    mine = jnp.sum(lax.all_to_all(mine, "dp", 0, 0, tiled=True), axis=0)
    whole = to_everyone(mine, "dp")
    return pl.pallas_call(
        functools.partial(place_kernel, side=side),
        out_shape=(
            jax.ShapeDtypeStruct((half_rank, part_width), f32),
            jax.ShapeDtypeStruct((half_rank, kv), f32),
        ),
        in_specs=[VMEM],
        out_specs=(VMEM, VMEM),
        compiler_params=PARAMS,
        name="placed",
    )(whole)


def solution(mesh):
    return jax.shard_map(
        body,
        mesh=mesh,
        in_specs=(
            P(("dp", "mp"), None),
            P(None, "mp"),
            P("mp"),
            P(),
            P(None, "mp"),
            P(("dp", "mp"), None),
            P(),
            P(("dp", "mp"), None),
            P(),
            P(("dp", "mp"), None),
            P(),
            P(("dp", "mp"), None),
            P(),
            P(("dp", "mp")),
        ),
        out_specs=(P("grp", "mp"), P("grp", None)),
        check_vma=False,
    )
```

```python
import functools

import jax
import jax.numpy as jnp
from jax import lax
from jax.experimental import pallas as pl
from jax.experimental.pallas import tpu as pltpu
from jax.sharding import PartitionSpec as P

ENC_DEV = 256
epsilon = 1e-06
f32 = jnp.float32
bf16 = jnp.bfloat16


def dot(a, b):
    return jnp.dot(a, b, preferred_element_type=f32)


def dot_tn(a, b):
    return lax.dot_general(a, b, (((0,), (0,)), ((), ())), preferred_element_type=f32)


def dot_nt(a, b):
    return lax.dot_general(a, b, (((1,), (1,)), ((), ())), preferred_element_type=f32)


def split_two(a):
    high = lax.reduce_precision(a, 8, 7)
    return high.astype(bf16), (a - high).astype(bf16)


def split_three(a):
    high = lax.reduce_precision(a, 8, 7)
    return (high.astype(bf16), *split_two(a - high))


def turned(array, axis, step):
    count = lax.axis_size(axis)
    return lax.ppermute(array, axis, [(i, (i + step) % count) for i in range(count)])


def crossed(array):
    return lax.ppermute(array, "grp", [(0, 1), (1, 0)])


def along(array, z_step, x_step, side):
    pairs = [
        (z * side + x, (z + z_step) % side * side + (x + x_step) % side)
        for z in range(side)
        for x in range(side)
    ]
    return lax.ppermute(array, "dp", pairs)


def to_everyone(array, axes):
    count = lax.axis_size(axes)
    return lax.all_to_all(
        jnp.broadcast_to(array[None], (count, *array.shape)), axes, 0, 0, tiled=True
    )


def cut(array, start, size, axis=0):
    starts = [jnp.int32(0)] * array.ndim
    starts[axis] = start
    sizes = list(array.shape)
    sizes[axis] = size
    return lax.dynamic_slice(array, starts, sizes, allow_negative_indices=False)


VMEM = pl.BlockSpec(memory_space=pltpu.VMEM)
SMEM = pl.BlockSpec(memory_space=pltpu.SMEM)
PARAMS = pltpu.CompilerParams(vmem_limit_bytes=48 * 1024 * 1024)


def block_start(col, k, side, size):
    return pl.multiple_of(((col + side - k) & (side - 1)) * size, 128)


def partial_kernel(
    place,
    near,
    far,
    gain,
    a_part,
    w0,
    w1,
    w2,
    w3,
    line,
    position,
    own,
    to1,
    to2,
    to3,
    sums,
    *,
    block,
    half_kv,
    rank,
    chunk,
    step,
):
    rows = near.shape[0]
    pieces = (w0, w1, w2, w3)
    side = len(pieces)
    per = chunk // 2
    wide_rows, lengths = [], []
    for piece in pieces:
        for z in range(side):
            both = piece[block + z * chunk : block + (z + 1) * chunk, :].astype(f32)
            wide_rows.append(both[:per])
            lengths.append(both[per:, :128])
    table = jnp.concatenate(wide_rows).astype(bf16)
    lengths = jnp.concatenate(lengths).astype(bf16)
    lane = lax.broadcasted_iota(jnp.int32, (rows, rank), 1)
    for h, source in enumerate((near, far)):
        out = slice(h * rows, (h + 1) * rows)
        values = jnp.zeros((rows, half_kv), f32)
        low = jnp.zeros((rows, rank), f32)
        squares = jnp.zeros((rows, 1), f32)
        for k, piece in enumerate(pieces):
            here = pl.ds(block_start(place[0], k, side, block), block)
            wide = source[:, here].astype(f32)
            scaled = (wide * gain[:, here]).astype(bf16)
            squares = squares + jnp.sum(wide * wide, axis=1, keepdims=True)
            values = values + dot(scaled, piece[:block, :])
            low = low + dot_nt(scaled, a_part[:, here])
        entries = lax.broadcasted_iota(jnp.int32, (rows, table.shape[0]), 1)
        pick = (line[out, :] == entries).astype(bf16)
        length = dot(pick, lengths)[:, :1]
        high = squares.astype(bf16).astype(f32)
        middle = (squares - high).astype(bf16).astype(f32)
        last = squares - high - middle
        extra = jnp.zeros((rows, rank), f32)
        for i, number in enumerate((high, middle, last, length)):
            extra = jnp.where(lane == i, number, extra)
        sums[out, :half_kv] = values
        sums[out, half_kv : half_kv + 2 * rank] = jnp.concatenate([low, extra], axis=1)
        sums[out, half_kv + 2 * rank :] = dot(pick, table)
    lane = lax.broadcasted_iota(jnp.int32, (step, 2 * rank), 1)
    for k, target in enumerate((own, to1, to2, to3)):
        for h in range(2):
            start = h * rows + k * step
            target[h * step : (h + 1) * step, :] = sums[pl.ds(start, step), :].astype(target.dtype)
            if k == 0:
                extra = sums[pl.ds(start, step), half_kv : half_kv + 2 * rank]
                extra = jnp.where(lane == rank + 4, position[pl.ds(start, step), :], extra)
                own[h * step : (h + 1) * step, half_kv : half_kv + 2 * rank] = extra


def row_kernel(own, got1, got2, got3, b_half, bias, packed, *, half_kv, rank, width):
    total = own[...]
    for got in (got1, got2, got3):
        total = total + got[...].astype(f32)
    raw_values = total[:, :half_kv]
    raw_low = total[:, half_kv : half_kv + rank]
    at = half_kv + rank
    squares = total[:, at : at + 1] + total[:, at + 1 : at + 2] + total[:, at + 2 : at + 3]
    length = total[:, at + 3 : at + 4]
    position = total[:, at + 4 : at + 5]
    weight = jnp.where(position < length, 1.0 / length, 0.0)
    inverse = lax.rsqrt(squares / width + epsilon)
    low = (raw_low * inverse).astype(bf16)
    values_out = raw_values * inverse + bias[...] + dot(low, b_half[...])
    dvalues = ((values_out - total[:, half_kv + 2 * rank :]) * weight).astype(bf16)
    dlow = dot_nt(dvalues, b_half[...]).astype(bf16)
    centre = (
        jnp.sum(dvalues.astype(f32) * raw_values, axis=1, keepdims=True)
        + jnp.sum(dlow.astype(f32) * raw_low, axis=1, keepdims=True)
    ) / width
    factor = inverse * inverse * inverse * centre
    lane = lax.broadcasted_iota(jnp.int32, (total.shape[0], rank), 1)
    extra = jnp.zeros((total.shape[0], rank), f32)
    for i, number in enumerate((inverse, factor)):
        for j in range(3):
            part = number.astype(bf16).astype(f32)
            extra = jnp.where(lane == 3 * i + j, part, extra)
            number = number - part
    packed[:, :half_kv] = dvalues
    packed[:, half_kv:] = jnp.concatenate([low.astype(f32), extra], axis=1).astype(bf16)


def image_kernel(
    place,
    packed,
    got1,
    got2,
    got3,
    near,
    far,
    low_near,
    low_far,
    gain,
    a_part,
    w0,
    w1,
    w2,
    w3,
    b_half,
    mine,
    give,
    rows,
    ranks,
    *,
    block,
    half_kv,
    rank,
    step,
):
    pieces = (w0, w1, w2, w3)
    side = len(pieces)
    count = near.shape[0]
    for k, source in enumerate((packed, got1, got2, got3)):
        for h in range(2):
            start = h * count + k * step
            rows[pl.ds(start, step), :] = source[h * step : (h + 1) * step, :]
    dvalues = rows[:, :half_kv]
    extra = rows[:, half_kv:]
    low = extra[:, :rank]
    numbers = extra[:, rank:].astype(f32)
    inverse = numbers[:, 0:1] + numbers[:, 1:2] + numbers[:, 2:3]
    factor = numbers[:, 3:4] + numbers[:, 4:5] + numbers[:, 5:6]
    dlow = dot_nt(dvalues, b_half[...]).astype(bf16)
    half = rank // 2
    grad = dot_tn(low, dvalues)
    mine[:, side * block :] = grad[:half]
    give[:, side * block :] = grad[half:]
    enc_low = jnp.concatenate([low_near[...], low_far[...]])
    for k, piece in enumerate(pieces):
        here = pl.ds(block_start(place[0], k, side, block), block)
        dnormed = dot_nt(dvalues, piece[:block, :]) + dot(dlow, a_part[:, here])
        wide = jnp.concatenate([near[:, here], far[:, here]]).astype(f32)
        dimage = (inverse * (gain[:, here] * dnormed) - wide * factor).astype(bf16)
        ranks[...] = dot_tn(enc_low, dimage)
        mine[:, here] = ranks[pl.ds(pl.multiple_of(place[1] * half, half), half), :]
        give[:, here] = ranks[pl.ds(pl.multiple_of((1 - place[1]) * half, half), half), :]


def place_kernel(whole, enc, llm, *, side):
    rows = whole.shape[1]
    enc_step, llm_step = enc.shape[1] // side, llm.shape[1] // side
    for i in range(side):
        for j in range(side):
            here = slice(i * rows, (i + 1) * rows)
            part = whole[i * side + j]
            enc[here, j * enc_step : (j + 1) * enc_step] = part[:, :enc_step]
            llm[here, j * llm_step : (j + 1) * llm_step] = part[:, enc_step:]


def body(
    hidden,
    enc_weight,
    enc_bias,
    enc_frozen,
    enc_adapter,
    text_rows,
    norm_gain,
    value_weight,
    value_bias,
    llm_frozen,
    llm_adapter,
    targets,
    dest_owner,
    seq_length,
):
    n_dp = lax.axis_size("dp")
    n_mp = lax.axis_size("mp")
    side = n_mp
    owners = n_dp * n_mp
    grp = lax.axis_index("grp")
    dp = lax.axis_index("dp")
    mp = lax.axis_index("mp")
    first = grp == 0
    width = text_rows.shape[1]
    part_width = enc_weight.shape[1]
    rank = enc_frozen.shape[1]
    half_rank = rank // 2
    kv = value_weight.shape[1]
    half_kv = kv // 2
    shard = value_weight.shape[0]
    block = side * shard
    block_rows = hidden.shape[0]
    mine_rows = block_rows // 2
    capacity = 2 * ENC_DEV // owners
    chunk = 2 * capacity
    area = capacity * n_dp
    slab, col = dp // side, dp & (side - 1)
    wrap = side - 1

    swap = [
        ((z * side + x) * side + y, (y * side + x) * side + z)
        for z in range(side)
        for x in range(side)
        for y in range(side)
    ]
    w_half = cut(value_weight, grp * half_kv, half_kv, 1)
    w_moved = lax.ppermute(w_half, ("dp", "mp"), swap)

    own_length = seq_length[0]
    t_half = cut(targets[:area], grp * half_kv, half_kv, 1)
    t_half = t_half.reshape(capacity, n_dp, half_kv).transpose(1, 0, 2)
    t_half = jnp.concatenate([t_half, jnp.full_like(t_half, own_length.astype(bf16))], axis=1)
    t_half = t_half.reshape(side, side * chunk, half_kv)
    w_line, t_line = [w_moved], [cut(t_half, slab, 1)[0]]
    for k in range(1, side):
        t_given = cut(t_half, (slab + k) & wrap, 1)[0]
        came = along(jnp.concatenate([w_moved, t_given]), k, 0, side)
        if k == 1:
            dest_owner, text_rows, _ = lax.optimization_barrier((dest_owner, text_rows, came))
        w_line.append(came[:shard])
        t_line.append(came[shard:])
    w_line = w_line[::-1]
    w_line = cut(jnp.concatenate(w_line + w_line), ((2 * side - 1 - slab) & wrap) * shard, block)
    t_line = jnp.stack(t_line).reshape(side, side, chunk, half_kv)
    pieces = []
    for k in range(side):
        t_given = cut(t_line, (col + k) & wrap, 1, 1).reshape(side * chunk, half_kv)
        piece = jnp.concatenate([w_line, t_given])
        pieces.append(along(piece, 0, k, side) if k else piece)

    own_hidden = cut(hidden, grp * mine_rows, mine_rows)
    hid_next, hid_last = turned(own_hidden, "mp", 1), turned(own_hidden, "mp", -1)
    hid = jnp.concatenate([own_hidden, hid_next, turned(hid_next, "mp", 1), hid_last])

    text_count = text_rows.shape[0] // 2
    text_wide = cut(text_rows, grp * text_count, text_count).astype(f32)
    text_inverse = lax.rsqrt(jnp.mean(text_wide * text_wide, axis=1, keepdims=True) + epsilon)

    a_half = cut(llm_frozen.T, grp * half_rank, half_rank)
    a_mine = to_everyone(a_half, ("dp", "mp"))
    a_both = [a.transpose(1, 0, 2).reshape(half_rank, width) for a in (a_mine, crossed(a_mine))]
    a_all = jnp.concatenate(a_both)
    a_part = cut(a_all, mp * part_width, part_width, 1)
    b_all = jnp.where(first, llm_adapter, jnp.roll(llm_adapter, half_rank, axis=0))
    b_half = cut(b_all, grp * half_kv, half_kv, 1)
    bias_wide = value_bias.astype(f32)[None]
    bias_half = cut(bias_wide, grp * half_kv, half_kv, 1)

    destiny = dest_owner[:, 0]
    block_dest = cut(destiny, dp * ENC_DEV, ENC_DEV)
    local = jnp.arange(ENC_DEV, dtype=jnp.int32)
    from_mp = (mp - (local % (ENC_DEV // 2)) // mine_rows) & wrap
    from_grp = (grp + local // (ENC_DEV // 2)) & 1
    place = from_mp * block_rows + from_grp * mine_rows + (local & (mine_rows - 1))
    own_dest = jnp.sum(jnp.where(place[:, None] == local[None, :], block_dest[None, :], 0), axis=1)
    earlier = (own_dest[:, None] == block_dest[None, :]) & (local[None, :] < place[:, None])
    slot = jnp.sum(earlier.astype(jnp.int32), axis=1)
    own_mp, own_col, own_slab = own_dest & wrap, (own_dest // side) & wrap, own_dest // (side * side)
    line = (((col - own_col) & wrap) * side + ((slab - own_slab) & wrap)) * capacity + slot
    line = jnp.where(own_mp == mp, line, -1)
    position = (slot * n_dp + dp).astype(f32)

    enc_low = dot(hid, enc_frozen).astype(bf16)
    merged = dot(hid, enc_weight) + enc_bias.astype(f32) + dot(enc_low, enc_adapter)
    image = merged.astype(bf16)
    gain_wide = norm_gain.astype(f32)[None]
    text_normed = (text_wide * text_inverse * gain_wide).astype(bf16)
    a_text = a_all
    text_low = dot_nt(text_normed, a_text).astype(bf16)
    owner_index = dp * n_mp + mp
    counts = jnp.sum((destiny.reshape(n_dp, ENC_DEV) == owner_index).astype(jnp.int32), axis=1)
    row = grp * text_count + jnp.arange(text_count, dtype=jnp.int32)
    taken = (row < area) & (
        row // n_dp
        < jnp.sum(
            jnp.where(
                (row & (n_dp - 1))[:, None] == jnp.arange(n_dp, dtype=jnp.int32)[None, :],
                counts,
                0,
            ),
            axis=1,
        )
    )
    keep = (row < own_length) & ~taken
    text_kept = jnp.where(keep[:, None], text_low, jnp.zeros_like(text_low))
    text_weight = 1.0 / own_length.astype(f32)
    text_sum = dot_tn(text_kept, text_normed) * text_weight
    own_text_targets = cut(targets, grp * text_count, text_count).astype(f32)
    rest = bias_wide + dot(text_low, b_all) - own_text_targets
    rest_high, rest_low = split_two(rest)
    rest_sum = dot_tn(
        jnp.concatenate([text_kept, text_kept]), jnp.concatenate([rest_high, rest_low])
    )
    rest_sum = rest_sum * text_weight
    both_sums = jnp.concatenate([text_sum, rest_sum], axis=1)
    both_sums = both_sums[:half_rank] + crossed(both_sums[half_rank:])
    image_far = crossed(image)
    enc_low_far = crossed(enc_low)
    gain_part = cut(gain_wide, mp * part_width, part_width, 1)
    where = jnp.stack([col, grp]).astype(jnp.int32)
    sizes = dict(half_kv=half_kv, rank=rank)
    lanes = kv + 2 * rank
    tokens = 2 * mine_rows
    to_one = jax.ShapeDtypeStruct((tokens, lanes), bf16)
    own, *to = pl.pallas_call(
        functools.partial(partial_kernel, chunk=chunk, block=block, step=mine_rows, **sizes),
        out_shape=(jax.ShapeDtypeStruct((tokens, lanes), f32), to_one, to_one, to_one),
        in_specs=[SMEM] + [VMEM] * 10,
        out_specs=(VMEM,) * 4,
        scratch_shapes=[pltpu.VMEM((ENC_DEV, lanes), f32)],
        compiler_params=PARAMS,
        name="partial_products",
    )(where, image, image_far, gain_part, a_part, *pieces, line[:, None], position[:, None])
    got = [turned(to[k - 1], "mp", -k) for k in range(1, n_mp)]
    packed = pl.pallas_call(
        functools.partial(row_kernel, width=float(width), **sizes),
        out_shape=jax.ShapeDtypeStruct((tokens, half_kv + 2 * rank), bf16),
        in_specs=[VMEM] * 6,
        out_specs=VMEM,
        compiler_params=PARAMS,
        name="row_work",
    )(own, *got, b_half, bias_half)
    text_parts = both_sums[:, :width].reshape(half_rank, owners, shard).transpose(1, 0, 2)
    text_parts = lax.all_to_all(text_parts.astype(bf16), ("dp", "mp"), 0, 0, tiled=True)
    got = [turned(packed, "mp", k) for k in range(1, n_mp)]
    text_here = jnp.sum(text_parts.astype(f32), axis=0)
    here_high, here_low = split_two(text_here)
    text_grad = dot(jnp.concatenate([here_high, here_low]), value_weight)
    text_grad = text_grad[:half_rank] + text_grad[half_rank:] + both_sums[:, width:]
    text_grad = text_grad + (
        turned(text_grad, "mp", 1) + turned(text_grad, "mp", 2) + turned(text_grad, "mp", 3)
    )
    enc_low_far, text_grad = lax.optimization_barrier((enc_low_far, text_grad))
    mine, give = pl.pallas_call(
        functools.partial(image_kernel, block=block, step=mine_rows, **sizes),
        out_shape=(jax.ShapeDtypeStruct((half_rank, part_width + half_kv), f32),) * 2,
        in_specs=[SMEM] + [VMEM] * 15,
        out_specs=(VMEM, VMEM),
        scratch_shapes=[
            pltpu.VMEM((ENC_DEV, half_kv + 2 * rank), bf16),
            pltpu.VMEM((rank, block), f32),
        ],
        compiler_params=PARAMS,
        name="image_gradients",
    )(
        where,
        packed,
        *got,
        image,
        image_far,
        enc_low,
        enc_low_far,
        gain_part,
        a_part,
        *pieces,
        b_half,
    )

    came = crossed(give)
    llm_mine, llm_came = mine[:, part_width:], came[:, part_width:]
    enc = (mine[:, :part_width] + came[:, :part_width]).reshape(side, 8, side, -1)
    llm = (
        jnp.concatenate(
            [jnp.where(first, llm_mine, llm_came), jnp.where(first, llm_came, llm_mine)], axis=1
        )
        + text_grad
    ).reshape(side, 8, side, -1)
    mine = jnp.concatenate([enc, llm], axis=3).transpose(0, 2, 1, 3).reshape(n_dp, 8, -1)
    mine = jnp.sum(lax.all_to_all(mine, "dp", 0, 0, tiled=True), axis=0)
    whole = to_everyone(mine, "dp")
    return pl.pallas_call(
        functools.partial(place_kernel, side=side),
        out_shape=(
            jax.ShapeDtypeStruct((half_rank, part_width), f32),
            jax.ShapeDtypeStruct((half_rank, kv), f32),
        ),
        in_specs=[VMEM],
        out_specs=(VMEM, VMEM),
        compiler_params=PARAMS,
        name="placed",
    )(whole)


def solution(mesh):
    return jax.shard_map(
        body,
        mesh=mesh,
        in_specs=(
            P(("dp", "mp"), None),
            P(None, "mp"),
            P("mp"),
            P(),
            P(None, "mp"),
            P(("dp", "mp"), None),
            P(),
            P(("dp", "mp"), None),
            P(),
            P(("dp", "mp"), None),
            P(),
            P(("dp", "mp"), None),
            P(),
            P(("dp", "mp")),
        ),
        out_specs=(P("grp", "mp"), P("grp", None)),
        check_vma=False,
    )
```
